128 devices in a mesh: px: 16 (over x, y), py: 8 (over z, core).
Axes of the slice: x: 4, y: 4, z: 4, core: 2. Of those that a mesh axis runs over, the one named last changes fastest.
Arguments:
- plastic_distortion: float32 [9, 256, 256, 256], P(None, 'px', 'py'), may hold values from -4 to 4
- grain_ids: int32 [256, 256, 256], P('px', 'py'), may hold values from 0 to 63
- grain_moduli: float32 [2, 64], replicated, may hold values from 0.5 to 2
- seg_source: int32 [65536, 1], P(('px', 'py')), may hold values from 0 to 127; in each aligned block of 512 rows (0 to 511, 512 to 1023, ...) at most 8 rows name the same one
- seg_tile: int32 [65536], P(('px', 'py')), may hold values from 0 to 1023
- seg_center: int32 [65536], P(('px', 'py')), may hold values from 0 to 127
- burgers: float32 [3, 65536], P(None, ('px', 'py')), may hold values from -4 to 4
- line_vector: float32 [3, 65536], P(None, ('px', 'py')), may hold values from -4 to 4
Outputs:
- stress_field: float32 [6, 256, 256, 256], P(None, 'px', 'py')
- seg_force: float32 [3, 65536], P(None, ('px', 'py'))
The draws below stay inside these ranges and needn't reach their ends.
Inputs may be any that keep to these rules, and one draw needn't show every extreme that they name: `seg_source`: among the segments of one device no source device is named more than 8 times; every device is named by some segment.
All inputs are finite; a program needn't handle non-finite values.
Results may differ from the reference program's by a relative error of at most 0.0003.
Values sent between devices are 32-bit elements; how exact they have to be, the bound alone decides.
A program may use at most 128 MiB of HBM per device.

```python
import math
import jax
import jax.numpy as jnp
import numpy as np
from jax import lax

GRID = 256
TILE = 128
GRAINS = 64
ITERS = 1
SEG_DEV = 512
SEGS = 65536
CAP = 8
TILES_DEV = 1024
N_PX = 16
N_PY = 8
DEVICES = 128


def draw_plastic_distortion(key, part):
    full_shape = (9, GRID, GRID, GRID)
    values = jnp.clip(jax.random.normal(key, full_shape, jnp.float32), -3.5, 3.5)
    return values.astype(jnp.float32)


def draw_grain_ids(key, part):
    seeds = jax.random.randint(key, (GRAINS, 3), 0, GRID)
    positions = jnp.arange(GRID, dtype=jnp.int32)
    labels = jnp.arange(GRAINS, dtype=jnp.int32)

    def one_plane(xpos):
        gap_x = jnp.abs(xpos - seeds[:, 0])
        gap_x = jnp.minimum(gap_x, GRID - gap_x)
        gap_y = jnp.abs(positions[:, None] - seeds[None, :, 1])
        gap_y = jnp.minimum(gap_y, GRID - gap_y)
        gap_z = jnp.abs(positions[:, None] - seeds[None, :, 2])
        gap_z = jnp.minimum(gap_z, GRID - gap_z)
        distance = gap_x[None, None, :] * gap_x[None, None, :] + gap_y[:, None, :] * gap_y[:, None, :] + gap_z[None, :, :] * gap_z[None, :, :]
        scores = distance * GRAINS + labels[None, None, :]
        return (jnp.min(scores, axis=-1) % GRAINS).astype(jnp.int32)
    return lax.map(one_plane, positions)


def set_ends(entries, stream_key, low, top_value):
    place = [jax.random.randint(jax.random.fold_in(stream_key, axis), (), 0, length) for axis, length in enumerate(entries.shape)]
    main_axis = entries.shape.index(max(entries.shape))
    neighbour = place[:main_axis] + [(place[main_axis] + 1) % entries.shape[main_axis]] + place[main_axis + 1:]
    return entries.at[tuple(place)].set(low).at[tuple(neighbour)].set(top_value)


def level_of(own_key, dims, shards, smallest, top_value):
    gain, own = 1.0, jax.random.fold_in(own_key, 6)
    for position, blocks in shards:
        heights = jnp.exp(jax.random.uniform(jax.random.fold_in(own, position), (blocks,), jnp.float32, smallest / len(shards), top_value / len(shards)))
        gain = gain * jnp.repeat(heights, dims[position] // blocks).reshape([-1 if axis == position else 1 for axis in range(len(dims))])
    return gain


def shared_out(key, own, number, rows, number_of, top, reach, slope):
    sequence = jax.random.permutation(key, number_of)
    crowded, ordinary = portions_of(number_of, rows * top, reach, slope, True), portions_of(number_of, rows * top, reach, slope, False)
    places = jnp.arange(number_of)

    def named(tallies, turn):
        used = int((tallies > 0).sum())
        fixed = max(1, used // 4)
        moved = fixed + (places - fixed + turn * (used - fixed)) % max(1, number_of - fixed)
        return jnp.zeros((number_of,), jnp.int32).at[sequence[jnp.where(places < fixed, places, moved)]].set(jnp.asarray(tallies, jnp.int32))

    tallies = jnp.where(number % 4 == 0, named(crowded, number // 4), named(ordinary, number - number // 4 - 1))
    mixed = jax.random.permutation(jax.random.fold_in(own, 3), number_of)
    giver, receiver = mixed[0:number_of // 2 * 2:2], mixed[1:number_of // 2 * 2:2]
    margin = jnp.minimum(tallies[giver] - 1, reach - tallies[receiver]) // 2
    margin = jnp.where((giver == sequence[0]) | (receiver == sequence[0]) | (tallies[receiver] == 0), 0, jnp.maximum(margin, 0))
    moved = jax.random.randint(jax.random.fold_in(own, 4), (number_of // 2,), 0, 1 << 20) % (margin + 1)
    tallies = tallies.at[giver].add(-moved).at[receiver].add(moved)
    members = jnp.searchsorted(jnp.cumsum(tallies), jnp.arange(rows * top), side="right").astype(jnp.int32)
    listing = members.reshape(top, rows).T
    listing = listing[jax.random.permutation(jax.random.fold_in(own, 1), rows)]
    turn = jax.random.randint(jax.random.fold_in(own, 2), (rows, 1), 0, top)
    return jnp.take_along_axis(listing, (jnp.arange(top)[None, :] + turn) % top, axis=1)


def portions_of(number_of, total, bound, lean, full):
    portions = [(1 << 20) // math.isqrt(standing ** lean) + 1 for standing in range(1, number_of + 1)]
    largest = bound if full else min(bound, max(-(-total // number_of), total * portions[0] // sum(portions)))
    least = 1 if total - largest >= number_of - 1 else 0
    counts, rest = [largest] + [least] * (number_of - 1), total - largest - least * (number_of - 1)
    while rest > 0:
        free = [i for i in range(1, number_of) if counts[i] < largest] or [i for i in range(1, number_of) if counts[i] < bound]
        mass, budget = sum([portions[i] for i in free]), rest
        for i in free:
            addition = min(bound - counts[i], max(1, budget * portions[i] // mass), rest)
            counts[i] = counts[i] + addition
            rest = rest - addition
    return np.array(counts)


def scatter_about(key, shape, scale, limit, cuts=(), held_as=jnp.bfloat16):
    entries = scale * jax.random.normal(key, shape, jnp.float32)
    if cuts:
        entries = entries * level_of(key, shape, cuts, -0.22, 0.18)
    return jnp.clip(entries, -limit, limit).astype(held_as)


def setup_inputs(seed: int = 0) -> dict:
    keys = jax.random.split(jax.random.key(seed), 9)
    plastic_distortion = draw_plastic_distortion(jax.random.fold_in(keys[8], 71), 0)
    grain_ids = draw_grain_ids(jax.random.fold_in(keys[8], 71), 0)
    grain_moduli = jnp.clip(jax.random.uniform(keys[2], (2, GRAINS), jnp.float32, 0.5, 2.0), 0.5, 2.0)
    seg_source_keys = jax.random.split(jax.random.fold_in(keys[3], 1), SEGS // SEG_DEV)
    seg_source_turns = jax.random.permutation(jax.random.fold_in(keys[3], 3), SEGS // SEG_DEV)
    seg_source = jax.vmap(lambda own, number: shared_out(jax.random.fold_in(keys[3], 2), own, number, SEG_DEV, DEVICES, 1, CAP, 2))(seg_source_keys, seg_source_turns).reshape((SEGS, 1))
    seg_tile = set_ends(jax.random.randint(keys[4], (SEGS,), 0, TILES_DEV), jax.random.fold_in(keys[4], 1), 0, TILES_DEV - 1).astype(jnp.int32)
    seg_center = set_ends(jax.random.randint(keys[5], (SEGS,), 0, TILE), jax.random.fold_in(keys[5], 1), 0, TILE - 1).astype(jnp.int32)
    burgers = scatter_about(keys[6], (3, SEGS), 1.0, 4.0, ((1, 128),), jnp.float32)
    line_vector = scatter_about(keys[7], (3, SEGS), 1.0, 4.0, ((1, 128),), jnp.float32)
    return {"plastic_distortion": plastic_distortion, "grain_ids": grain_ids, "grain_moduli": grain_moduli, "seg_source": seg_source, "seg_tile": seg_tile, "seg_center": seg_center, "burgers": burgers, "line_vector": line_vector}


ref_lambda = 1.25
ref_shear = 1.25


def symmetric_part(distortion):
    return jnp.stack([distortion[0], distortion[4], distortion[8], (distortion[5] + distortion[7]) * 0.5, (distortion[2] + distortion[6]) * 0.5, (distortion[1] + distortion[3]) * 0.5])


def stiffness(strain, lame_mod, shear_mod):
    trace_sum = strain[0] + strain[1] + strain[2]
    diagonal = [2.0 * shear_mod * strain[index] + lame_mod * trace_sum for index in range(3)]
    shears = [2.0 * shear_mod * strain[index] for index in range(3, 6)]
    return jnp.stack(diagonal + shears)


def polarization(strain, plastic, lame_mod, shear_mod):
    return stiffness(strain - plastic, lame_mod, shear_mod) - stiffness(strain, ref_lambda, ref_shear)


def divergence(grad_x, grad_y, grad_z):
    return jnp.stack([grad_x[0] + grad_y[5] + grad_z[4], grad_x[5] + grad_y[1] + grad_z[3], grad_x[4] + grad_y[3] + grad_z[2]])


def sym_gradient(grad_x, grad_y, grad_z):
    return jnp.stack([grad_x[0], grad_y[1], grad_z[2], (grad_z[1] + grad_y[2]) * 0.5, (grad_z[0] + grad_x[2]) * 0.5, (grad_y[0] + grad_x[1]) * 0.5])


def wave_numbers(first, length, total):
    index = first + jnp.arange(length, dtype=jnp.int32)
    angle = index.astype(jnp.float32) * (2.0 * math.pi / total)
    return jnp.sin(angle), (index % (total // 2)) == 0


def solve_waves(parts, wave_x, wave_y, wave_z, null_mode):
    squared = wave_x * wave_x + wave_y * wave_y + wave_z * wave_z
    inverse_sq = jnp.where(null_mode, 0.0, 1.0 / jnp.where(null_mode, 1.0, squared))
    coupling = (ref_lambda + ref_shear) / (ref_lambda + 2.0 * ref_shear)
    along_wave = wave_x * parts[0] + wave_y * parts[1] + wave_z * parts[2]
    common = coupling * inverse_sq * inverse_sq * along_wave
    return [(inverse_sq * parts[0] - common * wave_x) / ref_shear, (inverse_sq * parts[1] - common * wave_y) / ref_shear, (inverse_sq * parts[2] - common * wave_z) / ref_shear]


def core_weights(center, tile_len):
    offsets = jnp.arange(tile_len, dtype=jnp.float32)
    spread = tile_len / 8.0
    distance = offsets - center[..., None].astype(jnp.float32)
    weights = jnp.exp(-distance * distance / (2.0 * spread * spread))
    return weights / jnp.sum(weights, axis=-1, keepdims=True)


def peach_koehler(tensor, burgers, line_vector):
    push_x = tensor[0] * burgers[0] + tensor[5] * burgers[1] + tensor[4] * burgers[2]
    push_y = tensor[5] * burgers[0] + tensor[1] * burgers[1] + tensor[3] * burgers[2]
    push_z = tensor[4] * burgers[0] + tensor[3] * burgers[1] + tensor[2] * burgers[2]
    return jnp.stack([push_y * line_vector[2] - push_z * line_vector[1], push_z * line_vector[0] - push_x * line_vector[2], push_x * line_vector[1] - push_y * line_vector[0]])


def shifted_diff(values, axis):
    return (jnp.roll(values, -1, axis) - jnp.roll(values, 1, axis)) * 0.5


def all_diffs(values):
    return shifted_diff(values, 1), shifted_diff(values, 2), shifted_diff(values, 3)


def reference(plastic_distortion, grain_ids, grain_moduli, seg_source, seg_tile, seg_center, burgers, line_vector):
    plastic = symmetric_part(plastic_distortion)
    lame_mod = grain_moduli[0][grain_ids]
    shear_mod = grain_moduli[1][grain_ids]
    wave_line, null_line = wave_numbers(0, GRID, GRID)
    wave_x = wave_line[:, None, None]
    wave_y = wave_line[None, :, None]
    wave_z = wave_line[None, None, :]
    null_mode = null_line[:, None, None] & null_line[None, :, None] & null_line[None, None, :]
    strain = jnp.zeros_like(plastic)
    for step in range(ITERS):
        polar = polarization(strain, plastic, lame_mod, shear_mod)
        force_density = divergence(*all_diffs(polar))
        spectrum = jnp.fft.fftn(force_density, axes=(1, 2, 3))
        solved = solve_waves([spectrum[0], spectrum[1], spectrum[2]], wave_x, wave_y, wave_z, null_mode)
        displace = jnp.fft.ifftn(jnp.stack(solved), axes=(1, 2, 3)).real.astype(jnp.float32)
        strain = sym_gradient(*all_diffs(displace))
    stress_field = stiffness(strain - plastic, lame_mod, shear_mod)
    blocks_per = GRID // TILE
    width_x = GRID // N_PX
    width_y = GRID // N_PY
    source = seg_source[:, 0]
    col_x = (source // N_PY) * width_x + seg_tile // (width_y * blocks_per)
    col_y = (source % N_PY) * width_y + (seg_tile // blocks_per) % width_y
    block_index = seg_tile % blocks_per
    tiles = stress_field.reshape(6, GRID, GRID, blocks_per, TILE)
    picked = tiles[:, col_x, col_y, block_index, :]
    weights = core_weights(seg_center, TILE)
    seg_stress = jnp.sum(picked * weights[None], axis=-1)
    seg_force = peach_koehler(seg_stress, burgers, line_vector)
    return stress_field, seg_force
```

```python
import functools

import jax
import jax.numpy as jnp
import ml_dtypes
import numpy as np
from jax import lax
from jax.experimental import pallas as pl
from jax.experimental.pallas import tpu as pltpu
from jax.sharding import PartitionSpec as P

F32 = jnp.float32
BF16 = jnp.bfloat16
REF_LAMBDA = 1.25
REF_SHEAR = 1.25
GRID = 256
HALF = 128
NPX = 16
NPY = 8
NX = 16
NY = 32
VMEM_LIMIT = 56 * 1024 * 1024
VM = pl.BlockSpec(memory_space=pltpu.VMEM)


def two_parts(table):
    table = np.asarray(table, np.float32)
    high = table.astype(ml_dtypes.bfloat16)
    low = (table - high.astype(np.float32)).astype(ml_dtypes.bfloat16)
    return np.stack([high, low])


def z_tables():
    z = np.arange(GRID)
    fwd = np.zeros((GRID, GRID))
    inv = np.zeros((GRID, GRID))
    for row in range(GRID):
        p, kzlo, ri, kzhi = row // 32, (row // 8) % 4, (row // 4) % 2, row % 4
        wave = 16 * p + 4 * kzhi + kzlo
        angle = 2 * np.pi * ((wave * z) % GRID) / GRID
        if wave == 0:
            line = np.ones(GRID) if ri == 0 else 1.0 - 2.0 * (z % 2)
            fwd[row], inv[row] = line, line / GRID
        else:
            line = np.cos(angle) if ri == 0 else -np.sin(angle)
            fwd[row], inv[row] = line, 2 * line / GRID
    return fwd, inv


def half_tables():
    k = np.arange(HALF)
    fwd, inv = [], []
    for e in range(2):
        angle = 2 * np.pi * (((2 * k[:, None] + e) * k[None, :]) % GRID) / GRID
        cos, sin = np.cos(angle), np.sin(angle)
        fwd.append(np.block([[cos, sin], [-sin, cos]]))
        inv.append(np.block([[cos.T, -sin.T], [sin.T, cos.T]]) / GRID)
    return np.stack(fwd), np.stack(inv)


def sines():
    wave = np.arange(GRID)
    line = np.sin(2 * np.pi * wave / GRID)
    line[wave % HALF == 0] = 0.0
    return line


def wave_lines():
    line = sines()
    sx = np.stack([line[0::2], line[1::2]])[:, :, None] * np.ones((1, 1, 128))
    lane = np.arange(256)
    kz16 = (lane // 128) * 8 + (lane // 16) % 8
    ky16 = lane % 16
    sy = np.stack([line[2 * ((p % 8) * 16 + ky16) + p // 8] for p in range(NPX)])
    sz = np.stack([line[16 * p + kz16] for p in range(NPY)])
    return sx.astype(np.float32), sy.astype(np.float32), sz.astype(np.float32)


def tile_weights():
    v = np.arange(128, dtype=np.float64)
    weights = np.exp(-((v[None, :] - v[:, None]) ** 2) / (2.0 * 16.0**2))
    return weights / weights.sum(axis=1, keepdims=True)


def split(values):
    high = values.astype(BF16)
    low = (values - high.astype(F32)).astype(BF16)
    return high, low


def dot(a, b, dims=((1,), (0,))):
    return lax.dot_general(a, b, (dims, ((), ())), preferred_element_type=F32)


def dot3(a, b, dims=((1,), (0,))):
    (ah, al), (bh, bl) = a, b
    return dot(ah, bh, dims) + (dot(ah, bl, dims) + dot(al, bh, dims))


def swap_groups(values):
    count = len(values)
    width = 128 // count
    lane = lax.broadcasted_iota(jnp.int32, values[0].shape, values[0].ndim - 1)
    axis = values[0].ndim - 1
    values = list(values)
    step = 1
    while step < count:
        first = ((lane // (width * step)) % 2) == 0
        out = list(values)
        for i in range(count):
            if i & step == 0:
                low, high = values[i], values[i + step]
                out[i] = jnp.where(first, low, pltpu.roll(high, width * step, axis))
                out[i + step] = jnp.where(first, pltpu.roll(low, 128 - width * step, axis), high)
        values = out
        step *= 2
    return values


def call(body, out_shape, scratch=(), n_in=0):
    multi = isinstance(out_shape, (list, tuple))
    return pl.pallas_call(
        body,
        out_shape=out_shape,
        in_specs=[VM] * n_in,
        out_specs=[VM] * len(out_shape) if multi else VM,
        scratch_shapes=list(scratch),
        compiler_params=pltpu.CompilerParams(vmem_limit_bytes=VMEM_LIMIT),
    )


def sds(shape, dtype=F32):
    return jax.ShapeDtypeStruct(shape, dtype)


def moduli_of(table, ids):
    lame, shear = [], []
    for half in range(2):
        index = ids[:, half * 128 : (half + 1) * 128]
        lame.append(jnp.take_along_axis(table, index, axis=1))
        shear.append(jnp.take_along_axis(table, index + 64, axis=1))
    return jnp.concatenate(lame, axis=1), jnp.concatenate(shear, axis=1)


def table_of(moduli_ref):
    row = jnp.concatenate([moduli_ref[0:1, :], moduli_ref[1:2, :]], axis=1)
    return jnp.broadcast_to(row, (NY, 128))


def polar_body(dist, ids, moduli, polar, xlo, xhi, ylo, yhi):
    table = table_of(moduli)

    def at_x(x, carry):
        lame, shear = moduli_of(table, ids[x])
        exx, eyy, ezz = dist[0, x], dist[4, x], dist[8, x]
        trace = lame * (exx + eyy + ezz)
        twice = shear + shear
        polar[0, x] = -(twice * exx + trace)
        polar[1, x] = -(twice * eyy + trace)
        polar[2, x] = -(twice * ezz + trace)
        polar[3, x] = -(shear * (dist[5, x] + dist[7, x]))
        polar[4, x] = -(shear * (dist[2, x] + dist[6, x]))
        polar[5, x] = -(shear * (dist[1, x] + dist[3, x]))
        return carry

    lax.fori_loop(0, NX, at_x, 0)
    for slot, comp in enumerate((0, 5, 4)):
        xlo[slot] = polar[comp, 0]
        xhi[slot] = polar[comp, NX - 1]
    for slot, comp in enumerate((5, 1, 3)):
        ylo[slot] = polar[comp, :, 0, :]
        yhi[slot] = polar[comp, :, NY - 1, :]


def shift_y(values, before, after):
    row = lax.broadcasted_iota(jnp.int32, values.shape, 0)
    up = jnp.where(row == NY - 1, after, pltpu.roll(values, NY - 1, 0))
    down = jnp.where(row == 0, before, pltpu.roll(values, 1, 0))
    return up - down


def shift_z(values):
    return pltpu.roll(values, GRID - 1, 1) - pltpu.roll(values, 1, 1)


def forward_z_body(polar, xbefore, xafter, ybefore, yafter, tz, wire, force, swap):
    for c, (cx, cy, cz) in enumerate(((0, 5, 4), (5, 1, 3), (4, 3, 2))):
        for x in range(NX):
            after = xafter[c] if x == NX - 1 else polar[cx, x + 1]
            before = xbefore[c] if x == 0 else polar[cx, x - 1]
            grad_y = shift_y(polar[cy, x], ybefore[c, x : x + 1], yafter[c, x : x + 1])
            total = (after - before) + grad_y + shift_z(polar[cz, x])
            force[x * NY : (x + 1) * NY, :] = total * 0.5
        waves = dot3((tz[0], tz[1]), split(force[...]), ((1,), (1,)))
        for p in range(NPY):
            for xg in range(4):
                tiles = [
                    waves[p * 32 + kzlo * 8 : p * 32 + kzlo * 8 + 8, xg * 128 : xg * 128 + 128]
                    for kzlo in range(4)
                ]
                for x4, tile in enumerate(swap_groups(tiles)):
                    x = xg * 4 + x4
                    swap[p * 128 + x * 8 : p * 128 + x * 8 + 8, :] = tile
            for s in range(8):
                wire[p, c, s] = swap[pl.ds(p * 128 + s, NX, stride=8), :]


def forward_y_body(got, ty, wire, rows_h, rows_l):
    for c in range(3):
        for ri in range(2):
            for kzhi in range(4):
                s = ri * 4 + kzhi
                low = swap_groups([got[q, c, s] for q in range(4)])
                high = swap_groups([got[q + 4, c, s] for q in range(4)])
                for kzlo in range(4):
                    row = (kzhi * 4 + kzlo) * NX
                    for e in range(2):
                        mixed = low[kzlo] + high[kzlo] if e == 0 else low[kzlo] - high[kzlo]
                        hi, lo = split(mixed)
                        rows_h[e, row : row + NX, ri * 128 : ri * 128 + 128] = hi
                        rows_l[e, row : row + NX, ri * 128 : ri * 128 + 128] = lo
        for e in range(2):
            out = dot3((rows_h[e], rows_l[e]), (ty[0, e], ty[1, e]))
            for ri in range(2):
                for kzg in range(2):
                    tiles = [
                        out[(kzg * 8 + k) * NX : (kzg * 8 + k + 1) * NX, ri * 128 : ri * 128 + 128]
                        for k in range(8)
                    ]
                    lane = c * 256 + kzg * 128
                    for p8, tile in enumerate(swap_groups(tiles)):
                        wire[e * 8 + p8, ri, :, lane : lane + 128] = tile


def solve_x_body(got, tx, txi, sx, sy_all, sz_all, wire, rows_h, rows_l):
    sy = sy_all[pl.ds(lax.axis_index("px"), 1), :]
    sz = sz_all[pl.ds(lax.axis_index("py"), 1), :]
    for ri in range(2):
        for q in range(8):
            a, b = got[q, ri], got[q + 8, ri]
            row = ri * 128 + q * 16
            for e in range(2):
                hi, lo = split(a + b if e == 0 else a - b)
                rows_h[e, row : row + 16, :] = hi
                rows_l[e, row : row + 16, :] = lo
    coupling = (REF_LAMBDA + REF_SHEAR) / (REF_LAMBDA + 2.0 * REF_SHEAR)
    backs = []
    for e in range(2):
        waves = dot3((tx[0, e], tx[1, e]), (rows_h[e], rows_l[e]))
        wx = jnp.concatenate([sx[e], sx[e]], axis=1)
        squared = wx * wx + (sy * sy + sz * sz)
        null = squared == 0.0
        inverse = jnp.where(null, 0.0, 1.0 / jnp.where(null, 1.0, squared))
        scale = inverse * (1.0 / REF_SHEAR)
        for ri in range(2):
            parts = [waves[ri * 128 : ri * 128 + 128, c * 256 : c * 256 + 256] for c in range(3)]
            along = wx * parts[0] + sy * parts[1] + sz * parts[2]
            common = coupling * inverse * along
            for c, line in enumerate((wx, sy, sz)):
                hi, lo = split(scale * (parts[c] - common * line))
                rows_h[e, ri * 128 : ri * 128 + 128, c * 256 : c * 256 + 256] = hi
                rows_l[e, ri * 128 : ri * 128 + 128, c * 256 : c * 256 + 256] = lo
        backs.append(dot3((txi[0, e], txi[1, e]), (rows_h[e], rows_l[e])))
    first, second = backs[0] + backs[1], backs[0] - backs[1]
    for ri in range(2):
        for q in range(8):
            row = ri * 128 + q * 16
            wire[q, ri] = first[row : row + 16, :]
            wire[q + 8, ri] = second[row : row + 16, :]


def inverse_y_body(got, tyi, wire, rows_h, rows_l):
    for c in range(3):
        for e in range(2):
            for ri in range(2):
                for kzg in range(2):
                    lane = c * 256 + kzg * 128
                    tiles = swap_groups([got[e * 8 + p8, ri, :, lane : lane + 128] for p8 in range(8)])
                    for k, tile in enumerate(tiles):
                        row = (kzg * 8 + k) * NX
                        hi, lo = split(tile)
                        rows_h[e, row : row + NX, ri * 128 : ri * 128 + 128] = hi
                        rows_l[e, row : row + NX, ri * 128 : ri * 128 + 128] = lo
        even = dot3((rows_h[0], rows_l[0]), (tyi[0, 0], tyi[1, 0]))
        odd = dot3((rows_h[1], rows_l[1]), (tyi[0, 1], tyi[1, 1]))
        for half, out in enumerate((even + odd, even - odd)):
            for ri in range(2):
                for kzhi in range(4):
                    tiles = [
                        out[(kzhi * 4 + k) * NX : (kzhi * 4 + k + 1) * NX, ri * 128 : ri * 128 + 128]
                        for k in range(4)
                    ]
                    for q4, tile in enumerate(swap_groups(tiles)):
                        wire[half * 4 + q4, c, ri * 4 + kzhi] = tile


def inverse_z_body(got, tzi, disp, xlo, xhi, ylo, yhi, waves, swap):
    for c in range(3):
        for p in range(NPY):
            for s in range(8):
                swap[p * 128 + s * 16 : p * 128 + s * 16 + 16, :] = got[p, c, s]
            for xg in range(4):
                tiles = [swap[pl.ds(p * 128 + xg * 4 + x4, 8, stride=16), :] for x4 in range(4)]
                for kzlo, tile in enumerate(swap_groups(tiles)):
                    row = p * 32 + kzlo * 8
                    waves[row : row + 8, xg * 128 : xg * 128 + 128] = tile
        turned = jnp.transpose(waves[...])
        out = dot3(split(turned), (tzi[0], tzi[1]))
        for x in range(NX):
            disp[c, x] = out[x * NY : (x + 1) * NY, :]
        xlo[c] = disp[c, 0]
        xhi[c] = disp[c, NX - 1]
        ylo[c] = disp[c, :, 0, :]
        yhi[c] = disp[c, :, NY - 1, :]


def stress_body(
    disp, xbefore, xafter, ybefore, yafter, polar, ids, moduli, asked, weights, stress, reply, rows_h, rows_l
):
    table = table_of(moduli)
    for x in range(NX):
        lame, shear = moduli_of(table, ids[x])
        gx, gy, gz = [], [], []
        for c in range(3):
            after = xafter[c] if x == NX - 1 else disp[c, x + 1]
            before = xbefore[c] if x == 0 else disp[c, x - 1]
            gx.append(after - before)
            gy.append(shift_y(disp[c, x], ybefore[c, x : x + 1], yafter[c, x : x + 1]))
            gz.append(shift_z(disp[c, x]))
        trace = (0.5 * lame) * (gx[0] + gy[1] + gz[2])
        half = 0.5 * shear
        parts = (
            shear * gx[0] + trace,
            shear * gy[1] + trace,
            shear * gz[2] + trace,
            half * (gz[1] + gy[2]),
            half * (gz[0] + gx[2]),
            half * (gy[0] + gx[1]),
        )
        for c, part in enumerate(parts):
            total = part + polar[c, x]
            stress[c, x] = total
            hi, lo = split(total)
            rows_h[x * NY : (x + 1) * NY, c * 256 : c * 256 + 256] = hi
            rows_l[x * NY : (x + 1) * NY, c * 256 : c * 256 + 256] = lo
    column = lax.broadcasted_iota(jnp.int32, (128, 512), 1)
    lane = lax.broadcasted_iota(jnp.int32, (128, 128), 1)
    lane256 = lax.broadcasted_iota(jnp.int32, (128, 256), 1)
    out = jnp.zeros((128, 128), F32)
    wh, wl = weights[0], weights[1]
    for k in range(8):
        tile = asked[:, k : k + 1]
        centre = asked[:, 8 + k : 9 + k]
        pick = (column == tile // 2).astype(F32).astype(BF16)
        picked = dot(pick, rows_h[...]) + dot(pick, rows_l[...])
        at = (lane == centre).astype(F32).astype(BF16)
        row = dot(at, wh) + dot(at, wl)
        weight = jnp.where(lane256 // 128 == tile % 2, jnp.concatenate([row, row], axis=1), 0.0)
        for c in range(6):
            value = jnp.sum(picked[:, c * 256 : c * 256 + 256] * weight, axis=1, keepdims=True)
            out = jnp.where(lane == c * 8 + k, value, out)
    reply[...] = out


def request_body(source, tile, centre, asked, slot_out):
    src = jnp.broadcast_to(source[...], (512, 128)).astype(F32)
    src_lane = jnp.transpose(src)[0:1, :]
    same = src[:, 0:1] == src_lane
    first = lax.broadcasted_iota(jnp.int32, (512, 512), 0)
    second = lax.broadcasted_iota(jnp.int32, (512, 512), 1)
    slot_lane = jnp.sum(jnp.where(same & (first < second), 1.0, 0.0), axis=0, keepdims=True)
    slot_out[...] = jnp.sum(jnp.where(same & (second < first), 1.0, 0.0), axis=1, keepdims=True)
    match = (src == lax.broadcasted_iota(jnp.int32, (512, 128), 1).astype(F32)).astype(F32).astype(BF16)
    row = lax.broadcasted_iota(jnp.int32, (8, 512), 0).astype(F32)
    here = row == slot_lane
    tile_v = tile[...]
    values = [tile_v // 8, tile_v % 8, centre[...]]
    rows = [jnp.where(here, v.astype(F32), 0.0) for v in values]
    stacked = jnp.concatenate(rows + [jnp.zeros((8, 512), F32)], axis=0).astype(BF16)
    got = dot(stacked, match)
    both = jnp.concatenate([got[0:8] * 8.0 + got[8:16], got[16:24], jnp.zeros((112, 128), F32)], axis=0)
    asked[...] = jnp.transpose(both).astype(jnp.int32)


def force_body(reply, source, slot, burgers, line, out):
    src = jnp.broadcast_to(source[...], (512, 128))
    match = (src == lax.broadcasted_iota(jnp.int32, (512, 128), 1)).astype(F32).astype(BF16)
    value = reply[...]
    hi, lo = split(value)
    low = (value - hi.astype(F32) - lo.astype(F32)).astype(BF16)
    got = dot(match, hi) + (dot(match, lo) + dot(match, low))
    lane = lax.broadcasted_iota(jnp.int32, (512, 128), 1)
    slot_v = slot[...].astype(jnp.int32)
    mine = jnp.transpose(jnp.where(lane % 8 == slot_v, got, 0.0))
    t = [jnp.sum(mine[c * 8 : c * 8 + 8, :], axis=0, keepdims=True) for c in range(6)]
    b = [burgers[i : i + 1, :] for i in range(3)]
    v = [line[i : i + 1, :] for i in range(3)]
    push_x = t[0] * b[0] + t[5] * b[1] + t[4] * b[2]
    push_y = t[5] * b[0] + t[1] * b[1] + t[3] * b[2]
    push_z = t[4] * b[0] + t[3] * b[1] + t[2] * b[2]
    out[0:1, :] = push_y * v[2] - push_z * v[1]
    out[1:2, :] = push_z * v[0] - push_x * v[2]
    out[2:3, :] = push_x * v[1] - push_y * v[0]


def neighbours(low, high, axis, count):
    ahead = [(i, (i + 1) % count) for i in range(count)]
    back = [((i + 1) % count, i) for i in range(count)]
    return lax.ppermute(high, axis, ahead), lax.ppermute(low, axis, back)


def exchange(values, axis):
    return lax.all_to_all(values, axis, split_axis=0, concat_axis=0, tiled=True)


FACE_X = sds((3, NY, GRID))
FACE_Y = sds((3, NX, GRID))
FIELD_WIRE = (NPY, 3, 8, NX, 128)
WAVE_WIRE = (NPX, 2, NX, 768)


def shards(dist, ids, moduli, seg_source, seg_tile, seg_center, burgers, line_vector):
    fwd_z, inv_z = z_tables()
    fwd_h, inv_h = half_tables()
    tz, tzi = two_parts(fwd_z), two_parts(inv_z)
    tx, txi = two_parts(fwd_h), two_parts(inv_h)
    ty = two_parts(fwd_h.transpose(0, 2, 1))
    tyi = two_parts(inv_h.transpose(0, 2, 1))
    sx, sy, sz = wave_lines()
    weights = two_parts(tile_weights())

    asked, slot = call(request_body, (sds((128, 128), jnp.int32), sds((512, 1))), n_in=3)(
        seg_source, seg_tile.reshape(1, 512), seg_center.reshape(1, 512)
    )
    asked = exchange(asked, ("px", "py"))

    polar, xlo, xhi, ylo, yhi = call(
        polar_body, (sds((6, NX, NY, GRID)), FACE_X, FACE_X, FACE_Y, FACE_Y), n_in=3
    )(dist, ids, moduli)
    xbefore, xafter = neighbours(xlo, xhi, "px", NPX)
    ybefore, yafter = neighbours(ylo, yhi, "py", NPY)
    wire = call(
        forward_z_body,
        sds(FIELD_WIRE),
        [pltpu.VMEM((512, GRID), F32), pltpu.VMEM((1024, 128), F32)],
        n_in=6,
    )(polar, xbefore, xafter, ybefore, yafter, tz)
    got = exchange(wire.reshape(NPY, 384, 128), "py").reshape(FIELD_WIRE)
    pair = [pltpu.VMEM((2, 256, 256), BF16)] * 2
    wire = call(forward_y_body, sds(WAVE_WIRE), pair, n_in=2)(got, ty)
    got = exchange(wire.reshape(NPX, 32, 768), "px").reshape(WAVE_WIRE)
    wire = call(solve_x_body, sds(WAVE_WIRE), [pltpu.VMEM((2, 256, 768), BF16)] * 2, n_in=6)(
        got, tx, txi, sx, sy, sz
    )
    got = exchange(wire.reshape(NPX, 32, 768), "px").reshape(WAVE_WIRE)
    wire = call(inverse_y_body, sds(FIELD_WIRE), pair, n_in=2)(got, tyi)
    got = exchange(wire.reshape(NPY, 384, 128), "py").reshape(FIELD_WIRE)
    disp, xlo, xhi, ylo, yhi = call(
        inverse_z_body,
        (sds((3, NX, NY, GRID)), FACE_X, FACE_X, FACE_Y, FACE_Y),
        [pltpu.VMEM((256, 512), F32), pltpu.VMEM((1024, 128), F32)],
        n_in=2,
    )(got, tzi)
    xbefore, xafter = neighbours(xlo, xhi, "px", NPX)
    ybefore, yafter = neighbours(ylo, yhi, "py", NPY)
    stress, reply = call(
        stress_body,
        (sds((6, NX, NY, GRID)), sds((128, 128))),
        [pltpu.VMEM((512, 1536), BF16)] * 2,
        n_in=10,
    )(disp, xbefore, xafter, ybefore, yafter, polar, ids, moduli, asked, weights)
    reply = exchange(reply, ("px", "py"))
    seg_force = call(force_body, sds((3, 512)), n_in=5)(reply, seg_source, slot, burgers, line_vector)
    return stress, seg_force


def solution(mesh):
    return jax.shard_map(
        shards,
        mesh=mesh,
        in_specs=(
            P(None, "px", "py", None),
            P("px", "py", None),
            P(),
            P(("px", "py"), None),
            P(("px", "py")),
            P(("px", "py")),
            P(None, ("px", "py")),
            P(None, ("px", "py")),
        ),
        out_specs=(P(None, "px", "py", None), P(None, ("px", "py"))),
        check_vma=False,
    )
```

```python
import functools

import jax
import jax.numpy as jnp
import ml_dtypes
import numpy as np
from jax import lax
from jax.experimental import pallas as pl
from jax.experimental.pallas import tpu as pltpu
from jax.sharding import PartitionSpec as P

F32 = jnp.float32
BF16 = jnp.bfloat16
REF_LAMBDA = 1.25
REF_SHEAR = 1.25
GRID = 256
HALF = 128
NPX = 16
NPY = 8
NX = 16
NY = 32
VMEM_LIMIT = 56 * 1024 * 1024
VM = pl.BlockSpec(memory_space=pltpu.VMEM)


def two_parts(table):
    table = np.asarray(table, np.float32)
    high = table.astype(ml_dtypes.bfloat16)
    low = (table - high.astype(np.float32)).astype(ml_dtypes.bfloat16)
    return np.stack([high, low])


def z_tables():
    z = np.arange(GRID)
    fwd = np.zeros((GRID, GRID))
    inv = np.zeros((GRID, GRID))
    for row in range(GRID):
        p, kzlo, ri, kzhi = row // 32, (row // 8) % 4, (row // 4) % 2, row % 4
        wave = 16 * p + 4 * kzhi + kzlo
        angle = 2 * np.pi * ((wave * z) % GRID) / GRID
        if wave == 0:
            line = np.ones(GRID) if ri == 0 else 1.0 - 2.0 * (z % 2)
            fwd[row], inv[row] = line, line / GRID
        else:
            line = np.cos(angle) if ri == 0 else -np.sin(angle)
            fwd[row], inv[row] = line, 2 * line / GRID
    step = np.roll(np.eye(GRID), 1, 1) - np.roll(np.eye(GRID), -1, 1)
    fwd = 0.5 * np.stack([fwd, fwd @ step])
    inv = np.concatenate([inv, inv @ step.T], axis=1)
    return fwd, inv


def half_tables():
    k = np.arange(HALF)
    fwd, inv = [], []
    for e in range(2):
        angle = 2 * np.pi * (((2 * k[:, None] + e) * k[None, :]) % GRID) / GRID
        cos, sin = np.cos(angle), np.sin(angle)
        fwd.append(np.block([[cos, sin], [-sin, cos]]))
        inv.append(np.block([[cos.T, -sin.T], [sin.T, cos.T]]) / GRID)
    return np.stack(fwd), np.stack(inv)


def sines():
    wave = np.arange(GRID)
    line = np.sin(2 * np.pi * wave / GRID)
    line[wave % HALF == 0] = 0.0
    return line


def wave_lines():
    line = sines()
    sx = np.stack([line[0::2], line[1::2]])[:, :, None] * np.ones((1, 1, 128))
    sy = np.concatenate([line[0::2], line[1::2]])[None, :]
    sz = line[:128, None] * np.ones((1, 128))
    return sx.astype(np.float32), sy.astype(np.float32), sz.astype(np.float32)


def tile_weights():
    v = np.arange(128, dtype=np.float64)
    weights = np.exp(-((v[None, :] - v[:, None]) ** 2) / (2.0 * 16.0**2))
    return weights / weights.sum(axis=1, keepdims=True)


def split(values):
    high = values.astype(BF16)
    low = (values - high.astype(F32)).astype(BF16)
    return high, low


def dot(a, b, dims=((1,), (0,))):
    return lax.dot_general(a, b, (dims, ((), ())), preferred_element_type=F32)


def dot3(a, b, dims=((1,), (0,))):
    (ah, al), (bh, bl) = a, b
    return dot(ah, bh, dims) + (dot(ah, bl, dims) + dot(al, bh, dims))


def swap_groups(values):
    count = len(values)
    width = 128 // count
    lane = lax.broadcasted_iota(jnp.int32, values[0].shape, values[0].ndim - 1)
    axis = values[0].ndim - 1
    values = list(values)
    step = 1
    while step < count:
        first = ((lane // (width * step)) % 2) == 0
        out = list(values)
        for i in range(count):
            if i & step == 0:
                low, high = values[i], values[i + step]
                out[i] = jnp.where(first, low, pltpu.roll(high, width * step, axis))
                out[i + step] = jnp.where(first, pltpu.roll(low, 128 - width * step, axis), high)
        values = out
        step *= 2
    return values


def call(body, out_shape, scratch=(), n_in=0, n_any=0, collective=None):
    multi = isinstance(out_shape, (list, tuple))
    remote = {} if collective is None else {"collective_id": collective, "has_side_effects": True}
    return pl.pallas_call(
        body,
        out_shape=out_shape,
        in_specs=[VM] * n_in + [pl.BlockSpec(memory_space=pl.ANY)] * n_any,
        out_specs=[VM] * len(out_shape) if multi else VM,
        scratch_shapes=list(scratch),
        compiler_params=pltpu.CompilerParams(vmem_limit_bytes=VMEM_LIMIT, **remote),
    )


def send(src, dst, sems, where):
    return pltpu.make_async_remote_copy(
        src_ref=src,
        dst_ref=dst,
        send_sem=sems[0],
        recv_sem=sems[1],
        device_id=where,
        device_id_type=pl.DeviceIdType.MESH,
    )


def greet(px, py):
    barrier = pltpu.get_barrier_semaphore()

    def row(d, carry):
        pl.semaphore_signal(
            barrier, inc=1, device_id=(px, lax.rem(py + d, NPY)), device_id_type=pl.DeviceIdType.MESH
        )
        return carry

    def column(d, carry):
        pl.semaphore_signal(
            barrier, inc=1, device_id=(lax.rem(px + d, NPX), py), device_id_type=pl.DeviceIdType.MESH
        )
        return carry

    lax.fori_loop(1, NPY, row, 0)
    lax.fori_loop(1, NPX, column, 0)
    pl.semaphore_wait(barrier, NPX + NPY - 2)


class Exchange:
    def __init__(self, axis, wire, got, sems, own_sem):
        self.count = NPX if axis == "px" else NPY
        self.axis, self.wire, self.got, self.sems, self.own_sem = axis, wire, got, sems, own_sem
        self.px, self.py = lax.axis_index("px"), lax.axis_index("py")
        self.me = self.px if axis == "px" else self.py

    def copy(self, d, c):
        peer = lax.rem(self.me + d, self.count)
        where = (peer, self.py) if self.axis == "px" else (self.px, peer)
        sems = (self.sems.at[0, c, d], self.sems.at[1, c, d])
        return send(self.wire.at[c, peer], self.got.at[c, self.me], sems, where)

    def own(self, c):
        return pltpu.make_async_copy(
            self.wire.at[c, self.me], self.got.at[c, self.me], self.own_sem.at[c]
        )

    def start(self, c):
        self.own(c).start()
        lax.fori_loop(1, self.count, lambda d, k: (self.copy(d, c).start(), k)[1], 0)

    def arrive(self, c):
        self.own(c).wait()
        lax.fori_loop(1, self.count, lambda d, k: (self.copy(d, c).wait_recv(), k)[1], 0)

    def finish(self, c):
        lax.fori_loop(1, self.count, lambda d, k: (self.copy(d, c).wait_send(), k)[1], 0)


def exchange_scratch(axis, parts, block, dtype=F32):
    count = NPX if axis == "px" else NPY
    return [
        pltpu.VMEM((parts, count) + block, dtype),
        pltpu.VMEM((parts, count) + block, dtype),
        pltpu.SemaphoreType.DMA((2, parts, count)),
        pltpu.SemaphoreType.DMA((parts,)),
    ]


def sds(shape, dtype=F32):
    return jax.ShapeDtypeStruct(shape, dtype)


def moduli_of(table, ids):
    lame, shear = [], []
    for half in range(2):
        index = ids[:, half * 128 : (half + 1) * 128]
        lame.append(jnp.take_along_axis(table, index, axis=1))
        shear.append(jnp.take_along_axis(table, index + 64, axis=1))
    return jnp.concatenate(lame, axis=1), jnp.concatenate(shear, axis=1)


def table_of(moduli_ref):
    row = jnp.concatenate([moduli_ref[0:1, :], moduli_ref[1:2, :]], axis=1)
    return jnp.broadcast_to(row, (NY, 128))


def polar_part(dist, ids, moduli, polar, xlo, xhi, ylo, yhi):
    table = table_of(moduli)

    def at_x(x, carry):
        lame, shear = moduli_of(table, ids[x])
        exx, eyy, ezz = dist[0, x], dist[4, x], dist[8, x]
        trace = lame * (exx + eyy + ezz)
        twice = shear + shear
        polar[0, x] = -(twice * exx + trace)
        polar[1, x] = -(twice * eyy + trace)
        polar[2, x] = -(twice * ezz + trace)
        polar[3, x] = -(shear * (dist[5, x] + dist[7, x]))
        polar[4, x] = -(shear * (dist[2, x] + dist[6, x]))
        polar[5, x] = -(shear * (dist[1, x] + dist[3, x]))
        return carry

    lax.fori_loop(0, NX, at_x, 0)
    for slot, comp in enumerate((0, 5, 4)):
        xlo[slot] = polar[comp, 0]
        xhi[slot] = polar[comp, NX - 1]
    for slot, comp in enumerate((5, 1, 3)):
        ylo[slot] = polar[comp, :, 0, :]
        yhi[slot] = polar[comp, :, NY - 1, :]


def row_of(device):
    return (device % NPY) * NPX + device // NPY


def request_part(source, tile, centre, asked, slot_out):
    src = jnp.broadcast_to(source[...], (512, 128))
    src = row_of(src).astype(F32)
    src_lane = jnp.transpose(src)[0:1, :]
    same = src[:, 0:1] == src_lane
    first = lax.broadcasted_iota(jnp.int32, (512, 512), 0)
    second = lax.broadcasted_iota(jnp.int32, (512, 512), 1)
    slot_lane = jnp.sum(jnp.where(same & (first < second), 1.0, 0.0), axis=0, keepdims=True)
    slot_out[...] = jnp.sum(jnp.where(same & (second < first), 1.0, 0.0), axis=1, keepdims=True)
    match = (src == lax.broadcasted_iota(jnp.int32, (512, 128), 1).astype(F32)).astype(F32).astype(BF16)
    row = lax.broadcasted_iota(jnp.int32, (8, 512), 0).astype(F32)
    here = row == slot_lane
    tile_v = tile[...]
    values = [tile_v // 8, tile_v % 8, centre[...]]
    rows = [jnp.where(here, v.astype(F32), 0.0) for v in values]
    stacked = jnp.concatenate(rows + [jnp.zeros((8, 512), F32)], axis=0).astype(BF16)
    got = dot(stacked, match)
    both = jnp.concatenate([got[0:8] * 8.0 + got[8:16], got[16:24], jnp.zeros((112, 128), F32)], axis=0)
    asked[...] = jnp.transpose(both).astype(jnp.int32)


def prepare_body(
    dist, ids, moduli, source, tile, centre, polar, xlo, xhi, ylo, yhi, asked, slot
):
    request_part(source, tile, centre, asked, slot)
    polar_part(dist, ids, moduli, polar, xlo, xhi, ylo, yhi)


def shift_y(values, before, after):
    row = lax.broadcasted_iota(jnp.int32, values.shape, 0)
    up = jnp.where(row == NY - 1, after, pltpu.roll(values, NY - 1, 0))
    down = jnp.where(row == 0, before, pltpu.roll(values, 1, 0))
    return up - down


def forward_z(c, polar, faces, tz, wire, force, swap):
    cx, cy, cz = ((0, 5, 4), (5, 1, 3), (4, 3, 2))[c]
    xbefore, xafter, ybefore, yafter = faces
    for x in range(NX):
        after = xafter[c] if x == NX - 1 else polar[cx, x + 1]
        before = xbefore[c] if x == 0 else polar[cx, x - 1]
        grad_y = shift_y(polar[cy, x], ybefore[c, x : x + 1], yafter[c, x : x + 1])
        for part, values in enumerate(((after - before) + grad_y, polar[cz, x])):
            hi, lo = split(values)
            force[0, part, x * NY : (x + 1) * NY, :] = hi
            force[1, part, x * NY : (x + 1) * NY, :] = lo
    last = ((1,), (1,))
    waves = dot3((tz[0, 0], tz[1, 0]), (force[0, 0], force[1, 0]), last)
    waves = waves + dot3((tz[0, 1], tz[1, 1]), (force[0, 1], force[1, 1]), last)
    for p in range(NPY):
        for xg in range(4):
            tiles = [
                waves[p * 32 + kzlo * 8 : p * 32 + kzlo * 8 + 8, xg * 128 : xg * 128 + 128]
                for kzlo in range(4)
            ]
            for x4, tile in enumerate(swap_groups(tiles)):
                x = xg * 4 + x4
                swap[p * 128 + x * 8 : p * 128 + x * 8 + 8, :] = tile
        for s in range(8):
            wire[c, p, s] = swap[pl.ds(p * 128 + s, NX, stride=8), :]


def forward_y(c, got, ty, wire, rows):
    for ri in range(2):
        for kzhi in range(4):
            s = ri * 4 + kzhi
            low = swap_groups([got[c, q, s] for q in range(4)])
            high = swap_groups([got[c, q + 4, s] for q in range(4)])
            for kzlo in range(4):
                row = (kzhi * 4 + kzlo) * NX
                for e in range(2):
                    hi, lo = split(low[kzlo] + high[kzlo] if e == 0 else low[kzlo] - high[kzlo])
                    rows[0, e, row : row + NX, ri * 128 : ri * 128 + 128] = hi
                    rows[1, e, row : row + NX, ri * 128 : ri * 128 + 128] = lo
    for e in range(2):
        out = dot3((rows[0, e], rows[1, e]), (ty[0, e], ty[1, e]))
        for kz in range(NX):
            wire[c, kz, :, e * 256 : e * 256 + 256] = out[kz * NX : kz * NX + NX, :]


def forward_x(c, got, tx, waves, rows):
    for q in range(8):
        a, b = got[c, q], got[c, q + 8]
        for ex in range(2):
            hi, lo = split(a + b if ex == 0 else a - b)
            for ri in range(2):
                row = ri * 128 + q * 16
                for e in range(2):
                    lane = e * 256 + ri * 128
                    rows[0, ex, row : row + 16, e * 128 : e * 128 + 128] = hi[:, lane : lane + 128]
                    rows[1, ex, row : row + 16, e * 128 : e * 128 + 128] = lo[:, lane : lane + 128]
    for ex in range(2):
        waves[ex, c] = dot3((tx[0, ex], tx[1, ex]), (rows[0, ex], rows[1, ex]))


def solve(waves, solved, sx, sy, sz, py, px):
    sy = sy[...]
    sz = sz[pl.ds(py * 16 + px, 1), :]
    sz = jnp.concatenate([sz, sz], axis=1)
    coupling = (REF_LAMBDA + REF_SHEAR) / (REF_LAMBDA + 2.0 * REF_SHEAR)
    rest = sy * sy + sz * sz
    for ex in range(2):
        wx = jnp.concatenate([sx[ex], sx[ex]], axis=1)
        squared = wx * wx + rest
        null = squared == 0.0
        inverse = jnp.where(null, 0.0, 1.0 / jnp.where(null, 1.0, squared))
        scale = inverse * (1.0 / REF_SHEAR)
        for ri in range(2):
            parts = [waves[ex, c, ri * 128 : ri * 128 + 128, :] for c in range(3)]
            common = coupling * inverse * (wx * parts[0] + sy * parts[1] + sz * parts[2])
            for c, line in enumerate((wx, sy, sz)):
                hi, lo = split(scale * (parts[c] - common * line))
                solved[0, ex, c, ri * 128 : ri * 128 + 128, :] = hi
                solved[1, ex, c, ri * 128 : ri * 128 + 128, :] = lo


def inverse_x(c, solved, txi, wire):
    backs = [dot3((txi[0, ex], txi[1, ex]), (solved[0, ex, c], solved[1, ex, c])) for ex in range(2)]
    for half, out in enumerate((backs[0] + backs[1], backs[0] - backs[1])):
        for q in range(8):
            for ri in range(2):
                row = ri * 128 + q * 16
                for e in range(2):
                    lane = e * 256 + ri * 128
                    wire[c, half * 8 + q, :, lane : lane + 128] = out[row : row + 16, e * 128 : e * 128 + 128]


def inverse_y(c, got, tyi, wire):
    outs = []
    for e in range(2):
        rows = jnp.concatenate([got[c, kz, :, e * 256 : e * 256 + 256] for kz in range(NX)], axis=0)
        outs.append(dot3(split(rows), (tyi[0, e], tyi[1, e])))
    for half, out in enumerate((outs[0] + outs[1], outs[0] - outs[1])):
        for ri in range(2):
            for kzhi in range(4):
                tiles = [
                    out[(kzhi * 4 + k) * NX : (kzhi * 4 + k + 1) * NX, ri * 128 : ri * 128 + 128]
                    for k in range(4)
                ]
                for q4, tile in enumerate(swap_groups(tiles)):
                    wire[c, half * 4 + q4, ri * 4 + kzhi] = tile


def inverse_z(c, got, tzi, disp, grad, yface, waves, swap):
    for p in range(NPY):
        for s in range(8):
            swap[p * 128 + s * 16 : p * 128 + s * 16 + 16, :] = got[c, p, s]
        for xg in range(4):
            tiles = [swap[pl.ds(p * 128 + xg * 4 + x4, 8, stride=16), :] for x4 in range(4)]
            for kzlo, tile in enumerate(swap_groups(tiles)):
                row = p * 32 + kzlo * 8
                waves[row : row + 8, xg * 128 : xg * 128 + 128] = tile
    turned = split(jnp.transpose(waves[...]))
    out = dot3(turned, (tzi[0, :, :256], tzi[1, :, :256]))
    for x in range(NX):
        disp[c, x] = out[x * NY : (x + 1) * NY, :]
        yface[0, c, x : x + 1] = out[x * NY : x * NY + 1, :]
        yface[1, c, x : x + 1] = out[x * NY + NY - 1 : x * NY + NY, :]
    out = dot3(turned, (tzi[0, :, 256:], tzi[1, :, 256:]))
    for x in range(NX):
        grad[c, x] = out[x * NY : (x + 1) * NY, :]


def faces_copies(px, py, sources, targets, sems):
    left, right = lax.rem(px + NPX - 1, NPX), lax.rem(px + 1, NPX)
    down, up = lax.rem(py + NPY - 1, NPY), lax.rem(py + 1, NPY)
    plan = ((0, 1, (left, py)), (1, 0, (right, py)), (2, 3, (px, down)), (3, 2, (px, up)))
    return [send(sources[a], targets[b], (sems.at[0, b], sems.at[1, b]), where) for a, b, where in plan]


def solve_body(
    polar, xlo, xhi, ylo, yhi, asked_out, sx, sy, sz, tz_h, ty_h, tx_h, txi_h, tyi_h, tzi_h,
    disp, grad, xbefore, xafter, ybefore, yafter, asked,
    w1, g1, s1, o1, w2, g2, s2, o2, w3, g3, s3, o3, w4, g4, s4, o4,
    wa, ga, sa, oa, wb, gb, sb, ob,
    fx, fy, face_sem, back_sem, hx, hy, yface,
    tz, ty, tx, txi, tyi, tzi, table_sem,
    force, swap, rows, waves, solved, lines,
):
    px, py = lax.axis_index("px"), lax.axis_index("py")
    tables = [
        pltpu.make_async_copy(src, dst, table_sem.at[i])
        for i, (src, dst) in enumerate(
            ((tz_h, tz), (ty_h, ty), (tx_h, tx), (txi_h, txi), (tyi_h, tyi), (tzi_h, tzi))
        )
    ]
    for table in tables:
        table.start()
    greet(px, py)
    halo = faces_copies(
        px, py, (xlo, xhi, ylo, yhi), (fx.at[0], fx.at[1], fy.at[0], fy.at[1]), face_sem
    )
    for copy in halo:
        copy.start()
    ex1 = Exchange("py", w1, g1, s1, o1)
    ex2 = Exchange("px", w2, g2, s2, o2)
    ex3 = Exchange("px", w3, g3, s3, o3)
    ex4 = Exchange("py", w4, g4, s4, o4)
    exa = Exchange("py", wa, ga, sa, oa)
    exb = Exchange("px", wb, gb, sb, ob)
    for p in range(NPY):
        wa[0, p] = asked_out[p * NPX : p * NPX + NPX, :]
    exa.start(0)
    tables[0].wait()
    for copy in halo:
        copy.wait_recv()
    for c in range(3):
        forward_z(c, polar, (fx.at[0], fx.at[1], fy.at[0], fy.at[1]), tz, w1, force, swap)
        ex1.start(c)
    exa.arrive(0)
    asked[...] = ga[0].reshape(128, 128)
    for p in range(NPX):
        wb[0, p] = asked[pl.ds(p, NPY, stride=NPX), :]
    exb.start(0)
    tables[1].wait()
    for c in range(3):
        ex1.arrive(c)
        forward_y(c, g1, ty, w2, rows)
        ex2.start(c)
    tables[2].wait()
    for c in range(3):
        ex2.arrive(c)
        forward_x(c, g2, tx, waves, rows)
    solve(waves, solved, sx, sy, sz, py, px)
    tables[3].wait()
    for c in range(3):
        inverse_x(c, solved, txi, w3)
        ex3.start(c)
    tables[4].wait()
    exb.arrive(0)
    for p in range(NPX):
        asked[p * NPY : p * NPY + NPY, :] = gb[0, p]
    for c in range(3):
        ex3.arrive(c)
        inverse_y(c, g3, tyi, w4)
        ex4.start(c)
    tables[5].wait()
    backs = []
    for c in range(3):
        ex4.arrive(c)
        inverse_z(c, g4, tzi, disp, grad, yface, lines, swap)
        back = faces_copies(
            px,
            py,
            (disp.at[c, 0], disp.at[c, NX - 1], yface.at[0, c], yface.at[1, c]),
            (hx.at[0, c], hx.at[1, c], hy.at[0, c], hy.at[1, c]),
            back_sem.at[c],
        )
        for copy in back:
            copy.start()
        backs += back
    for copy in backs:
        copy.wait_recv()
    xbefore[...] = hx[0]
    xafter[...] = hx[1]
    ybefore[...] = hy[0]
    yafter[...] = hy[1]
    for copy in halo + backs:
        copy.wait_send()
    exa.finish(0)
    exb.finish(0)
    for c in range(3):
        for ex in (ex1, ex2, ex3, ex4):
            ex.finish(c)


def stress_body(
    disp, grad, xbefore, xafter, ybefore, yafter, polar, ids, moduli, asked, weights,
    stress, reply, rows_h, rows_l,
):
    table = table_of(moduli)
    for x in range(NX):
        lame, shear = moduli_of(table, ids[x])
        gx, gy, gz = [], [], []
        for c in range(3):
            after = xafter[c] if x == NX - 1 else disp[c, x + 1]
            before = xbefore[c] if x == 0 else disp[c, x - 1]
            gx.append(after - before)
            gy.append(shift_y(disp[c, x], ybefore[c, x : x + 1], yafter[c, x : x + 1]))
            gz.append(grad[c, x])
        trace = (0.5 * lame) * (gx[0] + gy[1] + gz[2])
        half = 0.5 * shear
        parts = (
            shear * gx[0] + trace,
            shear * gy[1] + trace,
            shear * gz[2] + trace,
            half * (gz[1] + gy[2]),
            half * (gz[0] + gx[2]),
            half * (gy[0] + gx[1]),
        )
        for c, part in enumerate(parts):
            total = part + polar[c, x]
            stress[c, x] = total
            hi, lo = split(total)
            rows_h[x * NY : (x + 1) * NY, c * 256 : c * 256 + 256] = hi
            rows_l[x * NY : (x + 1) * NY, c * 256 : c * 256 + 256] = lo
    column = lax.broadcasted_iota(jnp.int32, (128, 512), 1)
    lane = lax.broadcasted_iota(jnp.int32, (128, 128), 1)
    lane256 = lax.broadcasted_iota(jnp.int32, (128, 256), 1)
    out = jnp.zeros((128, 128), F32)
    wh, wl = weights[0], weights[1]
    for k in range(8):
        tile = asked[:, k : k + 1]
        centre = asked[:, 8 + k : 9 + k]
        pick = (column == tile // 2).astype(F32).astype(BF16)
        picked = dot(pick, rows_h[...]) + dot(pick, rows_l[...])
        at = (lane == centre).astype(F32).astype(BF16)
        row = dot(at, wh) + dot(at, wl)
        weight = jnp.where(lane256 // 128 == tile % 2, jnp.concatenate([row, row], axis=1), 0.0)
        for c in range(6):
            value = jnp.sum(picked[:, c * 256 : c * 256 + 256] * weight, axis=1, keepdims=True)
            out = jnp.where(lane == c * 8 + k, value, out)
    reply[...] = out


def force_body(
    reply, source, slot, burgers, line, out, wa, ga, sa, oa, wb, gb, sb, ob, turn
):
    px, py = lax.axis_index("px"), lax.axis_index("py")
    greet(px, py)
    exa = Exchange("px", wa, ga, sa, oa)
    exb = Exchange("py", wb, gb, sb, ob)
    for p in range(NPX):
        wa[0, p] = reply[p * NPY : p * NPY + NPY, :]
    exa.start(0)
    src = row_of(jnp.broadcast_to(source[...], (512, 128)))
    match = (src == lax.broadcasted_iota(jnp.int32, (512, 128), 1)).astype(F32).astype(BF16)
    exa.arrive(0)
    turn[...] = ga[0].reshape(128, 128)
    for p in range(NPY):
        wb[0, p] = turn[pl.ds(p, NPX, stride=NPY), :]
    exb.start(0)
    exb.arrive(0)
    value = gb[0].reshape(128, 128)
    hi, lo = split(value)
    low = (value - hi.astype(F32) - lo.astype(F32)).astype(BF16)
    got = dot(match, hi) + (dot(match, lo) + dot(match, low))
    lane = lax.broadcasted_iota(jnp.int32, (512, 128), 1)
    slot_v = slot[...].astype(jnp.int32)
    mine = jnp.transpose(jnp.where(lane % 8 == slot_v, got, 0.0))
    t = [jnp.sum(mine[c * 8 : c * 8 + 8, :], axis=0, keepdims=True) for c in range(6)]
    b = [burgers[i : i + 1, :] for i in range(3)]
    v = [line[i : i + 1, :] for i in range(3)]
    push_x = t[0] * b[0] + t[5] * b[1] + t[4] * b[2]
    push_y = t[5] * b[0] + t[1] * b[1] + t[3] * b[2]
    push_z = t[4] * b[0] + t[3] * b[1] + t[2] * b[2]
    out[0:1, :] = push_y * v[2] - push_z * v[1]
    out[1:2, :] = push_z * v[0] - push_x * v[2]
    out[2:3, :] = push_x * v[1] - push_y * v[0]
    exa.finish(0)
    exb.finish(0)


FACE_X = sds((3, NY, GRID))
FACE_Y = sds((3, NX, GRID))
FIELD = sds((3, NX, NY, GRID))


def solve_scratch():
    half = pltpu.VMEM((2, 2, 256, 256), BF16)
    field = (8, NX, 128)
    wave = (NX, 512)
    return (
        exchange_scratch("py", 3, field)
        + exchange_scratch("px", 3, wave)
        + exchange_scratch("px", 3, wave)
        + exchange_scratch("py", 3, field)
        + exchange_scratch("py", 1, (NPX, 128), jnp.int32)
        + exchange_scratch("px", 1, (NPY, 128), jnp.int32)
        + [pltpu.VMEM((2, 3, NY, GRID), F32), pltpu.VMEM((2, 3, NX, GRID), F32)]
        + [pltpu.SemaphoreType.DMA((2, 4)), pltpu.SemaphoreType.DMA((3, 2, 4))]
        + [pltpu.VMEM((2, 3, NY, GRID), F32), pltpu.VMEM((2, 3, NX, GRID), F32)]
        + [pltpu.VMEM((2, 3, NX, GRID), F32)]
        + [half] * 5
        + [pltpu.VMEM((2, 256, 512), BF16), pltpu.SemaphoreType.DMA((6,))]
        + [pltpu.VMEM((2, 2, 512, 256), BF16), pltpu.VMEM((1024, 128), F32), half]
        + [pltpu.VMEM((2, 3, 256, 256), F32), pltpu.VMEM((2, 2, 3, 256, 256), BF16)]
        + [pltpu.VMEM((256, 512), F32)]
    )


def shards(dist, ids, moduli, seg_source, seg_tile, seg_center, burgers, line_vector):
    fwd_z, inv_z = z_tables()
    fwd_h, inv_h = half_tables()
    tz, tzi = two_parts(fwd_z), two_parts(inv_z)
    tx, txi = two_parts(fwd_h), two_parts(inv_h)
    ty = two_parts(fwd_h.transpose(0, 2, 1))
    tyi = two_parts(inv_h.transpose(0, 2, 1))
    sx, sy, sz = wave_lines()
    weights = two_parts(tile_weights())

    faces = (FACE_X, FACE_X, FACE_Y, FACE_Y)
    polar, xlo, xhi, ylo, yhi, asked, slot = call(
        prepare_body,
        (sds((6, NX, NY, GRID)),) + faces + (sds((128, 128), jnp.int32), sds((512, 1))),
        n_in=6,
    )(dist, ids, moduli, seg_source, seg_tile.reshape(1, 512), seg_center.reshape(1, 512))
    disp, grad, xbefore, xafter, ybefore, yafter, asked = call(
        solve_body,
        (FIELD, FIELD) + faces + (sds((128, 128), jnp.int32),),
        solve_scratch(),
        n_in=9,
        n_any=6,
        collective=0,
    )(polar, xlo, xhi, ylo, yhi, asked, sx, sy, sz, tz, ty, tx, txi, tyi, tzi)
    stress, reply = call(
        stress_body,
        (sds((6, NX, NY, GRID)), sds((128, 128))),
        [pltpu.VMEM((512, 1536), BF16)] * 2,
        n_in=11,
    )(disp, grad, xbefore, xafter, ybefore, yafter, polar, ids, moduli, asked, weights)
    seg_force = call(
        force_body,
        sds((3, 512)),
        exchange_scratch("px", 1, (NPY, 128))
        + exchange_scratch("py", 1, (NPX, 128))
        + [pltpu.VMEM((128, 128), F32)],
        n_in=5,
        collective=1,
    )(reply, seg_source, slot, burgers, line_vector)
    return stress, seg_force


def solution(mesh):
    return jax.shard_map(
        shards,
        mesh=mesh,
        in_specs=(
            P(None, "px", "py", None),
            P("px", "py", None),
            P(),
            P(("px", "py"), None),
            P(("px", "py")),
            P(("px", "py")),
            P(None, ("px", "py")),
            P(None, ("px", "py")),
        ),
        out_specs=(P(None, "px", "py", None), P(None, ("px", "py"))),
        check_vma=False,
    )
```

```python
import functools

import jax
import jax.numpy as jnp
import ml_dtypes
import numpy as np
from jax import lax
from jax.experimental import pallas as pl
from jax.experimental.pallas import tpu as pltpu
from jax.sharding import PartitionSpec as P

F32 = jnp.float32
BF16 = jnp.bfloat16
REF_LAMBDA = 1.25
REF_SHEAR = 1.25
GRID = 256
HALF = 128
NPX = 16
NPY = 8
NX = 16
NY = 32
VMEM_LIMIT = 60 * 1024 * 1024
VM = pl.BlockSpec(memory_space=pltpu.VMEM)


def two_parts(table):
    table = np.asarray(table, np.float32)
    high = table.astype(ml_dtypes.bfloat16)
    low = (table - high.astype(np.float32)).astype(ml_dtypes.bfloat16)
    return np.stack([high, low])


def z_tables():
    z = np.arange(GRID)
    fwd = np.zeros((GRID, GRID))
    inv = np.zeros((GRID, GRID))
    for row in range(GRID):
        p, kzlo, ri, kzhi = row // 32, (row // 8) % 4, (row // 4) % 2, row % 4
        wave = 16 * p + 4 * kzhi + kzlo
        angle = 2 * np.pi * ((wave * z) % GRID) / GRID
        if wave == 0:
            line = np.ones(GRID) if ri == 0 else 1.0 - 2.0 * (z % 2)
            fwd[row], inv[row] = line, line / GRID
        else:
            line = np.cos(angle) if ri == 0 else -np.sin(angle)
            fwd[row], inv[row] = line, 2 * line / GRID
    step = np.roll(np.eye(GRID), 1, 1) - np.roll(np.eye(GRID), -1, 1)
    fwd = 0.5 * np.stack([fwd, fwd @ step])
    inv = np.concatenate([inv, inv @ step.T], axis=1)
    return fwd, inv


def half_tables():
    k = np.arange(HALF)
    fwd, inv = [], []
    for e in range(2):
        angle = 2 * np.pi * (((2 * k[:, None] + e) * k[None, :]) % GRID) / GRID
        cos, sin = np.cos(angle), np.sin(angle)
        fwd.append(np.block([[cos, sin], [-sin, cos]]))
        inv.append(np.block([[cos.T, -sin.T], [sin.T, cos.T]]) / GRID)
    return np.stack(fwd), np.stack(inv)


def sines():
    wave = np.arange(GRID)
    line = np.sin(2 * np.pi * wave / GRID)
    line[wave % HALF == 0] = 0.0
    return line


def wave_lines():
    line = sines()
    sx = np.stack([line[0::2], line[1::2]])[:, :, None] * np.ones((1, 1, 128))
    sy = np.concatenate([line[0::2], line[1::2]])[None, :]
    sz = line[:128, None] * np.ones((1, 128))
    return sx.astype(np.float32), sy.astype(np.float32), sz.astype(np.float32)


def tile_weights():
    v = np.arange(128, dtype=np.float64)
    weights = np.exp(-((v[None, :] - v[:, None]) ** 2) / (2.0 * 16.0**2))
    return weights / weights.sum(axis=1, keepdims=True)


def split(values):
    high = values.astype(BF16)
    low = (values - high.astype(F32)).astype(BF16)
    return high, low


def dot(a, b, dims=((1,), (0,))):
    return lax.dot_general(a, b, (dims, ((), ())), preferred_element_type=F32)


def dot3(a, b, dims=((1,), (0,))):
    (ah, al), (bh, bl) = a, b
    return dot(ah, bh, dims) + (dot(ah, bl, dims) + dot(al, bh, dims))


def swap_groups(values):
    count = len(values)
    width = 128 // count
    lane = lax.broadcasted_iota(jnp.int32, values[0].shape, values[0].ndim - 1)
    axis = values[0].ndim - 1
    values = list(values)
    step = 1
    while step < count:
        first = ((lane // (width * step)) % 2) == 0
        out = list(values)
        for i in range(count):
            if i & step == 0:
                low, high = values[i], values[i + step]
                out[i] = jnp.where(first, low, pltpu.roll(high, width * step, axis))
                out[i + step] = jnp.where(first, pltpu.roll(low, 128 - width * step, axis), high)
        values = out
        step *= 2
    return values


def send(src, dst, sems, where):
    return pltpu.make_async_remote_copy(
        src_ref=src,
        dst_ref=dst,
        send_sem=sems[0],
        recv_sem=sems[1],
        device_id=where,
        device_id_type=pl.DeviceIdType.MESH,
    )


def greet(px, py):
    barrier = pltpu.get_barrier_semaphore()
    for d in range(1, NPY):
        where = (px, lax.rem(py + d, NPY))
        pl.semaphore_signal(barrier, inc=1, device_id=where, device_id_type=pl.DeviceIdType.MESH)
    for d in range(1, NPX):
        where = (lax.rem(px + d, NPX), py)
        pl.semaphore_signal(barrier, inc=1, device_id=where, device_id_type=pl.DeviceIdType.MESH)


class Exchange:
    def __init__(self, axis, wire, got, sems, own_sem):
        self.count = NPX if axis == "px" else NPY
        self.axis, self.wire, self.got, self.sems, self.own_sem = axis, wire, got, sems, own_sem
        self.px, self.py = lax.axis_index("px"), lax.axis_index("py")
        self.me = self.px if axis == "px" else self.py

    def own(self, part):
        return pltpu.make_async_copy(
            self.wire.at[part, self.me], self.got.at[part, self.me], self.own_sem.at[part]
        )

    def start(self, part):
        for d in range(1, self.count):
            peer = lax.rem(self.me + d, self.count)
            where = (peer, self.py) if self.axis == "px" else (self.px, peer)
            sems = (self.sems.at[0, part], self.sems.at[1, part])
            send(self.wire.at[part, peer], self.got.at[part, self.me], sems, where).start()
        self.own(part).start()

    def all(self, side, part):
        block = self.got.at[part, pl.ds(0, self.count - 1)]
        return pltpu.make_async_copy(block, block, self.sems.at[side, part])

    def arrive(self, part):
        self.own(part).wait()
        self.all(1, part).wait()

    def finish(self, part):
        self.all(0, part).wait()


def exchange_scratch(axis, parts, block, dtype=F32):
    count = NPX if axis == "px" else NPY
    return [
        pltpu.VMEM((parts, count) + block, dtype),
        pltpu.VMEM((parts, count) + block, dtype),
        pltpu.SemaphoreType.DMA((2, parts)),
        pltpu.SemaphoreType.DMA((parts,)),
    ]


def sds(shape, dtype=F32):
    return jax.ShapeDtypeStruct(shape, dtype)


def moduli_of(table, ids):
    lame, shear = [], []
    for half in range(2):
        index = ids[:, half * 128 : (half + 1) * 128]
        lame.append(jnp.take_along_axis(table, index, axis=1))
        shear.append(jnp.take_along_axis(table, index + 64, axis=1))
    return jnp.concatenate(lame, axis=1), jnp.concatenate(shear, axis=1)


def table_of(moduli_ref):
    row = jnp.concatenate([moduli_ref[0:1, :], moduli_ref[1:2, :]], axis=1)
    return jnp.broadcast_to(row, (NY, 128))


def polar_part(first, count, dist, ids, table, polar, moduli):
    def at_x(x, carry):
        lame, shear = moduli_of(table, ids[x])
        moduli[0, x] = lame
        moduli[1, x] = shear
        exx, eyy, ezz = dist[0, x], dist[4, x], dist[8, x]
        trace = lame * (exx + eyy + ezz)
        twice = shear + shear
        polar[0, x] = -(twice * exx + trace)
        polar[1, x] = -(twice * eyy + trace)
        polar[2, x] = -(twice * ezz + trace)
        polar[3, x] = -(shear * (dist[5, x] + dist[7, x]))
        polar[4, x] = -(shear * (dist[2, x] + dist[6, x]))
        polar[5, x] = -(shear * (dist[1, x] + dist[3, x]))
        return carry

    lax.fori_loop(first, first + count, at_x, 0)


def row_of(device):
    return (device % NPY) * NPX + device // NPY


def request_part(source, tile, centre, asked):
    src_lane = row_of(source[...]).astype(F32)
    src = jnp.transpose(jnp.broadcast_to(src_lane, (128, 512)))
    same = src[:, 0:1] == src_lane
    first = lax.broadcasted_iota(jnp.int32, (512, 512), 0)
    second = lax.broadcasted_iota(jnp.int32, (512, 512), 1)
    slot_lane = jnp.sum(jnp.where(same & (first < second), 1.0, 0.0), axis=0, keepdims=True)
    match = (src == lax.broadcasted_iota(jnp.int32, (512, 128), 1).astype(F32)).astype(F32).astype(BF16)
    row = lax.broadcasted_iota(jnp.int32, (8, 512), 0).astype(F32)
    here = row == slot_lane
    tile_v = tile[...]
    values = [tile_v // 8, tile_v % 8, centre[...]]
    rows = [jnp.where(here, v.astype(F32), 0.0) for v in values]
    stacked = jnp.concatenate(rows + [jnp.zeros((8, 512), F32)], axis=0).astype(BF16)
    got = dot(stacked, match)
    both = jnp.concatenate([got[0:8] * 8.0 + got[8:16], got[16:24], jnp.zeros((112, 128), F32)], axis=0)
    asked[...] = jnp.transpose(both).astype(jnp.int32)
    return slot_lane


def shift_y(values, before, after):
    row = lax.broadcasted_iota(jnp.int32, values.shape, 0)
    up = jnp.where(row == NY - 1, after, pltpu.roll(values, NY - 1, 0))
    down = jnp.where(row == 0, before, pltpu.roll(values, 1, 0))
    return up - down


LAST = ((1,), (1,))


def forward_z_local(c, polar, tz, waves, force):
    for x in range(NX):
        hi, lo = split(polar[4 - c, x])
        force[0, x * NY : (x + 1) * NY, :] = hi
        force[1, x * NY : (x + 1) * NY, :] = lo
    waves[c, 0] = dot3((tz[0, 1], tz[1, 1]), (force[0, :256], force[1, :256]), LAST)
    waves[c, 1] = dot3((tz[0, 1], tz[1, 1]), (force[0, 256:], force[1, 256:]), LAST)


def forward_z(c, xh, polar, faces, tz, base, wire, force, swap):
    cx = (6 - c) * ((c + 1) // 2)
    cy = 5 - c - 3 * lax.rem(c, 2)
    part = c * 2 + xh
    fx, fy = faces
    for i in range(8):
        x = xh * 8 + i
        after = polar[cx, lax.rem(x + 1, NX)]
        before = polar[cx, lax.rem(x + NX - 1, NX)]
        if i == 0:
            before = jnp.where(xh == 0, fx[0, c], before)
        if i == 7:
            after = jnp.where(xh == 1, fx[1, c], after)
        ends = [fy[side, c, pl.ds(pl.multiple_of(xh * 8, 8), 8), :] for side in range(2)]
        grad_y = shift_y(polar[cy, x], ends[0][i : i + 1], ends[1][i : i + 1])
        hi, lo = split((after - before) + grad_y)
        force[0, i * NY : (i + 1) * NY, :] = hi
        force[1, i * NY : (i + 1) * NY, :] = lo
    waves = base[c, xh] + dot3((tz[0, 0], tz[1, 0]), (force[0, :256], force[1, :256]), LAST)
    for p in range(NPY):
        for xg in range(2):
            tiles = [
                waves[p * 32 + kzlo * 8 : p * 32 + kzlo * 8 + 8, xg * 128 : xg * 128 + 128]
                for kzlo in range(4)
            ]
            for x4, tile in enumerate(swap_groups(tiles)):
                row = p * 64 + (xg * 4 + x4) * 8
                swap[row : row + 8, :] = tile
        for s in range(8):
            wire[part, p, s] = swap[pl.ds(p * 64 + s, 8, stride=8), :]


def forward_y(part, got, ty, wire, rows):
    for ri in range(2):
        for kzhi in range(4):
            s = ri * 4 + kzhi
            low = swap_groups([got[part, q, s] for q in range(4)])
            high = swap_groups([got[part, q + 4, s] for q in range(4)])
            for kzlo in range(4):
                row = (kzhi * 4 + kzlo) * 8
                rows[0, row : row + 8, ri * 128 : ri * 128 + 128] = low[kzlo] + high[kzlo]
                rows[1, row : row + 8, ri * 128 : ri * 128 + 128] = low[kzlo] - high[kzlo]
    for e in range(2):
        out = dot3(split(rows[e]), (ty[0, e], ty[1, e]))
        for kz in range(NX):
            wire[part, kz, :, e * 256 : e * 256 + 256] = out[kz * 8 : kz * 8 + 8, :]


def forward_x(c, got, tx, waves, rows):
    for q in range(8):
        a = jnp.concatenate([got[2 * c, q], got[2 * c + 1, q]], axis=0)
        b = jnp.concatenate([got[2 * c, q + 8], got[2 * c + 1, q + 8]], axis=0)
        for ex in range(2):
            hi, lo = split(a + b if ex == 0 else a - b)
            for ri in range(2):
                row = ri * 128 + q * 16
                for e in range(2):
                    lane = e * 256 + ri * 128
                    rows[0, ex, row : row + 16, e * 128 : e * 128 + 128] = hi[:, lane : lane + 128]
                    rows[1, ex, row : row + 16, e * 128 : e * 128 + 128] = lo[:, lane : lane + 128]
    for ex in range(2):
        waves[ex, c] = dot3((tx[0, ex], tx[1, ex]), (rows[0, ex], rows[1, ex]))


def solve(waves, solved, sx, sy, sz, py, px):
    sy = sy[...]
    sz = sz[pl.ds(py * 16 + px, 1), :]
    sz = jnp.concatenate([sz, sz], axis=1)
    coupling = (REF_LAMBDA + REF_SHEAR) / (REF_LAMBDA + 2.0 * REF_SHEAR)
    rest = sy * sy + sz * sz
    for ex in range(2):
        wx = jnp.concatenate([sx[ex], sx[ex]], axis=1)
        squared = wx * wx + rest
        null = squared == 0.0
        inverse = jnp.where(null, 0.0, 1.0 / jnp.where(null, 1.0, squared))
        scale = inverse * (1.0 / REF_SHEAR)
        for ri in range(2):
            parts = [waves[ex, c, ri * 128 : ri * 128 + 128, :] for c in range(3)]
            common = coupling * inverse * (wx * parts[0] + sy * parts[1] + sz * parts[2])
            for c, line in enumerate((wx, sy, sz)):
                hi, lo = split(scale * (parts[c] - common * line))
                solved[0, ex, c, ri * 128 : ri * 128 + 128, :] = hi
                solved[1, ex, c, ri * 128 : ri * 128 + 128, :] = lo


def inverse_x(c, solved, txi, wire):
    backs = [dot3((txi[0, ex], txi[1, ex]), (solved[0, ex, c], solved[1, ex, c])) for ex in range(2)]
    for half, out in enumerate((backs[0] + backs[1], backs[0] - backs[1])):
        for q in range(8):
            for xh in range(2):
                for ri in range(2):
                    row = ri * 128 + q * 16 + xh * 8
                    for e in range(2):
                        lane = e * 256 + ri * 128
                        wire[2 * c + xh, half * 8 + q, :, lane : lane + 128] = out[
                            row : row + 8, e * 128 : e * 128 + 128
                        ]


def inverse_y(part, got, tyi, wire):
    outs = []
    for e in range(2):
        rows = jnp.concatenate([got[part, kz, :, e * 256 : e * 256 + 256] for kz in range(NX)], axis=0)
        outs.append(dot3(split(rows), (tyi[0, e], tyi[1, e])))
    for half, out in enumerate((outs[0] + outs[1], outs[0] - outs[1])):
        for ri in range(2):
            for kzhi in range(4):
                tiles = [
                    out[(kzhi * 4 + k) * 8 : (kzhi * 4 + k + 1) * 8, ri * 128 : ri * 128 + 128]
                    for k in range(4)
                ]
                for q4, tile in enumerate(swap_groups(tiles)):
                    wire[part, half * 4 + q4, ri * 4 + kzhi] = tile


def inverse_z(c, xh, got, tzi, disp, grad, yface, waves, swap):
    part = c * 2 + xh
    for p in range(NPY):
        for s in range(8):
            swap[p * 64 + s * 8 : p * 64 + s * 8 + 8, :] = got[part, p, s]
        for xg in range(2):
            tiles = [swap[pl.ds(p * 64 + xg * 4 + x4, 8, stride=8), :] for x4 in range(4)]
            for kzlo, tile in enumerate(swap_groups(tiles)):
                row = p * 32 + kzlo * 8
                waves[row : row + 8, xg * 128 : xg * 128 + 128] = tile
    turned = split(jnp.transpose(waves[...]))
    out = dot3(turned, (tzi[0, :, :256], tzi[1, :, :256]))
    for i in range(8):
        x = xh * 8 + i
        disp[c, x] = out[i * NY : (i + 1) * NY, :]
        yface[xh, 0, c, i : i + 1] = out[i * NY : i * NY + 1, :]
        yface[xh, 1, c, i : i + 1] = out[i * NY + NY - 1 : i * NY + NY, :]
    out = dot3(turned, (tzi[0, :, 256:], tzi[1, :, 256:]))
    for i in range(8):
        grad[c, xh * 8 + i] = out[i * NY : (i + 1) * NY, :]


def stress_part(first, count, disp, grad, hx, hy, polar, moduli, stress, rows):
    xh = first // 8

    def at_x(x, carry):
        lame, shear = moduli[0, x], moduli[1, x]
        gx, gy, gz = [], [], []
        i = x - xh * 8
        for c in range(3):
            after = hx[1, c] if first == NX - 1 else disp[c, x + 1]
            before = hx[0, c] if first == 0 else disp[c, x - 1]
            gx.append(after - before)
            gy.append(shift_y(disp[c, x], hy[xh, 0, c, pl.ds(i, 1), :], hy[xh, 1, c, pl.ds(i, 1), :]))
            gz.append(grad[c, x])
        trace = (0.5 * lame) * (gx[0] + gy[1] + gz[2])
        half = 0.5 * shear
        parts = (
            shear * gx[0] + trace,
            shear * gy[1] + trace,
            shear * gz[2] + trace,
            half * (gz[1] + gy[2]),
            half * (gz[0] + gx[2]),
            half * (gy[0] + gx[1]),
        )
        row = pl.ds(pl.multiple_of(x * NY, NY), NY)
        for c, part in enumerate(parts):
            total = part + polar[c, x]
            stress[c, x] = total
            hi, lo = split(total)
            rows[0, row, c * 256 : c * 256 + 256] = hi
            rows[1, row, c * 256 : c * 256 + 256] = lo
        return carry

    lax.fori_loop(first, first + count, at_x, 0)


def reply_part(xh, asked, weights, rows, reply):
    column = lax.broadcasted_iota(jnp.int32, (128, 256), 1) + xh * 256
    lane = lax.broadcasted_iota(jnp.int32, (128, 128), 1)
    lane256 = lax.broadcasted_iota(jnp.int32, (128, 256), 1)
    out = reply[...] if xh else jnp.zeros((128, 128), F32)
    wh, wl = weights[0], weights[1]
    for k in range(8):
        tile = asked[:, k : k + 1]
        centre = asked[:, 8 + k : 9 + k]
        pick = (column == tile // 2).astype(F32).astype(BF16)
        here = slice(xh * 256, xh * 256 + 256)
        picked = dot(pick, rows[0, here, :]) + dot(pick, rows[1, here, :])
        at = (lane == centre).astype(F32).astype(BF16)
        row = dot(at, wh) + dot(at, wl)
        weight = jnp.where(lane256 // 128 == tile % 2, jnp.concatenate([row, row], axis=1), 0.0)
        for c in range(6):
            value = jnp.sum(picked[:, c * 256 : c * 256 + 256] * weight, axis=1, keepdims=True)
            out = out + jnp.where(lane == c * 8 + k, value, 0.0)
    reply[...] = out


def force_part(reply, source, slot, burgers, line, out):
    match = lax.broadcasted_iota(jnp.int32, (128, 512), 0) == row_of(source[...])
    match = match.astype(F32).astype(BF16)
    hi, lo = split(reply)
    low = (reply - hi.astype(F32) - lo.astype(F32)).astype(BF16)
    first = ((0,), (0,))
    got = dot(hi, match, first) + (dot(lo, match, first) + dot(low, match, first))
    lane = lax.broadcasted_iota(jnp.int32, (128, 512), 0)
    mine = jnp.where((lane % 8).astype(F32) == slot[...], got, 0.0)
    t = [jnp.sum(mine[c * 8 : c * 8 + 8, :], axis=0, keepdims=True) for c in range(6)]
    b = [burgers[i : i + 1, :] for i in range(3)]
    v = [line[i : i + 1, :] for i in range(3)]
    push_x = t[0] * b[0] + t[5] * b[1] + t[4] * b[2]
    push_y = t[5] * b[0] + t[1] * b[1] + t[3] * b[2]
    push_z = t[4] * b[0] + t[3] * b[1] + t[2] * b[2]
    out[0:1, :] = push_y * v[2] - push_z * v[1]
    out[1:2, :] = push_z * v[0] - push_x * v[2]
    out[2:3, :] = push_x * v[1] - push_y * v[0]


def scratch_plan():
    half = pltpu.VMEM((2, 2, 256, 256), BF16)
    sem = pltpu.SemaphoreType.DMA
    plan = {
        "dist": pltpu.VMEM((9, NX, NY, GRID), F32),
        "ids": pltpu.VMEM((NX, NY, GRID), jnp.int32),
        "load_sem": sem((2, 4)),
        "polar": pltpu.VMEM((6, NX, NY, GRID), F32),
        "moduli": pltpu.VMEM((2, NX, NY, GRID), F32),
        "tz": half,
        "ty": half,
        "tx": half,
        "txi": half,
        "tyi": half,
        "tzi": pltpu.VMEM((2, 256, 512), BF16),
        "table_sem": sem((6,)),
        "ox": pltpu.VMEM((2, 3, NY, GRID), F32),
        "oy": pltpu.VMEM((2, 3, NX, GRID), F32),
        "fx": pltpu.VMEM((2, 3, NY, GRID), F32),
        "fy": pltpu.VMEM((2, 3, NX, GRID), F32),
        "face_sem": sem((2, 4)),
        "hx": pltpu.VMEM((2, 3, NY, GRID), F32),
        "hy": pltpu.VMEM((2, 2, 3, 8, GRID), F32),
        "yface": pltpu.VMEM((2, 2, 3, 8, GRID), F32),
        "back_sem": sem((2, 6)),
        "base": pltpu.VMEM((3, 2, 256, 256), F32),
        "force": pltpu.VMEM((2, 512, 256), BF16),
        "swap": pltpu.VMEM((512, 128), F32),
        "yrows": pltpu.VMEM((2, 128, 256), F32),
        "xrows": half,
        "waves": pltpu.VMEM((2, 3, 256, 256), F32),
        "solved": pltpu.VMEM((2, 2, 3, 256, 256), BF16),
        "lines": pltpu.VMEM((256, 256), F32),
        "disp": pltpu.VMEM((3, NX, NY, GRID), F32),
        "grad": pltpu.VMEM((3, NX, NY, GRID), F32),
        "stress": pltpu.VMEM((6, NX, NY, GRID), F32),
        "store_sem": sem((2,)),
        "rows": pltpu.VMEM((2, 512, 1536), BF16),
        "asked": pltpu.VMEM((128, 128), jnp.int32),
        "slot": pltpu.VMEM((1, 512), F32),
        "reply": pltpu.VMEM((128, 128), F32),
    }
    exchanges = {
        "ex1": ("py", 6, (8, 8, 128), F32),
        "ex2": ("px", 6, (8, 512), F32),
        "ex3": ("px", 6, (8, 512), F32),
        "ex4": ("py", 6, (8, 8, 128), F32),
        "exa": ("py", 1, (NPX, 128), jnp.int32),
        "exb": ("px", 1, (NPY, 128), jnp.int32),
        "exc": ("px", 1, (NPY, 128), F32),
        "exd": ("py", 1, (NPX, 128), F32),
    }
    return plan, exchanges


class Names:
    pass


def whole_body(*refs):
    plan, exchanges = scratch_plan()
    n_in, n_out = 18, 2
    (
        moduli_in, source, tile, centre, burgers, line, sx, sy, sz, weights,
        dist_h, ids_h, tz_h, ty_h, tx_h, txi_h, tyi_h, tzi_h,
    ) = refs[:n_in]
    stress_h, seg_force = refs[n_in : n_in + n_out]
    rest = list(refs[n_in + n_out :])
    r = Names()
    for name in plan:
        setattr(r, name, rest.pop(0))
    for name, (axis, _, _, _) in exchanges.items():
        setattr(r, name, Exchange(axis, rest.pop(0), rest.pop(0), rest.pop(0), rest.pop(0)))

    px, py = lax.axis_index("px"), lax.axis_index("py")
    greet(px, py)
    loads = []
    for g in range(4):
        here = pl.ds(g * 4, 4)
        loads.append(
            (
                pltpu.make_async_copy(dist_h.at[:, here], r.dist.at[:, here], r.load_sem.at[0, g]),
                pltpu.make_async_copy(ids_h.at[here], r.ids.at[here], r.load_sem.at[1, g]),
            )
        )
        for load in loads[-1]:
            load.start()
    pairs = ((tz_h, r.tz), (ty_h, r.ty), (tx_h, r.tx), (txi_h, r.txi), (tyi_h, r.tyi), (tzi_h, r.tzi))
    tables = [pltpu.make_async_copy(a, b, r.table_sem.at[i]) for i, (a, b) in enumerate(pairs)]
    for table in tables:
        table.start()

    slot = request_part(source, tile, centre, r.asked)
    r.slot[...] = slot
    for p in range(NPY):
        r.exa.wire[0, p] = r.asked[p * NPX : p * NPX + NPX, :]
    lookup = table_of(moduli_in)
    for g in range(4):
        for load in loads[g]:
            load.wait()
        polar_part(g * 4, 4, r.dist, r.ids, lookup, r.polar, r.moduli)
    for side in range(2):
        for k, comp in enumerate((0, 5, 4)):
            r.ox[side, k] = r.polar[comp, side * (NX - 1)]
        for k, comp in enumerate((5, 1, 3)):
            r.oy[side, k] = r.polar[comp, :, side * (NY - 1), :]

    left, right = lax.rem(px + NPX - 1, NPX), lax.rem(px + 1, NPX)
    down, up = lax.rem(py + NPY - 1, NPY), lax.rem(py + 1, NPY)
    sides = [(left, py), (right, py), (px, down), (px, up)]

    def face(src, dst, sems, to, k):
        return send(src, dst, (sems.at[0, k], sems.at[1, k]), sides[to])

    halo = [
        face(r.ox.at[0], r.fx.at[1], r.face_sem, 0, 1),
        face(r.ox.at[1], r.fx.at[0], r.face_sem, 1, 0),
        face(r.oy.at[0], r.fy.at[1], r.face_sem, 2, 3),
        face(r.oy.at[1], r.fy.at[0], r.face_sem, 3, 2),
    ]
    pl.semaphore_wait(pltpu.get_barrier_semaphore(), NPX + NPY - 2)
    for copy in halo:
        copy.start()
    r.exa.start(0)
    tables[0].wait()

    def local(c, carry):
        forward_z_local(c, r.polar, r.tz, r.base, r.force)
        return carry

    lax.fori_loop(0, 3, local, 0)
    for copy in halo:
        copy.wait_recv()

    def step_z(j, carry):
        c, xh = j // 2, lax.rem(j, 2)
        forward_z(c, xh, r.polar, (r.fx, r.fy), r.tz, r.base, r.ex1.wire, r.force, r.swap)
        r.ex1.start(j)
        return carry

    lax.fori_loop(0, 6, step_z, 0)
    tables[1].wait()

    def step_y(j, carry):
        r.ex1.arrive(j)
        forward_y(j, r.ex1.got, r.ty, r.ex2.wire, r.yrows)
        r.ex2.start(j)
        return carry

    lax.fori_loop(0, 6, step_y, 0)
    r.exa.arrive(0)
    r.asked[...] = r.exa.got[0].reshape(128, 128)
    for p in range(NPX):
        r.exb.wire[0, p] = r.asked[pl.ds(p, NPY, stride=NPX), :]
    tables[2].wait()

    def step_x(c, carry):
        r.ex2.arrive(2 * c)
        r.ex2.arrive(2 * c + 1)
        forward_x(c, r.ex2.got, r.tx, r.waves, r.xrows)
        return carry

    lax.fori_loop(0, 3, step_x, 0)
    solve(r.waves, r.solved, sx, sy, sz, py, px)
    tables[3].wait()

    def step_xi(c, carry):
        inverse_x(c, r.solved, r.txi, r.ex3.wire)
        r.ex3.start(2 * c)
        return carry

    lax.fori_loop(0, 3, step_xi, 0)
    for c in range(3):
        r.ex3.start(2 * c + 1)
    r.exb.start(0)
    tables[4].wait()

    def step_yi(j, carry):
        part = lax.rem(j, 3) * 2 + j // 3
        r.ex3.arrive(part)
        inverse_y(part, r.ex3.got, r.tyi, r.ex4.wire)
        r.ex4.start(part)
        return carry

    lax.fori_loop(0, 6, step_yi, 0)
    r.exb.arrive(0)
    for p in range(NPX):
        r.asked[p * NPY : p * NPY + NPY, :] = r.exb.got[0, p]
    tables[5].wait()

    def back_half(xh):
        def step_zi(c, carry):
            r.ex4.arrive(c * 2 + xh)
            inverse_z(c, xh, r.ex4.got, r.tzi, r.disp, r.grad, r.yface, r.lines, r.swap)
            return carry

        lax.fori_loop(0, 3, step_zi, 0)
        x_side = NX - 1 if xh else 0
        copies = [
            face(r.disp.at[:, x_side], r.hx.at[1 - xh], r.back_sem, xh, 3 * xh),
            face(r.yface.at[xh, 0], r.hy.at[xh, 1], r.back_sem, 2, 3 * xh + 1),
            face(r.yface.at[xh, 1], r.hy.at[xh, 0], r.back_sem, 3, 3 * xh + 2),
        ]
        for copy in copies:
            copy.start()
        return copies

    def store(xh):
        here = pl.ds(xh * 8, 8)
        return pltpu.make_async_copy(r.stress.at[:, here], stress_h.at[:, here], r.store_sem.at[xh])

    def stress(first, count):
        stress_part(
            first, count, r.disp, r.grad, r.hx, r.hy, r.polar, r.moduli, r.stress, r.rows
        )

    backs = back_half(0)
    for copy in backs[1:]:
        copy.wait_recv()
    stress(1, 6)
    backs += back_half(1)
    stress(7, 1)
    backs[3].wait_recv()
    stress(0, 1)
    store(0).start()
    reply_part(0, r.asked, weights, r.rows, r.reply)
    backs[0].wait_recv()
    for copy in backs[4:]:
        copy.wait_recv()
    stress(8, 7)
    stress(15, 1)
    store(1).start()
    reply_part(1, r.asked, weights, r.rows, r.reply)
    for p in range(NPX):
        r.exc.wire[0, p] = r.reply[p * NPY : p * NPY + NPY, :]
    r.exc.start(0)
    for copy in halo + backs:
        copy.wait_send()
    for part in range(6):
        for ex in (r.ex1, r.ex2, r.ex3, r.ex4):
            ex.finish(part)
    r.exa.finish(0)
    r.exb.finish(0)
    r.exc.arrive(0)
    r.reply[...] = r.exc.got[0].reshape(128, 128)
    for p in range(NPY):
        r.exd.wire[0, p] = r.reply[pl.ds(p, NPX, stride=NPY), :]
    r.exd.start(0)
    store(0).wait()
    store(1).wait()
    r.exd.arrive(0)
    force_part(r.exd.got[0].reshape(128, 128), source, r.slot, burgers, line, seg_force)
    r.exc.finish(0)
    r.exd.finish(0)


def shards(dist, ids, moduli, seg_source, seg_tile, seg_center, burgers, line_vector):
    fwd_z, inv_z = z_tables()
    fwd_h, inv_h = half_tables()
    tz, tzi = two_parts(fwd_z), two_parts(inv_z)
    tx, txi = two_parts(fwd_h), two_parts(inv_h)
    ty = two_parts(fwd_h.transpose(0, 2, 1))
    tyi = two_parts(inv_h.transpose(0, 2, 1))
    sx, sy, sz = wave_lines()
    weights = two_parts(tile_weights())
    plan, exchanges = scratch_plan()
    scratch = list(plan.values())
    for axis, parts, block, dtype in exchanges.values():
        scratch += exchange_scratch(axis, parts, block, dtype)
    hbm = pl.BlockSpec(memory_space=pl.ANY)
    return tuple(
        pl.pallas_call(
            whole_body,
            out_shape=(sds((6, NX, NY, GRID)), sds((3, 512))),
            in_specs=[VM] * 10 + [hbm] * 8,
            out_specs=(hbm, VM),
            scratch_shapes=scratch,
            compiler_params=pltpu.CompilerParams(
                vmem_limit_bytes=VMEM_LIMIT, collective_id=0, has_side_effects=True
            ),
        )(
            moduli,
            seg_source.reshape(1, 512),
            seg_tile.reshape(1, 512),
            seg_center.reshape(1, 512),
            burgers,
            line_vector,
            sx,
            sy,
            sz,
            weights,
            dist,
            ids,
            tz,
            ty,
            tx,
            txi,
            tyi,
            tzi,
        )
    )


def solution(mesh):
    return jax.shard_map(
        shards,
        mesh=mesh,
        in_specs=(
            P(None, "px", "py", None),
            P("px", "py", None),
            P(),
            P(("px", "py"), None),
            P(("px", "py")),
            P(("px", "py")),
            P(None, ("px", "py")),
            P(None, ("px", "py")),
        ),
        out_specs=(P(None, "px", "py", None), P(None, ("px", "py"))),
        check_vma=False,
    )
```

```python
import functools

import jax
import jax.numpy as jnp
import ml_dtypes
import numpy as np
from jax import lax
from jax.experimental import pallas as pl
from jax.experimental.pallas import tpu as pltpu
from jax.sharding import PartitionSpec as P

F32 = jnp.float32
BF16 = jnp.bfloat16
REF_LAMBDA = 1.25
REF_SHEAR = 1.25
GRID = 256
HALF = 128
NPX = 16
NPY = 8
DEVICES = NPX * NPY
NX = 16
NY = 32
VMEM_LIMIT = 60 * 1024 * 1024
VM = pl.BlockSpec(memory_space=pltpu.VMEM)


def two_parts(table):
    table = np.asarray(table, np.float32)
    high = table.astype(ml_dtypes.bfloat16)
    low = (table - high.astype(np.float32)).astype(ml_dtypes.bfloat16)
    return np.stack([high, low])


def z_tables():
    z = np.arange(GRID)
    fwd = np.zeros((GRID, GRID))
    inv = np.zeros((GRID, GRID))
    for row in range(GRID):
        wave, ri = row // 2, row % 2
        angle = 2 * np.pi * ((wave * z) % GRID) / GRID
        if wave == 0:
            line = np.ones(GRID) if ri == 0 else 1.0 - 2.0 * (z % 2)
            fwd[row], inv[row] = line, line / GRID
        else:
            line = np.cos(angle) if ri == 0 else -np.sin(angle)
            fwd[row], inv[row] = line, 2 * line / GRID
    step = np.roll(np.eye(GRID), 1, 1) - np.roll(np.eye(GRID), -1, 1)
    fwd = 0.5 * np.stack([fwd, fwd @ step])
    inv = np.concatenate([inv, inv @ step.T], axis=1)
    return fwd, inv


def half_tables():
    k = np.arange(HALF)
    fwd, inv = [], []
    for e in range(2):
        angle = 2 * np.pi * (((2 * k[:, None] + e) * k[None, :]) % GRID) / GRID
        cos, sin = np.cos(angle), np.sin(angle)
        fwd.append(np.block([[cos, sin], [-sin, cos]]))
        inv.append(np.block([[cos.T, -sin.T], [sin.T, cos.T]]) / GRID)
    return np.stack(fwd), np.stack(inv)


def x_order():
    index = np.arange(HALF).reshape(8, 4, 4)
    order = index.transpose(1, 0, 2).reshape(-1)
    return np.concatenate([order, order + HALF])


def sines():
    wave = np.arange(GRID)
    line = np.sin(2 * np.pi * wave / GRID)
    line[wave % HALF == 0] = 0.0
    return line


def wave_lines():
    line = sines()
    sx = np.stack([line[0::2], line[1::2]])[:, :, None] * np.ones((1, 1, 128))
    sy = np.concatenate([line[0::2], line[1::2]])[None, :]
    sz = line[:128, None] * np.ones((1, 128))
    return sx.astype(np.float32), sy.astype(np.float32), sz.astype(np.float32)


def tile_weights():
    v = np.arange(128, dtype=np.float64)
    weights = np.exp(-((v[None, :] - v[:, None]) ** 2) / (2.0 * 16.0**2))
    return weights / weights.sum(axis=1, keepdims=True)


def split(values):
    high = values.astype(BF16)
    low = (values - high.astype(F32)).astype(BF16)
    return high, low


def dot(a, b, dims=((1,), (0,))):
    return lax.dot_general(a, b, (dims, ((), ())), preferred_element_type=F32)


def dot3(a, b, dims=((1,), (0,))):
    (ah, al), (bh, bl) = a, b
    return dot(ah, bh, dims) + (dot(ah, bl, dims) + dot(al, bh, dims))


def swap_groups(values):
    count = len(values)
    width = 128 // count
    lane = lax.broadcasted_iota(jnp.int32, values[0].shape, values[0].ndim - 1)
    axis = values[0].ndim - 1
    values = list(values)
    step = 1
    while step < count:
        first = ((lane // (width * step)) % 2) == 0
        out = list(values)
        for i in range(count):
            if i & step == 0:
                low, high = values[i], values[i + step]
                out[i] = jnp.where(first, low, pltpu.roll(high, width * step, axis))
                out[i + step] = jnp.where(first, pltpu.roll(low, 128 - width * step, axis), high)
        values = out
        step *= 2
    return values


def send(src, dst, sems, where):
    return pltpu.make_async_remote_copy(
        src_ref=src,
        dst_ref=dst,
        send_sem=sems[0],
        recv_sem=sems[1],
        device_id=where,
        device_id_type=pl.DeviceIdType.MESH,
    )


def peers(px, py):
    me = px * NPY + py
    return [lax.rem(me + (53 * k) % DEVICES, DEVICES) for k in range(1, DEVICES)]


def place(device):
    return (device // NPY, lax.rem(device, NPY))


def greet(px, py):
    barrier = pltpu.get_barrier_semaphore()
    for peer in peers(px, py):
        pl.semaphore_signal(
            barrier, inc=1, device_id=place(peer), device_id_type=pl.DeviceIdType.MESH
        )


class Turn:
    def __init__(self, wire, got, sems, own_sem):
        self.wire, self.got, self.sems, self.own_sem = wire, got, sems, own_sem
        self.px, self.py = lax.axis_index("px"), lax.axis_index("py")
        self.me = self.px * NPY + self.py

    def rows(self, ref, part, device):
        return ref.at[part, pl.ds(pl.multiple_of(device * 8, 8), 8)]

    def own(self, part):
        return pltpu.make_async_copy(
            self.rows(self.wire, part, self.me), self.rows(self.got, part, self.me), self.own_sem.at[part]
        )

    def start(self, part):
        sems = (self.sems.at[0, part], self.sems.at[1, part])
        for peer in peers(self.px, self.py):
            send(
                self.rows(self.wire, part, peer), self.rows(self.got, part, self.me), sems, place(peer)
            ).start()
        self.own(part).start()

    def all(self, side, part):
        block = self.got.at[part, pl.ds(0, 8 * DEVICES - 8)]
        return pltpu.make_async_copy(block, block, self.sems.at[side, part])

    def arrive(self, part):
        self.own(part).wait()
        self.all(1, part).wait()

    def finish(self, part):
        self.all(0, part).wait()


def turn_scratch():
    return [
        pltpu.VMEM((3, 8 * DEVICES, 128), F32),
        pltpu.VMEM((3, 8 * DEVICES, 128), F32),
        pltpu.SemaphoreType.DMA((2, 3)),
        pltpu.SemaphoreType.DMA((3,)),
    ]


class Exchange:
    def __init__(self, axis, wire, got, sems, own_sem):
        self.count = NPX if axis == "px" else NPY
        self.axis, self.wire, self.got, self.sems, self.own_sem = axis, wire, got, sems, own_sem
        self.px, self.py = lax.axis_index("px"), lax.axis_index("py")
        self.me = self.px if axis == "px" else self.py

    def own(self, part):
        return pltpu.make_async_copy(
            self.wire.at[part, self.me], self.got.at[part, self.me], self.own_sem.at[part]
        )

    def start(self, part):
        for d in range(1, self.count):
            peer = lax.rem(self.me + d, self.count)
            where = (peer, self.py) if self.axis == "px" else (self.px, peer)
            sems = (self.sems.at[0, part], self.sems.at[1, part])
            send(self.wire.at[part, peer], self.got.at[part, self.me], sems, where).start()
        self.own(part).start()

    def all(self, side, part):
        block = self.got.at[part, pl.ds(0, self.count - 1)]
        return pltpu.make_async_copy(block, block, self.sems.at[side, part])

    def arrive(self, part):
        self.own(part).wait()
        self.all(1, part).wait()

    def finish(self, part):
        self.all(0, part).wait()


def exchange_scratch(axis, parts, block, dtype=F32):
    count = NPX if axis == "px" else NPY
    return [
        pltpu.VMEM((parts, count) + block, dtype),
        pltpu.VMEM((parts, count) + block, dtype),
        pltpu.SemaphoreType.DMA((2, parts)),
        pltpu.SemaphoreType.DMA((parts,)),
    ]


def sds(shape, dtype=F32):
    return jax.ShapeDtypeStruct(shape, dtype)


def moduli_of(table, ids):
    lame, shear = [], []
    for half in range(2):
        index = ids[:, half * 128 : (half + 1) * 128]
        lame.append(jnp.take_along_axis(table, index, axis=1))
        shear.append(jnp.take_along_axis(table, index + 64, axis=1))
    return jnp.concatenate(lame, axis=1), jnp.concatenate(shear, axis=1)


def table_of(moduli_ref):
    row = jnp.concatenate([moduli_ref[0:1, :], moduli_ref[1:2, :]], axis=1)
    return jnp.broadcast_to(row, (NY, 128))


def polar_part(first, count, dist, ids, table, polar, moduli):
    def at_x(x, carry):
        lame, shear = moduli_of(table, ids[x])
        moduli[0, x] = lame
        moduli[1, x] = shear
        exx, eyy, ezz = dist[0, x], dist[4, x], dist[8, x]
        trace = lame * (exx + eyy + ezz)
        twice = shear + shear
        polar[0, x] = -(twice * exx + trace)
        polar[1, x] = -(twice * eyy + trace)
        polar[2, x] = -(twice * ezz + trace)
        polar[3, x] = -(shear * (dist[5, x] + dist[7, x]))
        polar[4, x] = -(shear * (dist[2, x] + dist[6, x]))
        polar[5, x] = -(shear * (dist[1, x] + dist[3, x]))
        return carry

    lax.fori_loop(first, first + count, at_x, 0)


def row_of(device):
    return (device % NPY) * NPX + device // NPY


def request_part(source, tile, centre, asked):
    src_lane = row_of(source[...]).astype(F32)
    src = jnp.transpose(jnp.broadcast_to(src_lane, (128, 512)))
    same = src[:, 0:1] == src_lane
    first = lax.broadcasted_iota(jnp.int32, (512, 512), 0)
    second = lax.broadcasted_iota(jnp.int32, (512, 512), 1)
    slot_lane = jnp.sum(jnp.where(same & (first < second), 1.0, 0.0), axis=0, keepdims=True)
    match = (src == lax.broadcasted_iota(jnp.int32, (512, 128), 1).astype(F32)).astype(F32).astype(BF16)
    row = lax.broadcasted_iota(jnp.int32, (8, 512), 0).astype(F32)
    here = row == slot_lane
    tile_v = tile[...]
    values = [tile_v // 8, tile_v % 8, centre[...]]
    rows = [jnp.where(here, v.astype(F32), 0.0) for v in values]
    stacked = jnp.concatenate(rows + [jnp.zeros((8, 512), F32)], axis=0).astype(BF16)
    got = dot(stacked, match)
    both = jnp.concatenate([got[0:8] * 8.0 + got[8:16], got[16:24], jnp.zeros((112, 128), F32)], axis=0)
    asked[...] = jnp.transpose(both).astype(jnp.int32)
    return slot_lane


def shift_y(values, before, after):
    row = lax.broadcasted_iota(jnp.int32, values.shape, 0)
    up = jnp.where(row == NY - 1, after, pltpu.roll(values, NY - 1, 0))
    down = jnp.where(row == 0, before, pltpu.roll(values, 1, 0))
    return up - down


LAST = ((1,), (1,))


def forward_z_local(c, polar, tz, waves, force):
    for x in range(NX):
        hi, lo = split(polar[4 - c, x])
        force[0, x * NY : (x + 1) * NY, :] = hi
        force[1, x * NY : (x + 1) * NY, :] = lo
    waves[c] = dot3((tz[0, 1], tz[1, 1]), (force[0], force[1]), LAST)


def forward_z(c, polar, faces, tz, base, wire, force):
    cx = (6 - c) * ((c + 1) // 2)
    cy = 5 - c - 3 * lax.rem(c, 2)
    fx, fy = faces
    for x in range(NX):
        after = fx[1, c] if x == NX - 1 else polar[cx, x + 1]
        before = fx[0, c] if x == 0 else polar[cx, x - 1]
        grad_y = shift_y(polar[cy, x], fy[0, c, x : x + 1, :], fy[1, c, x : x + 1, :])
        hi, lo = split((after - before) + grad_y)
        force[0, x * NY : (x + 1) * NY, :] = hi
        force[1, x * NY : (x + 1) * NY, :] = lo
    waves = base[c] + dot3((tz[0, 0], tz[1, 0]), (force[0], force[1]), LAST)
    for t in range(32):
        for xg in range(4):
            wire[c, pl.ds(32 * t + xg, 8, stride=4), :] = waves[
                8 * t : 8 * t + 8, xg * 128 : xg * 128 + 128
            ]


def forward_plane(c, got, ty, tx, waves, yrows, xrows):
    for q in range(NPX):
        row = q * 64
        low = swap_groups([got[c, row + p * 8 : row + p * 8 + 8, :] for p in range(4)])
        high = swap_groups([got[c, row + p * 8 : row + p * 8 + 8, :] for p in range(4, 8)])
        for x4 in range(4):
            to = pl.ds(q * 4 + x4, 8, stride=64)
            yrows[0, to, :] = low[x4] + high[x4]
            yrows[1, to, :] = low[x4] - high[x4]
    for e in range(2):
        rows = jnp.concatenate([yrows[e, :256, :], yrows[e, 256:, :]], axis=1)
        out = dot3(split(rows), (ty[0, e], ty[1, e]))
        for xg in range(4):
            a, b = out[xg * 64 : xg * 64 + 32, :], out[xg * 64 + 32 : xg * 64 + 64, :]
            for ex in range(2):
                hi, lo = split(a + b if ex == 0 else a - b)
                for ri in range(2):
                    to = slice(ri * 128 + xg * 32, ri * 128 + xg * 32 + 32)
                    xrows[0, ex, to, e * 128 : e * 128 + 128] = hi[:, ri * 128 : ri * 128 + 128]
                    xrows[1, ex, to, e * 128 : e * 128 + 128] = lo[:, ri * 128 : ri * 128 + 128]
    for ex in range(2):
        waves[ex, c] = dot3((tx[0, ex], tx[1, ex]), (xrows[0, ex], xrows[1, ex]))


def solve(waves, solved, sx, sy, sz, kz):
    sy = sy[...]
    sz = sz[pl.ds(kz, 1), :]
    sz = jnp.concatenate([sz, sz], axis=1)
    coupling = (REF_LAMBDA + REF_SHEAR) / (REF_LAMBDA + 2.0 * REF_SHEAR)
    rest = sy * sy + sz * sz
    for ex in range(2):
        wx = jnp.concatenate([sx[ex], sx[ex]], axis=1)
        squared = wx * wx + rest
        null = squared == 0.0
        inverse = jnp.where(null, 0.0, 1.0 / jnp.where(null, 1.0, squared))
        scale = inverse * (1.0 / REF_SHEAR)
        for ri in range(2):
            parts = [waves[ex, c, ri * 128 : ri * 128 + 128, :] for c in range(3)]
            common = coupling * inverse * (wx * parts[0] + sy * parts[1] + sz * parts[2])
            for c, line in enumerate((wx, sy, sz)):
                hi, lo = split(scale * (parts[c] - common * line))
                solved[0, ex, c, ri * 128 : ri * 128 + 128, :] = hi
                solved[1, ex, c, ri * 128 : ri * 128 + 128, :] = lo


def inverse_plane(c, solved, txi, tyi, wire, yrows):
    backs = [dot3((txi[0, ex], txi[1, ex]), (solved[0, ex, c], solved[1, ex, c])) for ex in range(2)]
    halves = (backs[0] + backs[1], backs[0] - backs[1])
    outs = []
    for e in range(2):
        lane = slice(e * 128, e * 128 + 128)
        sides = []
        for ri in range(2):
            blocks = []
            for xg in range(4):
                row = ri * 128 + xg * 32
                blocks += [halves[0][row : row + 32, lane], halves[1][row : row + 32, lane]]
            sides.append(jnp.concatenate(blocks, axis=0))
        outs.append(dot3(split(jnp.concatenate(sides, axis=1)), (tyi[0, e], tyi[1, e])))
    for half, out in enumerate((outs[0] + outs[1], outs[0] - outs[1])):
        yrows[half, :256, :] = out[:, :128]
        yrows[half, 256:, :] = out[:, 128:]
    for q in range(NPX):
        for half in range(2):
            tiles = [yrows[half, pl.ds(q * 4 + x4, 8, stride=64), :] for x4 in range(4)]
            for p, tile in enumerate(swap_groups(tiles)):
                row = q * 64 + half * 32 + p * 8
                wire[c, row : row + 8, :] = tile


def inverse_z(c, got, tzi, disp, grad, yface, lines):
    for xg in range(4):
        turned = jnp.transpose(got[c, pl.ds(xg, 256, stride=4), :])
        hi, lo = split(turned)
        lines[0, xg * 128 : xg * 128 + 128, :] = hi
        lines[1, xg * 128 : xg * 128 + 128, :] = lo
    pair = (lines[0], lines[1])
    out = dot3(pair, (tzi[0, :, :256], tzi[1, :, :256]))
    for x in range(NX):
        disp[c, x] = out[x * NY : (x + 1) * NY, :]
        yface[0, c, x : x + 1] = out[x * NY : x * NY + 1, :]
        yface[1, c, x : x + 1] = out[x * NY + NY - 1 : x * NY + NY, :]
    out = dot3(pair, (tzi[0, :, 256:], tzi[1, :, 256:]))
    for x in range(NX):
        grad[c, x] = out[x * NY : (x + 1) * NY, :]


def stress_part(first, count, disp, grad, hx, hy, polar, moduli, stress, rows):
    def at_x(x, carry):
        lame, shear = moduli[0, x], moduli[1, x]
        gx, gy, gz = [], [], []
        for c in range(3):
            after = hx[1, c] if first == NX - 1 else disp[c, x + 1]
            before = hx[0, c] if first == 0 else disp[c, x - 1]
            gx.append(after - before)
            gy.append(shift_y(disp[c, x], hy[0, c, pl.ds(x, 1), :], hy[1, c, pl.ds(x, 1), :]))
            gz.append(grad[c, x])
        trace = (0.5 * lame) * (gx[0] + gy[1] + gz[2])
        half = 0.5 * shear
        parts = (
            shear * gx[0] + trace,
            shear * gy[1] + trace,
            shear * gz[2] + trace,
            half * (gz[1] + gy[2]),
            half * (gz[0] + gx[2]),
            half * (gy[0] + gx[1]),
        )
        row = pl.ds(pl.multiple_of(x * NY, NY), NY)
        for c, part in enumerate(parts):
            total = part + polar[c, x]
            stress[c, x] = total
            hi, lo = split(total)
            rows[0, row, c * 256 : c * 256 + 256] = hi
            rows[1, row, c * 256 : c * 256 + 256] = lo
        return carry

    lax.fori_loop(first, first + count, at_x, 0)


def reply_part(asked, weights, rows, reply):
    column = lax.broadcasted_iota(jnp.int32, (128, 512), 1)
    lane = lax.broadcasted_iota(jnp.int32, (128, 128), 1)
    lane256 = lax.broadcasted_iota(jnp.int32, (128, 256), 1)
    out = jnp.zeros((128, 128), F32)
    wh, wl = weights[0], weights[1]
    for k in range(8):
        tile = asked[:, k : k + 1]
        centre = asked[:, 8 + k : 9 + k]
        pick = (column == tile // 2).astype(F32).astype(BF16)
        picked = dot(pick, rows[0]) + dot(pick, rows[1])
        at = (lane == centre).astype(F32).astype(BF16)
        row = dot(at, wh) + dot(at, wl)
        weight = jnp.where(lane256 // 128 == tile % 2, jnp.concatenate([row, row], axis=1), 0.0)
        for c in range(6):
            value = jnp.sum(picked[:, c * 256 : c * 256 + 256] * weight, axis=1, keepdims=True)
            out = jnp.where(lane == c * 8 + k, value, out)
    reply[...] = out


def force_part(reply, source, slot, burgers, line, out):
    match = lax.broadcasted_iota(jnp.int32, (128, 512), 0) == row_of(source[...])
    match = match.astype(F32).astype(BF16)
    hi, lo = split(reply)
    low = (reply - hi.astype(F32) - lo.astype(F32)).astype(BF16)
    first = ((0,), (0,))
    got = dot(hi, match, first) + (dot(lo, match, first) + dot(low, match, first))
    lane = lax.broadcasted_iota(jnp.int32, (128, 512), 0)
    mine = jnp.where((lane % 8).astype(F32) == slot[...], got, 0.0)
    t = [jnp.sum(mine[c * 8 : c * 8 + 8, :], axis=0, keepdims=True) for c in range(6)]
    b = [burgers[i : i + 1, :] for i in range(3)]
    v = [line[i : i + 1, :] for i in range(3)]
    push_x = t[0] * b[0] + t[5] * b[1] + t[4] * b[2]
    push_y = t[5] * b[0] + t[1] * b[1] + t[3] * b[2]
    push_z = t[4] * b[0] + t[3] * b[1] + t[2] * b[2]
    out[0:1, :] = push_y * v[2] - push_z * v[1]
    out[1:2, :] = push_z * v[0] - push_x * v[2]
    out[2:3, :] = push_x * v[1] - push_y * v[0]


def scratch_plan():
    half = pltpu.VMEM((2, 2, 256, 256), BF16)
    sem = pltpu.SemaphoreType.DMA
    plan = {
        "dist": pltpu.VMEM((9, NX, NY, GRID), F32),
        "ids": pltpu.VMEM((NX, NY, GRID), jnp.int32),
        "load_sem": sem((2, 4)),
        "polar": pltpu.VMEM((6, NX, NY, GRID), F32),
        "moduli": pltpu.VMEM((2, NX, NY, GRID), F32),
        "tz": half,
        "ty": half,
        "tx": half,
        "txi": half,
        "tyi": half,
        "tzi": pltpu.VMEM((2, 256, 512), BF16),
        "table_sem": sem((6,)),
        "ox": pltpu.VMEM((2, 3, NY, GRID), F32),
        "oy": pltpu.VMEM((2, 3, NX, GRID), F32),
        "fx": pltpu.VMEM((2, 3, NY, GRID), F32),
        "fy": pltpu.VMEM((2, 3, NX, GRID), F32),
        "face_sem": sem((2, 4)),
        "hx": pltpu.VMEM((2, 3, NY, GRID), F32),
        "hy": pltpu.VMEM((2, 3, NX, GRID), F32),
        "yface": pltpu.VMEM((2, 3, NX, GRID), F32),
        "back_sem": sem((3, 2, 4)),
        "base": pltpu.VMEM((3, 256, 512), F32),
        "force": pltpu.VMEM((2, 512, 256), BF16),
        "yrows": pltpu.VMEM((2, 512, 128), F32),
        "xrows": half,
        "waves": pltpu.VMEM((2, 3, 256, 256), F32),
        "solved": pltpu.VMEM((2, 2, 3, 256, 256), BF16),
        "lines": pltpu.VMEM((2, 512, 256), BF16),
        "disp": pltpu.VMEM((3, NX, NY, GRID), F32),
        "grad": pltpu.VMEM((3, NX, NY, GRID), F32),
        "stress": pltpu.VMEM((6, NX, NY, GRID), F32),
        "store_sem": sem((1,)),
        "rows": pltpu.VMEM((2, 512, 1536), BF16),
        "asked": pltpu.VMEM((128, 128), jnp.int32),
        "slot": pltpu.VMEM((1, 512), F32),
        "reply": pltpu.VMEM((128, 128), F32),
    }
    exchanges = {
        "exa": ("py", 1, (NPX, 128), jnp.int32),
        "exb": ("px", 1, (NPY, 128), jnp.int32),
        "exc": ("px", 1, (NPY, 128), F32),
        "exd": ("py", 1, (NPX, 128), F32),
    }
    return plan, exchanges


class Names:
    pass


def whole_body(*refs):
    plan, exchanges = scratch_plan()
    n_in, n_out = 18, 2
    (
        moduli_in, source, tile, centre, burgers, line, sx, sy, sz, weights,
        dist_h, ids_h, tz_h, ty_h, tx_h, txi_h, tyi_h, tzi_h,
    ) = refs[:n_in]
    stress_h, seg_force = refs[n_in : n_in + n_out]
    rest = list(refs[n_in + n_out :])
    r = Names()
    for name in plan:
        setattr(r, name, rest.pop(0))
    for name, (axis, _, _, _) in exchanges.items():
        setattr(r, name, Exchange(axis, rest.pop(0), rest.pop(0), rest.pop(0), rest.pop(0)))

    r.there = Turn(rest.pop(0), rest.pop(0), rest.pop(0), rest.pop(0))
    r.back = Turn(rest.pop(0), rest.pop(0), rest.pop(0), rest.pop(0))

    px, py = lax.axis_index("px"), lax.axis_index("py")
    greet(px, py)
    loads = []
    for g in range(4):
        here = pl.ds(g * 4, 4)
        loads.append(
            (
                pltpu.make_async_copy(dist_h.at[:, here], r.dist.at[:, here], r.load_sem.at[0, g]),
                pltpu.make_async_copy(ids_h.at[here], r.ids.at[here], r.load_sem.at[1, g]),
            )
        )
        for load in loads[-1]:
            load.start()
    pairs = ((tz_h, r.tz), (ty_h, r.ty), (tx_h, r.tx), (txi_h, r.txi), (tyi_h, r.tyi), (tzi_h, r.tzi))
    tables = [pltpu.make_async_copy(a, b, r.table_sem.at[i]) for i, (a, b) in enumerate(pairs)]
    for table in tables:
        table.start()

    slot = request_part(source, tile, centre, r.asked)
    r.slot[...] = slot
    for p in range(NPY):
        r.exa.wire[0, p] = r.asked[p * NPX : p * NPX + NPX, :]
    lookup = table_of(moduli_in)
    for g in range(4):
        for load in loads[g]:
            load.wait()
        polar_part(g * 4, 4, r.dist, r.ids, lookup, r.polar, r.moduli)
    for side in range(2):
        for k, comp in enumerate((0, 5, 4)):
            r.ox[side, k] = r.polar[comp, side * (NX - 1)]
        for k, comp in enumerate((5, 1, 3)):
            r.oy[side, k] = r.polar[comp, :, side * (NY - 1), :]

    left, right = lax.rem(px + NPX - 1, NPX), lax.rem(px + 1, NPX)
    down, up = lax.rem(py + NPY - 1, NPY), lax.rem(py + 1, NPY)
    sides = [(left, py), (right, py), (px, down), (px, up)]

    def face(src, dst, sems, to, k):
        return send(src, dst, (sems.at[0, k], sems.at[1, k]), sides[to])

    halo = [
        face(r.ox.at[0], r.fx.at[1], r.face_sem, 0, 1),
        face(r.ox.at[1], r.fx.at[0], r.face_sem, 1, 0),
        face(r.oy.at[0], r.fy.at[1], r.face_sem, 2, 3),
        face(r.oy.at[1], r.fy.at[0], r.face_sem, 3, 2),
    ]
    pl.semaphore_wait(pltpu.get_barrier_semaphore(), DEVICES - 1)
    for copy in halo:
        copy.start()
    r.exa.start(0)
    tables[0].wait()

    def local(c, carry):
        forward_z_local(c, r.polar, r.tz, r.base, r.force)
        return carry

    lax.fori_loop(0, 3, local, 0)
    for copy in halo:
        copy.wait_recv()

    for c in range(3):
        forward_z(c, r.polar, (r.fx, r.fy), r.tz, r.base, r.there.wire, r.force)
        r.there.start(c)
    r.exa.arrive(0)
    r.asked[...] = r.exa.got[0].reshape(128, 128)
    for p in range(NPX):
        r.exb.wire[0, p] = r.asked[pl.ds(p, NPY, stride=NPX), :]
    tables[1].wait()
    tables[2].wait()

    def step_plane(c, carry):
        r.there.arrive(c)
        forward_plane(c, r.there.got, r.ty, r.tx, r.waves, r.yrows, r.xrows)
        return carry

    lax.fori_loop(0, 3, step_plane, 0)
    solve(r.waves, r.solved, sx, sy, sz, px * NPY + py)
    tables[3].wait()
    tables[4].wait()

    def step_back(c, carry):
        inverse_plane(c, r.solved, r.txi, r.tyi, r.back.wire, r.yrows)
        r.back.start(c)
        return carry

    lax.fori_loop(0, 3, step_back, 0)
    r.exb.start(0)
    tables[5].wait()
    r.exb.arrive(0)
    for p in range(NPX):
        r.asked[p * NPY : p * NPY + NPY, :] = r.exb.got[0, p]

    def faces_back(c):
        sems = r.back_sem.at[c]
        return [
            face(r.disp.at[c, 0], r.hx.at[1, c], sems, 0, 1),
            face(r.disp.at[c, NX - 1], r.hx.at[0, c], sems, 1, 0),
            face(r.yface.at[0, c], r.hy.at[1, c], sems, 2, 3),
            face(r.yface.at[1, c], r.hy.at[0, c], sems, 3, 2),
        ]

    backs = []
    for c in range(3):
        r.back.arrive(c)
        inverse_z(c, r.back.got, r.tzi, r.disp, r.grad, r.yface, r.lines)
        backs += faces_back(c)
        for copy in backs[4 * c :]:
            copy.start()

    for copy in backs:
        copy.wait_recv()
    for first, count in ((0, 1), (1, 14), (15, 1)):
        stress_part(
            first, count, r.disp, r.grad, r.hx, r.hy, r.polar, r.moduli, r.stress, r.rows
        )
    store = pltpu.make_async_copy(r.stress, stress_h, r.store_sem.at[0])
    store.start()
    reply_part(r.asked, weights, r.rows, r.reply)
    for p in range(NPX):
        r.exc.wire[0, p] = r.reply[p * NPY : p * NPY + NPY, :]
    r.exc.start(0)
    for copy in halo + backs:
        copy.wait_send()
    for c in range(3):
        r.there.finish(c)
        r.back.finish(c)
    r.exa.finish(0)
    r.exb.finish(0)
    r.exc.arrive(0)
    r.reply[...] = r.exc.got[0].reshape(128, 128)
    for p in range(NPY):
        r.exd.wire[0, p] = r.reply[pl.ds(p, NPX, stride=NPY), :]
    r.exd.start(0)
    store.wait()
    r.exd.arrive(0)
    force_part(r.exd.got[0].reshape(128, 128), source, r.slot, burgers, line, seg_force)
    r.exc.finish(0)
    r.exd.finish(0)


def shards(dist, ids, moduli, seg_source, seg_tile, seg_center, burgers, line_vector):
    fwd_z, inv_z = z_tables()
    fwd_h, inv_h = half_tables()
    order = x_order()
    tz, tzi = two_parts(fwd_z), two_parts(inv_z)
    tx, txi = two_parts(fwd_h[:, :, order]), two_parts(inv_h[:, order, :])
    ty = two_parts(fwd_h.transpose(0, 2, 1))
    tyi = two_parts(inv_h.transpose(0, 2, 1))
    sx, sy, sz = wave_lines()
    weights = two_parts(tile_weights())
    plan, exchanges = scratch_plan()
    scratch = list(plan.values())
    for axis, parts, block, dtype in exchanges.values():
        scratch += exchange_scratch(axis, parts, block, dtype)
    scratch += turn_scratch() + turn_scratch()
    hbm = pl.BlockSpec(memory_space=pl.ANY)
    return tuple(
        pl.pallas_call(
            whole_body,
            out_shape=(sds((6, NX, NY, GRID)), sds((3, 512))),
            in_specs=[VM] * 10 + [hbm] * 8,
            out_specs=(hbm, VM),
            scratch_shapes=scratch,
            compiler_params=pltpu.CompilerParams(
                vmem_limit_bytes=VMEM_LIMIT, collective_id=0, has_side_effects=True
            ),
        )(
            moduli,
            seg_source.reshape(1, 512),
            seg_tile.reshape(1, 512),
            seg_center.reshape(1, 512),
            burgers,
            line_vector,
            sx,
            sy,
            sz,
            weights,
            dist,
            ids,
            tz,
            ty,
            tx,
            txi,
            tyi,
            tzi,
        )
    )


def solution(mesh):
    return jax.shard_map(
        shards,
        mesh=mesh,
        in_specs=(
            P(None, "px", "py", None),
            P("px", "py", None),
            P(),
            P(("px", "py"), None),
            P(("px", "py")),
            P(("px", "py")),
            P(None, ("px", "py")),
            P(None, ("px", "py")),
        ),
        out_specs=(P(None, "px", "py", None), P(None, ("px", "py"))),
        check_vma=False,
    )
```

```python
import functools

import jax
import jax.numpy as jnp
import ml_dtypes
import numpy as np
from jax import lax
from jax.experimental import pallas as pl
from jax.experimental.pallas import tpu as pltpu
from jax.sharding import PartitionSpec as P

F32 = jnp.float32
BF16 = jnp.bfloat16
REF_LAMBDA = 1.25
REF_SHEAR = 1.25
GRID = 256
HALF = 128
NPX = 16
NPY = 8
DEVICES = NPX * NPY
NX = 16
NY = 32
VMEM_LIMIT = 60 * 1024 * 1024
VM = pl.BlockSpec(memory_space=pltpu.VMEM)


def two_parts(table):
    table = np.asarray(table, np.float32)
    high = table.astype(ml_dtypes.bfloat16)
    low = (table - high.astype(np.float32)).astype(ml_dtypes.bfloat16)
    return np.stack([high, low])


def z_tables():
    z = np.arange(GRID)
    fwd = np.zeros((GRID, GRID))
    inv = np.zeros((GRID, GRID))
    for row in range(GRID):
        wave, ri = row // 2, row % 2
        angle = 2 * np.pi * ((wave * z) % GRID) / GRID
        if wave == 0:
            line = np.ones(GRID) if ri == 0 else 1.0 - 2.0 * (z % 2)
            fwd[row], inv[row] = line, line / GRID
        else:
            line = np.cos(angle) if ri == 0 else -np.sin(angle)
            fwd[row], inv[row] = line, 2 * line / GRID
    step = np.roll(np.eye(GRID), 1, 1) - np.roll(np.eye(GRID), -1, 1)
    fwd = 0.5 * np.stack([fwd, fwd @ step])
    inv = np.concatenate([inv, inv @ step.T], axis=1)
    return fwd, inv


def half_tables():
    k = np.arange(HALF)
    fwd, inv = [], []
    for e in range(2):
        angle = 2 * np.pi * (((2 * k[:, None] + e) * k[None, :]) % GRID) / GRID
        cos, sin = np.cos(angle), np.sin(angle)
        fwd.append(np.block([[cos, sin], [-sin, cos]]))
        inv.append(np.block([[cos.T, -sin.T], [sin.T, cos.T]]) / GRID)
    return np.stack(fwd), np.stack(inv)


def x_order():
    index = np.arange(HALF).reshape(8, 4, 4)
    order = index.transpose(1, 0, 2).reshape(-1)
    return np.concatenate([order, order + HALF])


def sines():
    wave = np.arange(GRID)
    line = np.sin(2 * np.pi * wave / GRID)
    line[wave % HALF == 0] = 0.0
    return line


def wave_lines():
    line = sines()
    sx = np.stack([line[0::2], line[1::2]])[:, :, None] * np.ones((1, 1, 128))
    sy = np.concatenate([line[0::2], line[1::2]])[None, :]
    sz = line[:128, None] * np.ones((1, 128))
    return sx.astype(np.float32), sy.astype(np.float32), sz.astype(np.float32)


def tile_weights():
    v = np.arange(128, dtype=np.float64)
    weights = np.exp(-((v[None, :] - v[:, None]) ** 2) / (2.0 * 16.0**2))
    return weights / weights.sum(axis=1, keepdims=True)


def split(values):
    high = values.astype(BF16)
    low = (values - high.astype(F32)).astype(BF16)
    return high, low


def dot(a, b, dims=((1,), (0,))):
    return lax.dot_general(a, b, (dims, ((), ())), preferred_element_type=F32)


def dot3(a, b, dims=((1,), (0,))):
    (ah, al), (bh, bl) = a, b
    return dot(ah, bh, dims) + (dot(ah, bl, dims) + dot(al, bh, dims))


def swap_groups(values):
    count = len(values)
    width = 128 // count
    lane = lax.broadcasted_iota(jnp.int32, values[0].shape, values[0].ndim - 1)
    axis = values[0].ndim - 1
    values = list(values)
    step = 1
    while step < count:
        first = ((lane // (width * step)) % 2) == 0
        out = list(values)
        for i in range(count):
            if i & step == 0:
                low, high = values[i], values[i + step]
                out[i] = jnp.where(first, low, pltpu.roll(high, width * step, axis))
                out[i + step] = jnp.where(first, pltpu.roll(low, 128 - width * step, axis), high)
        values = out
        step *= 2
    return values


def send(src, dst, sems, where):
    return pltpu.make_async_remote_copy(
        src_ref=src,
        dst_ref=dst,
        send_sem=sems[0],
        recv_sem=sems[1],
        device_id=where,
        device_id_type=pl.DeviceIdType.MESH,
    )


def peers(px, py):
    me = px * NPY + py
    return [lax.rem(me + (53 * k) % DEVICES, DEVICES) for k in range(1, DEVICES)]


def place(device):
    return (device // NPY, lax.rem(device, NPY))


def greet(px, py):
    barrier = pltpu.get_barrier_semaphore()
    for d in range(1, NPY):
        where = (px, lax.rem(py + d, NPY))
        pl.semaphore_signal(barrier, inc=1, device_id=where, device_id_type=pl.DeviceIdType.MESH)
    for d in range(1, NPX):
        where = (lax.rem(px + d, NPX), py)
        pl.semaphore_signal(barrier, inc=1, device_id=where, device_id_type=pl.DeviceIdType.MESH)


def greet_on(inside, px, py):
    for d in range(1, NPX):
        where = (lax.rem(px + d, NPX), py)
        pl.semaphore_signal(inside, inc=1, device_id=where, device_id_type=pl.DeviceIdType.MESH)


class Turn:
    def __init__(self, wire, got, sems, own_sem):
        self.wire, self.got, self.sems, self.own_sem = wire, got, sems, own_sem
        self.px, self.py = lax.axis_index("px"), lax.axis_index("py")
        self.me = self.px * NPY + self.py

    def rows(self, ref, part, device):
        return ref.at[part, pl.ds(pl.multiple_of(device * 8, 8), 8)]

    def own(self, part):
        return pltpu.make_async_copy(
            self.rows(self.wire, part, self.me), self.rows(self.got, part, self.me), self.own_sem.at[part]
        )

    def start(self, part):
        sems = (self.sems.at[0, part], self.sems.at[1, part])
        for peer in peers(self.px, self.py):
            send(
                self.rows(self.wire, part, peer), self.rows(self.got, part, self.me), sems, place(peer)
            ).start()
        self.own(part).start()

    def all(self, side, part):
        block = self.got.at[part, pl.ds(0, 8 * DEVICES - 8)]
        return pltpu.make_async_copy(block, block, self.sems.at[side, part])

    def arrive(self, part):
        self.own(part).wait()
        self.all(1, part).wait()

    def finish(self, part):
        self.all(0, part).wait()


def turn_scratch():
    return [
        pltpu.VMEM((3, 8 * DEVICES, 128), F32),
        pltpu.VMEM((3, 8 * DEVICES, 128), F32),
        pltpu.SemaphoreType.DMA((2, 3)),
        pltpu.SemaphoreType.DMA((3,)),
    ]


class Exchange:
    def __init__(self, axis, wire, got, sems, own_sem):
        self.count = NPX if axis == "px" else NPY
        self.axis, self.wire, self.got, self.sems, self.own_sem = axis, wire, got, sems, own_sem
        self.px, self.py = lax.axis_index("px"), lax.axis_index("py")
        self.me = self.px if axis == "px" else self.py

    def own(self, part):
        return pltpu.make_async_copy(
            self.wire.at[part, self.me], self.got.at[part, self.me], self.own_sem.at[part]
        )

    def start(self, part):
        for d in range(1, self.count):
            peer = lax.rem(self.me + d, self.count)
            where = (peer, self.py) if self.axis == "px" else (self.px, peer)
            sems = (self.sems.at[0, part], self.sems.at[1, part])
            send(self.wire.at[part, peer], self.got.at[part, self.me], sems, where).start()
        self.own(part).start()

    def all(self, side, part):
        block = self.got.at[part, pl.ds(0, self.count - 1)]
        return pltpu.make_async_copy(block, block, self.sems.at[side, part])

    def arrive(self, part):
        self.own(part).wait()
        self.all(1, part).wait()

    def finish(self, part):
        self.all(0, part).wait()


def exchange_scratch(axis, parts, block, dtype=F32):
    count = NPX if axis == "px" else NPY
    return [
        pltpu.VMEM((parts, count) + block, dtype),
        pltpu.VMEM((parts, count) + block, dtype),
        pltpu.SemaphoreType.DMA((2, parts)),
        pltpu.SemaphoreType.DMA((parts,)),
    ]


def sds(shape, dtype=F32):
    return jax.ShapeDtypeStruct(shape, dtype)


def moduli_of(table, ids):
    lame, shear = [], []
    for half in range(2):
        index = ids[:, half * 128 : (half + 1) * 128]
        lame.append(jnp.take_along_axis(table, index, axis=1))
        shear.append(jnp.take_along_axis(table, index + 64, axis=1))
    return jnp.concatenate(lame, axis=1), jnp.concatenate(shear, axis=1)


def table_of(moduli_ref):
    row = jnp.concatenate([moduli_ref[0:1, :], moduli_ref[1:2, :]], axis=1)
    return jnp.broadcast_to(row, (NY, 128))


def polar_part(first, count, dist, ids, table, polar, moduli):
    def at_x(x, carry):
        lame, shear = moduli_of(table, ids[x])
        moduli[0, x] = lame
        moduli[1, x] = shear
        exx, eyy, ezz = dist[0, x], dist[4, x], dist[8, x]
        trace = lame * (exx + eyy + ezz)
        twice = shear + shear
        polar[0, x] = -(twice * exx + trace)
        polar[1, x] = -(twice * eyy + trace)
        polar[2, x] = -(twice * ezz + trace)
        polar[3, x] = -(shear * (dist[5, x] + dist[7, x]))
        polar[4, x] = -(shear * (dist[2, x] + dist[6, x]))
        polar[5, x] = -(shear * (dist[1, x] + dist[3, x]))
        return carry

    lax.fori_loop(first, first + count, at_x, 0)


def row_of(device):
    return (device % NPY) * NPX + device // NPY


def request_part(source, tile, centre, asked):
    src_lane = row_of(source[...]).astype(F32)
    src = jnp.transpose(jnp.broadcast_to(src_lane, (128, 512)))
    same = src[:, 0:1] == src_lane
    first = lax.broadcasted_iota(jnp.int32, (512, 512), 0)
    second = lax.broadcasted_iota(jnp.int32, (512, 512), 1)
    slot_lane = jnp.sum(jnp.where(same & (first < second), 1.0, 0.0), axis=0, keepdims=True)
    match = (src == lax.broadcasted_iota(jnp.int32, (512, 128), 1).astype(F32)).astype(F32).astype(BF16)
    row = lax.broadcasted_iota(jnp.int32, (8, 512), 0).astype(F32)
    here = row == slot_lane
    tile_v = tile[...]
    values = [tile_v // 8, tile_v % 8, centre[...]]
    rows = [jnp.where(here, v.astype(F32), 0.0) for v in values]
    stacked = jnp.concatenate(rows + [jnp.zeros((8, 512), F32)], axis=0).astype(BF16)
    got = dot(stacked, match)
    both = jnp.concatenate([got[0:8] * 8.0 + got[8:16], got[16:24], jnp.zeros((112, 128), F32)], axis=0)
    asked[...] = jnp.transpose(both).astype(jnp.int32)
    return slot_lane


def shift_y(values, before, after):
    row = lax.broadcasted_iota(jnp.int32, values.shape, 0)
    up = jnp.where(row == NY - 1, after, pltpu.roll(values, NY - 1, 0))
    down = jnp.where(row == 0, before, pltpu.roll(values, 1, 0))
    return up - down


LAST = ((1,), (1,))


def forward_z_local(c, polar, tz, waves, force):
    for x in range(NX):
        hi, lo = split(polar[4 - c, x])
        force[0, x * NY : (x + 1) * NY, :] = hi
        force[1, x * NY : (x + 1) * NY, :] = lo
    waves[c] = dot3((tz[0, 1], tz[1, 1]), (force[0], force[1]), LAST)


def forward_z(c, polar, faces, tz, base, wire, force):
    cx = (6 - c) * ((c + 1) // 2)
    cy = 5 - c - 3 * lax.rem(c, 2)
    fx, fy = faces
    for x in range(NX):
        after = fx[1, c] if x == NX - 1 else polar[cx, x + 1]
        before = fx[0, c] if x == 0 else polar[cx, x - 1]
        grad_y = shift_y(polar[cy, x], fy[0, c, x : x + 1, :], fy[1, c, x : x + 1, :])
        hi, lo = split((after - before) + grad_y)
        force[0, x * NY : (x + 1) * NY, :] = hi
        force[1, x * NY : (x + 1) * NY, :] = lo
    waves = base[c] + dot3((tz[0, 0], tz[1, 0]), (force[0], force[1]), LAST)
    for t in range(32):
        for xg in range(4):
            wire[c, pl.ds(32 * t + xg, 8, stride=4), :] = waves[
                8 * t : 8 * t + 8, xg * 128 : xg * 128 + 128
            ]


def forward_plane(c, got, ty, tx, waves, yrows, xrows):
    for q in range(NPX):
        row = q * 64
        low = swap_groups([got[c, row + p * 8 : row + p * 8 + 8, :] for p in range(4)])
        high = swap_groups([got[c, row + p * 8 : row + p * 8 + 8, :] for p in range(4, 8)])
        for x4 in range(4):
            to = pl.ds(q * 4 + x4, 8, stride=64)
            yrows[0, to, :] = low[x4] + high[x4]
            yrows[1, to, :] = low[x4] - high[x4]
    for e in range(2):
        rows = jnp.concatenate([yrows[e, :256, :], yrows[e, 256:, :]], axis=1)
        out = dot3(split(rows), (ty[0, e], ty[1, e]))
        for xg in range(4):
            a, b = out[xg * 64 : xg * 64 + 32, :], out[xg * 64 + 32 : xg * 64 + 64, :]
            for ex in range(2):
                hi, lo = split(a + b if ex == 0 else a - b)
                for ri in range(2):
                    to = slice(ri * 128 + xg * 32, ri * 128 + xg * 32 + 32)
                    xrows[0, ex, to, e * 128 : e * 128 + 128] = hi[:, ri * 128 : ri * 128 + 128]
                    xrows[1, ex, to, e * 128 : e * 128 + 128] = lo[:, ri * 128 : ri * 128 + 128]
    for ex in range(2):
        waves[ex, c] = dot3((tx[0, ex], tx[1, ex]), (xrows[0, ex], xrows[1, ex]))


def solve(waves, solved, sx, sy, sz, kz):
    sy = sy[...]
    sz = sz[pl.ds(kz, 1), :]
    sz = jnp.concatenate([sz, sz], axis=1)
    coupling = (REF_LAMBDA + REF_SHEAR) / (REF_LAMBDA + 2.0 * REF_SHEAR)
    rest = sy * sy + sz * sz
    for ex in range(2):
        wx = jnp.concatenate([sx[ex], sx[ex]], axis=1)
        squared = wx * wx + rest
        null = squared == 0.0
        inverse = jnp.where(null, 0.0, 1.0 / jnp.where(null, 1.0, squared))
        scale = inverse * (1.0 / REF_SHEAR)
        for ri in range(2):
            parts = [waves[ex, c, ri * 128 : ri * 128 + 128, :] for c in range(3)]
            common = coupling * inverse * (wx * parts[0] + sy * parts[1] + sz * parts[2])
            for c, line in enumerate((wx, sy, sz)):
                hi, lo = split(scale * (parts[c] - common * line))
                solved[0, ex, c, ri * 128 : ri * 128 + 128, :] = hi
                solved[1, ex, c, ri * 128 : ri * 128 + 128, :] = lo


def inverse_plane(c, solved, txi, tyi, wire, yrows):
    backs = [dot3((txi[0, ex], txi[1, ex]), (solved[0, ex, c], solved[1, ex, c])) for ex in range(2)]
    halves = (backs[0] + backs[1], backs[0] - backs[1])
    outs = []
    for e in range(2):
        lane = slice(e * 128, e * 128 + 128)
        sides = []
        for ri in range(2):
            blocks = []
            for xg in range(4):
                row = ri * 128 + xg * 32
                blocks += [halves[0][row : row + 32, lane], halves[1][row : row + 32, lane]]
            sides.append(jnp.concatenate(blocks, axis=0))
        outs.append(dot3(split(jnp.concatenate(sides, axis=1)), (tyi[0, e], tyi[1, e])))
    for half, out in enumerate((outs[0] + outs[1], outs[0] - outs[1])):
        yrows[half, :256, :] = out[:, :128]
        yrows[half, 256:, :] = out[:, 128:]
    for q in range(NPX):
        for half in range(2):
            tiles = [yrows[half, pl.ds(q * 4 + x4, 8, stride=64), :] for x4 in range(4)]
            for p, tile in enumerate(swap_groups(tiles)):
                row = q * 64 + half * 32 + p * 8
                wire[c, row : row + 8, :] = tile


def inverse_z(c, got, tzi, disp, yface, lines):
    for xg in range(4):
        turned = jnp.transpose(got[c, pl.ds(xg, 256, stride=4), :])
        hi, lo = split(turned)
        lines[0, xg * 128 : xg * 128 + 128, :] = hi
        lines[1, xg * 128 : xg * 128 + 128, :] = lo
    out = dot3((lines[0], lines[1]), (tzi[0, :, :256], tzi[1, :, :256]))
    for x in range(NX):
        disp[c, x] = out[x * NY : (x + 1) * NY, :]
        yface[0, c, x : x + 1] = out[x * NY : x * NY + 1, :]
        yface[1, c, x : x + 1] = out[x * NY + NY - 1 : x * NY + NY, :]


def inverse_z_grad(c, tzi, grad, lines):
    out = dot3((lines[0], lines[1]), (tzi[0, :, 256:], tzi[1, :, 256:]))
    for x in range(NX):
        grad[c, x] = out[x * NY : (x + 1) * NY, :]


def stress_part(first, count, disp, grad, hx, hy, polar, moduli, stress, rows):
    def at_x(x, carry):
        lame, shear = moduli[0, x], moduli[1, x]
        gx, gy, gz = [], [], []
        for c in range(3):
            after = hx[1, c] if first == NX - 1 else disp[c, x + 1]
            before = hx[0, c] if first == 0 else disp[c, x - 1]
            gx.append(after - before)
            gy.append(shift_y(disp[c, x], hy[0, c, pl.ds(x, 1), :], hy[1, c, pl.ds(x, 1), :]))
            gz.append(grad[c, x])
        trace = (0.5 * lame) * (gx[0] + gy[1] + gz[2])
        half = 0.5 * shear
        parts = (
            shear * gx[0] + trace,
            shear * gy[1] + trace,
            shear * gz[2] + trace,
            half * (gz[1] + gy[2]),
            half * (gz[0] + gx[2]),
            half * (gy[0] + gx[1]),
        )
        row = pl.ds(pl.multiple_of(x * NY, NY), NY)
        for c, part in enumerate(parts):
            total = part + polar[c, x]
            stress[c, x] = total
            hi, lo = split(total)
            rows[0, row, c * 256 : c * 256 + 256] = hi
            rows[1, row, c * 256 : c * 256 + 256] = lo
        return carry

    lax.fori_loop(first, first + count, at_x, 0)


def pick_part(asked, weights, pick, gain):
    column = lax.broadcasted_iota(jnp.int32, (128, 512), 1)
    lane = lax.broadcasted_iota(jnp.int32, (128, 128), 1)
    lane256 = lax.broadcasted_iota(jnp.int32, (128, 256), 1)
    for k in range(8):
        here = slice(k * 128, k * 128 + 128)
        tile = asked[:, k : k + 1]
        centre = asked[:, 8 + k : 9 + k]
        pick[here, :] = (column == tile // 2).astype(F32).astype(BF16)
        at = (lane == centre).astype(F32).astype(BF16)
        row = dot(at, weights[0]) + dot(at, weights[1])
        row = jnp.concatenate([row, row], axis=1)
        gain[here, :] = jnp.where(lane256 // 128 == tile % 2, row, 0.0)


def reply_part(pick, gain, rows, reply):
    lane = lax.broadcasted_iota(jnp.int32, (128, 128), 1)
    out = jnp.zeros((128, 128), F32)
    for c in range(6):
        here = slice(c * 256, c * 256 + 256)
        picked = dot(pick[...], rows[0, :, here]) + dot(pick[...], rows[1, :, here])
        picked = picked * gain[...]
        total = jnp.sum(picked[:, :128] + picked[:, 128:], axis=1, keepdims=True)
        for k in range(8):
            out = jnp.where(lane == c * 8 + k, total[k * 128 : k * 128 + 128], out)
    reply[...] = out


def force_part(reply, match, mine, burgers, line, out):
    hi, lo = split(reply)
    low = (reply - hi.astype(F32) - lo.astype(F32)).astype(BF16)
    first = ((0,), (0,))
    match = match[...]
    got = dot(hi, match, first) + (dot(lo, match, first) + dot(low, match, first))
    mine = got * mine[...]
    t = [jnp.sum(mine[c * 8 : c * 8 + 8, :], axis=0, keepdims=True) for c in range(6)]
    b = [burgers[i : i + 1, :] for i in range(3)]
    v = [line[i : i + 1, :] for i in range(3)]
    push_x = t[0] * b[0] + t[5] * b[1] + t[4] * b[2]
    push_y = t[5] * b[0] + t[1] * b[1] + t[3] * b[2]
    push_z = t[4] * b[0] + t[3] * b[1] + t[2] * b[2]
    out[0:1, :] = push_y * v[2] - push_z * v[1]
    out[1:2, :] = push_z * v[0] - push_x * v[2]
    out[2:3, :] = push_x * v[1] - push_y * v[0]


def scratch_plan():
    half = pltpu.VMEM((2, 2, 256, 256), BF16)
    sem = pltpu.SemaphoreType.DMA
    plan = {
        "inside": pltpu.SemaphoreType.REGULAR,
        "dist": pltpu.VMEM((9, NX, NY, GRID), F32),
        "ids": pltpu.VMEM((NX, NY, GRID), jnp.int32),
        "load_sem": sem((2, 4)),
        "polar": pltpu.VMEM((6, NX, NY, GRID), F32),
        "moduli": pltpu.VMEM((2, NX, NY, GRID), F32),
        "tz": half,
        "ty": half,
        "tx": half,
        "txi": half,
        "tyi": half,
        "tzi": pltpu.VMEM((2, 256, 512), BF16),
        "table_sem": sem((6,)),
        "ox": pltpu.VMEM((2, 3, NY, GRID), F32),
        "oy": pltpu.VMEM((2, 3, NX, GRID), F32),
        "fx": pltpu.VMEM((2, 3, NY, GRID), F32),
        "fy": pltpu.VMEM((2, 3, NX, GRID), F32),
        "face_sem": sem((2, 4)),
        "hx": pltpu.VMEM((2, 3, NY, GRID), F32),
        "hy": pltpu.VMEM((2, 3, NX, GRID), F32),
        "yface": pltpu.VMEM((2, 3, NX, GRID), F32),
        "back_sem": sem((3, 2, 4)),
        "base": pltpu.VMEM((3, 256, 512), F32),
        "force": pltpu.VMEM((2, 512, 256), BF16),
        "yrows": pltpu.VMEM((2, 512, 128), F32),
        "xrows": half,
        "waves": pltpu.VMEM((2, 3, 256, 256), F32),
        "solved": pltpu.VMEM((2, 2, 3, 256, 256), BF16),
        "lines": pltpu.VMEM((2, 512, 256), BF16),
        "disp": pltpu.VMEM((3, NX, NY, GRID), F32),
        "grad": pltpu.VMEM((3, NX, NY, GRID), F32),
        "stress": pltpu.VMEM((6, NX, NY, GRID), F32),
        "store_sem": sem((1,)),
        "rows": pltpu.VMEM((2, 512, 1536), BF16),
        "asked": pltpu.VMEM((128, 128), jnp.int32),
        "pick": pltpu.VMEM((1024, 512), BF16),
        "gain": pltpu.VMEM((1024, 256), F32),
        "slot": pltpu.VMEM((1, 512), F32),
        "reply": pltpu.VMEM((128, 128), F32),
        "match": pltpu.VMEM((128, 512), BF16),
        "mine": pltpu.VMEM((128, 512), F32),
    }
    exchanges = {
        "exa": ("py", 1, (NPX, 128), jnp.int32),
        "exb": ("px", 1, (NPY, 128), jnp.int32),
        "exc": ("px", 1, (NPY, 128), F32),
        "exd": ("py", 1, (NPX, 128), F32),
    }
    return plan, exchanges


class Names:
    pass


def whole_body(*refs):
    plan, exchanges = scratch_plan()
    n_in, n_out = 18, 2
    (
        moduli_in, source, tile, centre, burgers, line, sx, sy, sz, weights,
        dist_h, ids_h, tz_h, ty_h, tx_h, txi_h, tyi_h, tzi_h,
    ) = refs[:n_in]
    stress_h, seg_force = refs[n_in : n_in + n_out]
    rest = list(refs[n_in + n_out :])
    r = Names()
    for name in plan:
        setattr(r, name, rest.pop(0))
    for name, (axis, _, _, _) in exchanges.items():
        setattr(r, name, Exchange(axis, rest.pop(0), rest.pop(0), rest.pop(0), rest.pop(0)))

    r.there = Turn(rest.pop(0), rest.pop(0), rest.pop(0), rest.pop(0))
    r.back = Turn(rest.pop(0), rest.pop(0), rest.pop(0), rest.pop(0))

    px, py = lax.axis_index("px"), lax.axis_index("py")
    loads = []
    for g in range(4):
        here = pl.ds(g * 4, 4)
        loads.append(
            (
                pltpu.make_async_copy(dist_h.at[:, here], r.dist.at[:, here], r.load_sem.at[0, g]),
                pltpu.make_async_copy(ids_h.at[here], r.ids.at[here], r.load_sem.at[1, g]),
            )
        )
        for load in loads[-1]:
            load.start()
    pairs = ((tz_h, r.tz), (ty_h, r.ty), (tx_h, r.tx), (txi_h, r.txi), (tyi_h, r.tyi), (tzi_h, r.tzi))
    tables = [pltpu.make_async_copy(a, b, r.table_sem.at[i]) for i, (a, b) in enumerate(pairs)]
    for table in tables:
        table.start()
    greet(px, py)

    slot = request_part(source, tile, centre, r.asked)
    r.slot[...] = slot
    for p in range(NPY):
        r.exa.wire[0, p] = r.asked[p * NPX : p * NPX + NPX, :]
    lookup = table_of(moduli_in)
    for g in range(4):
        for load in loads[g]:
            load.wait()
        polar_part(g * 4, 4, r.dist, r.ids, lookup, r.polar, r.moduli)
    for side in range(2):
        for k, comp in enumerate((0, 5, 4)):
            r.ox[side, k] = r.polar[comp, side * (NX - 1)]
        for k, comp in enumerate((5, 1, 3)):
            r.oy[side, k] = r.polar[comp, :, side * (NY - 1), :]

    left, right = lax.rem(px + NPX - 1, NPX), lax.rem(px + 1, NPX)
    down, up = lax.rem(py + NPY - 1, NPY), lax.rem(py + 1, NPY)
    sides = [(left, py), (right, py), (px, down), (px, up)]

    def face(src, dst, sems, to, k):
        return send(src, dst, (sems.at[0, k], sems.at[1, k]), sides[to])

    halo = [
        face(r.ox.at[0], r.fx.at[1], r.face_sem, 0, 1),
        face(r.ox.at[1], r.fx.at[0], r.face_sem, 1, 0),
        face(r.oy.at[0], r.fy.at[1], r.face_sem, 2, 3),
        face(r.oy.at[1], r.fy.at[0], r.face_sem, 3, 2),
    ]
    pl.semaphore_wait(pltpu.get_barrier_semaphore(), NPX + NPY - 2)
    for copy in halo:
        copy.start()
    greet_on(r.inside, px, py)
    r.exa.start(0)
    tables[0].wait()

    def local(c, carry):
        forward_z_local(c, r.polar, r.tz, r.base, r.force)
        return carry

    lax.fori_loop(0, 3, local, 0)
    for copy in halo:
        copy.wait_recv()

    for c in range(3):
        forward_z(c, r.polar, (r.fx, r.fy), r.tz, r.base, r.there.wire, r.force)
        if c == 0:
            pl.semaphore_wait(r.inside, NPX - 1)
        r.there.start(c)
    r.exa.arrive(0)
    r.asked[...] = r.exa.got[0].reshape(128, 128)
    for p in range(NPX):
        r.exb.wire[0, p] = r.asked[pl.ds(p, NPY, stride=NPX), :]
    r.exb.start(0)
    owners = lax.broadcasted_iota(jnp.int32, (128, 512), 0)
    r.match[...] = (owners == row_of(source[...])).astype(F32).astype(BF16)
    r.mine[...] = jnp.where((owners % 8).astype(F32) == r.slot[...], 1.0, 0.0)
    tables[1].wait()
    tables[2].wait()

    def step_plane(c, carry):
        r.there.arrive(c)
        forward_plane(c, r.there.got, r.ty, r.tx, r.waves, r.yrows, r.xrows)
        return carry

    lax.fori_loop(0, 3, step_plane, 0)
    solve(r.waves, r.solved, sx, sy, sz, px * NPY + py)
    tables[3].wait()
    tables[4].wait()

    def step_back(c, carry):
        inverse_plane(c, r.solved, r.txi, r.tyi, r.back.wire, r.yrows)
        r.back.start(c)
        return carry

    lax.fori_loop(0, 3, step_back, 0)
    tables[5].wait()
    r.exb.arrive(0)
    for p in range(NPX):
        r.asked[p * NPY : p * NPY + NPY, :] = r.exb.got[0, p]
    pick_part(r.asked, weights, r.pick, r.gain)

    def faces_back(c):
        sems = r.back_sem.at[c]
        return [
            face(r.disp.at[c, 0], r.hx.at[1, c], sems, 0, 1),
            face(r.disp.at[c, NX - 1], r.hx.at[0, c], sems, 1, 0),
            face(r.yface.at[0, c], r.hy.at[1, c], sems, 2, 3),
            face(r.yface.at[1, c], r.hy.at[0, c], sems, 3, 2),
        ]

    backs = []
    for c in range(3):
        r.back.arrive(c)
        inverse_z(c, r.back.got, r.tzi, r.disp, r.yface, r.lines)
        backs += faces_back(c)
        for copy in backs[4 * c :]:
            copy.start()
        inverse_z_grad(c, r.tzi, r.grad, r.lines)

    for copy in backs:
        copy.wait_recv()
    for first, count in ((0, 1), (1, 14), (15, 1)):
        stress_part(
            first, count, r.disp, r.grad, r.hx, r.hy, r.polar, r.moduli, r.stress, r.rows
        )
    store = pltpu.make_async_copy(r.stress, stress_h, r.store_sem.at[0])
    store.start()
    reply_part(r.pick, r.gain, r.rows, r.reply)
    for p in range(NPX):
        r.exc.wire[0, p] = r.reply[p * NPY : p * NPY + NPY, :]
    r.exc.start(0)
    for copy in halo + backs:
        copy.wait_send()
    for c in range(3):
        r.there.finish(c)
        r.back.finish(c)
    r.exa.finish(0)
    r.exb.finish(0)
    r.exc.arrive(0)
    r.reply[...] = r.exc.got[0].reshape(128, 128)
    for p in range(NPY):
        r.exd.wire[0, p] = r.reply[pl.ds(p, NPX, stride=NPY), :]
    r.exd.start(0)
    store.wait()
    r.exd.arrive(0)
    force_part(r.exd.got[0].reshape(128, 128), r.match, r.mine, burgers, line, seg_force)
    r.exc.finish(0)
    r.exd.finish(0)


def shards(dist, ids, moduli, seg_source, seg_tile, seg_center, burgers, line_vector):
    fwd_z, inv_z = z_tables()
    fwd_h, inv_h = half_tables()
    order = x_order()
    tz, tzi = two_parts(fwd_z), two_parts(inv_z)
    tx, txi = two_parts(fwd_h[:, :, order]), two_parts(inv_h[:, order, :])
    ty = two_parts(fwd_h.transpose(0, 2, 1))
    tyi = two_parts(inv_h.transpose(0, 2, 1))
    sx, sy, sz = wave_lines()
    weights = two_parts(tile_weights())
    plan, exchanges = scratch_plan()
    scratch = list(plan.values())
    for axis, parts, block, dtype in exchanges.values():
        scratch += exchange_scratch(axis, parts, block, dtype)
    scratch += turn_scratch() + turn_scratch()
    hbm = pl.BlockSpec(memory_space=pl.ANY)
    return tuple(
        pl.pallas_call(
            whole_body,
            out_shape=(sds((6, NX, NY, GRID)), sds((3, 512))),
            in_specs=[VM] * 10 + [hbm] * 8,
            out_specs=(hbm, VM),
            scratch_shapes=scratch,
            compiler_params=pltpu.CompilerParams(
                vmem_limit_bytes=VMEM_LIMIT, collective_id=0, has_side_effects=True
            ),
        )(
            moduli,
            seg_source.reshape(1, 512),
            seg_tile.reshape(1, 512),
            seg_center.reshape(1, 512),
            burgers,
            line_vector,
            sx,
            sy,
            sz,
            weights,
            dist,
            ids,
            tz,
            ty,
            tx,
            txi,
            tyi,
            tzi,
        )
    )


def solution(mesh):
    return jax.shard_map(
        shards,
        mesh=mesh,
        in_specs=(
            P(None, "px", "py", None),
            P("px", "py", None),
            P(),
            P(("px", "py"), None),
            P(("px", "py")),
            P(("px", "py")),
            P(None, ("px", "py")),
            P(None, ("px", "py")),
        ),
        out_specs=(P(None, "px", "py", None), P(None, ("px", "py"))),
        check_vma=False,
    )
```

```python
import functools

import jax
import jax.numpy as jnp
import ml_dtypes
import numpy as np
from jax import lax
from jax.experimental import pallas as pl
from jax.experimental.pallas import tpu as pltpu
from jax.sharding import PartitionSpec as P

F32 = jnp.float32
BF16 = jnp.bfloat16
REF_LAMBDA = 1.25
REF_SHEAR = 1.25
GRID = 256
HALF = 128
NPX = 16
NPY = 8
DEVICES = NPX * NPY
NX = 16
NY = 32
VMEM_LIMIT = 60 * 1024 * 1024
VM = pl.BlockSpec(memory_space=pltpu.VMEM)


def two_parts(table):
    table = np.asarray(table, np.float32)
    high = table.astype(ml_dtypes.bfloat16)
    low = (table - high.astype(np.float32)).astype(ml_dtypes.bfloat16)
    return np.stack([high, low])


def z_tables():
    z = np.arange(GRID)
    fwd = np.zeros((GRID, GRID))
    inv = np.zeros((GRID, GRID))
    for row in range(GRID):
        wave, ri = row // 2, row % 2
        angle = 2 * np.pi * ((wave * z) % GRID) / GRID
        if wave == 0:
            line = np.ones(GRID) if ri == 0 else 1.0 - 2.0 * (z % 2)
            fwd[row], inv[row] = line, line / GRID
        else:
            line = np.cos(angle) if ri == 0 else -np.sin(angle)
            fwd[row], inv[row] = line, 2 * line / GRID
    step = np.roll(np.eye(GRID), 1, 1) - np.roll(np.eye(GRID), -1, 1)
    fwd = 0.5 * np.stack([fwd, fwd @ step])
    inv = np.concatenate([inv, inv @ step.T], axis=1)
    return fwd, inv


def half_tables():
    k = np.arange(HALF)
    fwd, inv = [], []
    for e in range(2):
        angle = 2 * np.pi * (((2 * k[:, None] + e) * k[None, :]) % GRID) / GRID
        cos, sin = np.cos(angle), np.sin(angle)
        fwd.append(np.block([[cos, sin], [-sin, cos]]))
        inv.append(np.block([[cos.T, -sin.T], [sin.T, cos.T]]) / GRID)
    return np.stack(fwd), np.stack(inv)


def x_order():
    index = np.arange(HALF).reshape(8, 4, 4)
    order = index.transpose(1, 0, 2).reshape(-1)
    return np.concatenate([order, order + HALF])


def sines():
    wave = np.arange(GRID)
    line = np.sin(2 * np.pi * wave / GRID)
    line[wave % HALF == 0] = 0.0
    return line


def wave_lines():
    line = sines()
    sx = np.stack([line[0::2], line[1::2]])[:, :, None] * np.ones((1, 1, 128))
    sy = np.concatenate([line[0::2], line[1::2]])[None, :]
    sz = line[:128, None] * np.ones((1, 128))
    return sx.astype(np.float32), sy.astype(np.float32), sz.astype(np.float32)


def tile_weights():
    v = np.arange(128, dtype=np.float64)
    weights = np.exp(-((v[None, :] - v[:, None]) ** 2) / (2.0 * 16.0**2))
    return weights / weights.sum(axis=1, keepdims=True)


def split(values):
    high = values.astype(BF16)
    low = (values - high.astype(F32)).astype(BF16)
    return high, low


def dot(a, b, dims=((1,), (0,))):
    return lax.dot_general(a, b, (dims, ((), ())), preferred_element_type=F32)


def dot3(a, b, dims=((1,), (0,))):
    (ah, al), (bh, bl) = a, b
    return dot(ah, bh, dims) + (dot(ah, bl, dims) + dot(al, bh, dims))


def swap_groups(values):
    count = len(values)
    width = 128 // count
    lane = lax.broadcasted_iota(jnp.int32, values[0].shape, values[0].ndim - 1)
    axis = values[0].ndim - 1
    values = list(values)
    step = 1
    while step < count:
        first = ((lane // (width * step)) % 2) == 0
        out = list(values)
        for i in range(count):
            if i & step == 0:
                low, high = values[i], values[i + step]
                out[i] = jnp.where(first, low, pltpu.roll(high, width * step, axis))
                out[i + step] = jnp.where(first, pltpu.roll(low, 128 - width * step, axis), high)
        values = out
        step *= 2
    return values


def send(src, dst, sems, where):
    return pltpu.make_async_remote_copy(
        src_ref=src,
        dst_ref=dst,
        send_sem=sems[0],
        recv_sem=sems[1],
        device_id=where,
        device_id_type=pl.DeviceIdType.MESH,
    )


def peers(px, py):
    me = px * NPY + py
    return [lax.rem(me + (53 * k) % DEVICES, DEVICES) for k in range(1, DEVICES)]


def place(device):
    return (device // NPY, lax.rem(device, NPY))


def greet(px, py):
    barrier = pltpu.get_barrier_semaphore()
    for d in range(1, NPY):
        where = (px, lax.rem(py + d, NPY))
        pl.semaphore_signal(barrier, inc=1, device_id=where, device_id_type=pl.DeviceIdType.MESH)
    for d in range(1, NPX):
        where = (lax.rem(px + d, NPX), py)
        pl.semaphore_signal(barrier, inc=1, device_id=where, device_id_type=pl.DeviceIdType.MESH)


def greet_on(inside, px, py):
    for d in range(1, NPX):
        where = (lax.rem(px + d, NPX), py)
        pl.semaphore_signal(inside, inc=1, device_id=where, device_id_type=pl.DeviceIdType.MESH)


class Turn:
    def __init__(self, wire, got, sems, own_sem):
        self.wire, self.got, self.sems, self.own_sem = wire, got, sems, own_sem
        self.px, self.py = lax.axis_index("px"), lax.axis_index("py")
        self.me = self.px * NPY + self.py

    def rows(self, ref, part, device):
        return ref.at[part, pl.ds(pl.multiple_of(device * 8, 8), 8)]

    def own(self, part):
        return pltpu.make_async_copy(
            self.rows(self.wire, part, self.me), self.rows(self.got, part, self.me), self.own_sem.at[part]
        )

    def start(self, part):
        sems = (self.sems.at[0, part], self.sems.at[1, part])
        for peer in peers(self.px, self.py):
            send(
                self.rows(self.wire, part, peer), self.rows(self.got, part, self.me), sems, place(peer)
            ).start()
        self.own(part).start()

    def all(self, side, part):
        block = self.got.at[part, pl.ds(0, 8 * DEVICES - 8)]
        return pltpu.make_async_copy(block, block, self.sems.at[side, part])

    def arrive(self, part):
        self.own(part).wait()
        self.all(1, part).wait()

    def finish(self, part):
        self.all(0, part).wait()


def turn_scratch():
    return [
        pltpu.VMEM((3, 8 * DEVICES, 128), F32),
        pltpu.VMEM((3, 8 * DEVICES, 128), F32),
        pltpu.SemaphoreType.DMA((2, 3)),
        pltpu.SemaphoreType.DMA((3,)),
    ]


class Exchange:
    def __init__(self, axis, wire, got, sems, own_sem):
        self.count = NPX if axis == "px" else NPY
        self.axis, self.wire, self.got, self.sems, self.own_sem = axis, wire, got, sems, own_sem
        self.px, self.py = lax.axis_index("px"), lax.axis_index("py")
        self.me = self.px if axis == "px" else self.py

    def own(self, part):
        return pltpu.make_async_copy(
            self.wire.at[part, self.me], self.got.at[part, self.me], self.own_sem.at[part]
        )

    def start(self, part):
        for d in range(1, self.count):
            peer = lax.rem(self.me + d, self.count)
            where = (peer, self.py) if self.axis == "px" else (self.px, peer)
            sems = (self.sems.at[0, part], self.sems.at[1, part])
            send(self.wire.at[part, peer], self.got.at[part, self.me], sems, where).start()
        self.own(part).start()

    def all(self, side, part):
        block = self.got.at[part, pl.ds(0, self.count - 1)]
        return pltpu.make_async_copy(block, block, self.sems.at[side, part])

    def arrive(self, part):
        self.own(part).wait()
        self.all(1, part).wait()

    def finish(self, part):
        self.all(0, part).wait()


def exchange_scratch(axis, parts, block, dtype=F32):
    count = NPX if axis == "px" else NPY
    return [
        pltpu.VMEM((parts, count) + block, dtype),
        pltpu.VMEM((parts, count) + block, dtype),
        pltpu.SemaphoreType.DMA((2, parts)),
        pltpu.SemaphoreType.DMA((parts,)),
    ]


def sds(shape, dtype=F32):
    return jax.ShapeDtypeStruct(shape, dtype)


def moduli_of(table, ids):
    lame, shear = [], []
    for half in range(2):
        index = ids[:, half * 128 : (half + 1) * 128]
        lame.append(jnp.take_along_axis(table, index, axis=1))
        shear.append(jnp.take_along_axis(table, index + 64, axis=1))
    return jnp.concatenate(lame, axis=1), jnp.concatenate(shear, axis=1)


def table_of(moduli_ref):
    row = jnp.concatenate([moduli_ref[0:1, :], moduli_ref[1:2, :]], axis=1)
    return jnp.broadcast_to(row, (NY, 128))


def polar_part(first, count, dist, ids, table, polar, moduli):
    def at_x(x, carry):
        lame, shear = moduli_of(table, ids[x])
        moduli[0, x] = lame
        moduli[1, x] = shear
        exx, eyy, ezz = dist[0, x], dist[4, x], dist[8, x]
        trace = lame * (exx + eyy + ezz)
        twice = shear + shear
        polar[0, x] = -(twice * exx + trace)
        polar[1, x] = -(twice * eyy + trace)
        polar[2, x] = -(twice * ezz + trace)
        polar[3, x] = -(shear * (dist[5, x] + dist[7, x]))
        polar[4, x] = -(shear * (dist[2, x] + dist[6, x]))
        polar[5, x] = -(shear * (dist[1, x] + dist[3, x]))
        return carry

    lax.fori_loop(first, first + count, at_x, 0)


def row_of(device):
    return (device % NPY) * NPX + device // NPY


def request_part(source, tile, centre, asked):
    src_lane = row_of(source[...]).astype(F32)
    src = jnp.transpose(jnp.broadcast_to(src_lane, (128, 512)))
    same = src[:, 0:1] == src_lane
    first = lax.broadcasted_iota(jnp.int32, (512, 512), 0)
    second = lax.broadcasted_iota(jnp.int32, (512, 512), 1)
    slot_lane = jnp.sum(jnp.where(same & (first < second), 1.0, 0.0), axis=0, keepdims=True)
    match = (src == lax.broadcasted_iota(jnp.int32, (512, 128), 1).astype(F32)).astype(F32).astype(BF16)
    row = lax.broadcasted_iota(jnp.int32, (8, 512), 0).astype(F32)
    here = row == slot_lane
    tile_v = tile[...]
    values = [tile_v // 8, tile_v % 8, centre[...]]
    rows = [jnp.where(here, v.astype(F32), 0.0) for v in values]
    stacked = jnp.concatenate(rows + [jnp.zeros((8, 512), F32)], axis=0).astype(BF16)
    got = dot(stacked, match)
    both = jnp.concatenate([got[0:8] * 8.0 + got[8:16], got[16:24], jnp.zeros((112, 128), F32)], axis=0)
    asked[...] = jnp.transpose(both).astype(jnp.int32)
    return slot_lane


def shift_y(values, before, after):
    row = lax.broadcasted_iota(jnp.int32, values.shape, 0)
    up = jnp.where(row == NY - 1, after, pltpu.roll(values, NY - 1, 0))
    down = jnp.where(row == 0, before, pltpu.roll(values, 1, 0))
    return up - down


LAST = ((1,), (1,))


def forward_z_local(c, polar, tz, waves, force):
    for x in range(NX):
        hi, lo = split(polar[4 - c, x])
        force[0, x * NY : (x + 1) * NY, :] = hi
        force[1, x * NY : (x + 1) * NY, :] = lo
    waves[c] = dot3((tz[0, 1], tz[1, 1]), (force[0], force[1]), LAST)


def forward_z(c, polar, faces, tz, base, wire, force):
    cx = (6 - c) * ((c + 1) // 2)
    cy = 5 - c - 3 * lax.rem(c, 2)
    fx, fy = faces
    for x in range(NX):
        after = fx[1, c] if x == NX - 1 else polar[cx, x + 1]
        before = fx[0, c] if x == 0 else polar[cx, x - 1]
        grad_y = shift_y(polar[cy, x], fy[0, c, x : x + 1, :], fy[1, c, x : x + 1, :])
        hi, lo = split((after - before) + grad_y)
        force[0, x * NY : (x + 1) * NY, :] = hi
        force[1, x * NY : (x + 1) * NY, :] = lo
    waves = base[c] + dot3((tz[0, 0], tz[1, 0]), (force[0], force[1]), LAST)
    for t in range(32):
        for xg in range(4):
            wire[c, pl.ds(32 * t + xg, 8, stride=4), :] = waves[
                8 * t : 8 * t + 8, xg * 128 : xg * 128 + 128
            ]


def forward_plane(c, got, ty, tx, waves, yrows, xrows):
    for q in range(NPX):
        row = q * 64
        low = swap_groups([got[c, row + p * 8 : row + p * 8 + 8, :] for p in range(4)])
        high = swap_groups([got[c, row + p * 8 : row + p * 8 + 8, :] for p in range(4, 8)])
        for x4 in range(4):
            to = pl.ds(q * 4 + x4, 8, stride=64)
            yrows[0, to, :] = low[x4] + high[x4]
            yrows[1, to, :] = low[x4] - high[x4]
    for e in range(2):
        rows = jnp.concatenate([yrows[e, :256, :], yrows[e, 256:, :]], axis=1)
        out = dot3(split(rows), (ty[0, e], ty[1, e]))
        for xg in range(4):
            a, b = out[xg * 64 : xg * 64 + 32, :], out[xg * 64 + 32 : xg * 64 + 64, :]
            for ex in range(2):
                hi, lo = split(a + b if ex == 0 else a - b)
                for ri in range(2):
                    to = slice(ri * 128 + xg * 32, ri * 128 + xg * 32 + 32)
                    xrows[0, ex, to, e * 128 : e * 128 + 128] = hi[:, ri * 128 : ri * 128 + 128]
                    xrows[1, ex, to, e * 128 : e * 128 + 128] = lo[:, ri * 128 : ri * 128 + 128]
    for ex in range(2):
        waves[ex, c] = dot3((tx[0, ex], tx[1, ex]), (xrows[0, ex], xrows[1, ex]))


def solve(waves, solved, sx, sy, sz, kz):
    sy = sy[...]
    sz = sz[pl.ds(kz, 1), :]
    sz = jnp.concatenate([sz, sz], axis=1)
    coupling = (REF_LAMBDA + REF_SHEAR) / (REF_LAMBDA + 2.0 * REF_SHEAR)
    rest = sy * sy + sz * sz
    for ex in range(2):
        wx = jnp.concatenate([sx[ex], sx[ex]], axis=1)
        squared = wx * wx + rest
        null = squared == 0.0
        inverse = jnp.where(null, 0.0, 1.0 / jnp.where(null, 1.0, squared))
        scale = inverse * (1.0 / REF_SHEAR)
        for ri in range(2):
            parts = [waves[ex, c, ri * 128 : ri * 128 + 128, :] for c in range(3)]
            common = coupling * inverse * (wx * parts[0] + sy * parts[1] + sz * parts[2])
            for c, line in enumerate((wx, sy, sz)):
                hi, lo = split(scale * (parts[c] - common * line))
                solved[0, ex, c, ri * 128 : ri * 128 + 128, :] = hi
                solved[1, ex, c, ri * 128 : ri * 128 + 128, :] = lo


def inverse_plane(c, solved, txi, tyi, wire, yrows):
    backs = [dot3((txi[0, ex], txi[1, ex]), (solved[0, ex, c], solved[1, ex, c])) for ex in range(2)]
    halves = (backs[0] + backs[1], backs[0] - backs[1])
    outs = []
    for e in range(2):
        lane = slice(e * 128, e * 128 + 128)
        sides = []
        for ri in range(2):
            blocks = []
            for xg in range(4):
                row = ri * 128 + xg * 32
                blocks += [halves[0][row : row + 32, lane], halves[1][row : row + 32, lane]]
            sides.append(jnp.concatenate(blocks, axis=0))
        outs.append(dot3(split(jnp.concatenate(sides, axis=1)), (tyi[0, e], tyi[1, e])))
    for half, out in enumerate((outs[0] + outs[1], outs[0] - outs[1])):
        yrows[half, :256, :] = out[:, :128]
        yrows[half, 256:, :] = out[:, 128:]
    for q in range(NPX):
        for half in range(2):
            tiles = [yrows[half, pl.ds(q * 4 + x4, 8, stride=64), :] for x4 in range(4)]
            for p, tile in enumerate(swap_groups(tiles)):
                row = q * 64 + half * 32 + p * 8
                wire[c, row : row + 8, :] = tile


def inverse_z(c, got, tzi, disp, yface, lines):
    for xg in range(4):
        turned = jnp.transpose(got[c, pl.ds(xg, 256, stride=4), :])
        hi, lo = split(turned)
        lines[0, xg * 128 : xg * 128 + 128, :] = hi
        lines[1, xg * 128 : xg * 128 + 128, :] = lo
    out = dot3((lines[0], lines[1]), (tzi[0, :, :256], tzi[1, :, :256]))
    for x in range(NX):
        disp[c, x] = out[x * NY : (x + 1) * NY, :]
        yface[0, c, x : x + 1] = out[x * NY : x * NY + 1, :]
        yface[1, c, x : x + 1] = out[x * NY + NY - 1 : x * NY + NY, :]


def inverse_z_grad(c, tzi, grad, lines):
    out = dot3((lines[0], lines[1]), (tzi[0, :, 256:], tzi[1, :, 256:]))
    for x in range(NX):
        grad[c, x] = out[x * NY : (x + 1) * NY, :]


def stress_part(first, count, late, disp, grad, hx, hy, polar, moduli, stress, rows):
    def at_x(x, carry):
        shear = moduli[1, x]
        row = pl.ds(pl.multiple_of(x * NY, NY), NY)

        def grad_x(c):
            after = hx[1, c] if first == NX - 1 else disp[c, x + 1]
            before = hx[0, c] if first == 0 else disp[c, x - 1]
            return after - before

        def grad_y(c):
            return shift_y(disp[c, x], hy[0, c, pl.ds(x, 1), :], hy[1, c, pl.ds(x, 1), :])

        half = 0.5 * shear
        if late:
            parts = {3: half * (grad[1, x] + grad_y(2)), 4: half * (grad[0, x] + grad_x(2))}
        else:
            exx, eyy, ezz = grad_x(0), grad_y(1), grad[2, x]
            trace = (0.5 * moduli[0, x]) * (exx + eyy + ezz)
            parts = {
                0: shear * exx + trace,
                1: shear * eyy + trace,
                2: shear * ezz + trace,
                5: half * (grad_y(0) + grad_x(1)),
            }
        for c, part in parts.items():
            total = part + polar[c, x]
            stress[c, x] = total
            hi, lo = split(total)
            rows[0, row, c * 256 : c * 256 + 256] = hi
            rows[1, row, c * 256 : c * 256 + 256] = lo
        return carry

    lax.fori_loop(first, first + count, at_x, 0)


def pick_part(asked, weights, pick, gain):
    column = lax.broadcasted_iota(jnp.int32, (128, 512), 1)
    lane = lax.broadcasted_iota(jnp.int32, (128, 128), 1)
    lane256 = lax.broadcasted_iota(jnp.int32, (128, 256), 1)
    for k in range(8):
        here = slice(k * 128, k * 128 + 128)
        tile = asked[:, k : k + 1]
        centre = asked[:, 8 + k : 9 + k]
        pick[here, :] = (column == tile // 2).astype(F32).astype(BF16)
        at = (lane == centre).astype(F32).astype(BF16)
        row = dot(at, weights[0]) + dot(at, weights[1])
        row = jnp.concatenate([row, row], axis=1)
        gain[here, :] = jnp.where(lane256 // 128 == tile % 2, row, 0.0)


def reply_part(comps, pick, gain, rows, out):
    lane = lax.broadcasted_iota(jnp.int32, (128, 128), 1)
    for c in comps:
        here = slice(c * 256, c * 256 + 256)
        picked = dot(pick[...], rows[0, :, here]) + dot(pick[...], rows[1, :, here])
        picked = picked * gain[...]
        total = jnp.sum(picked[:, :128] + picked[:, 128:], axis=1, keepdims=True)
        for k in range(8):
            out = jnp.where(lane == c * 8 + k, total[k * 128 : k * 128 + 128], out)
    return out


def force_part(reply, match, mine, burgers, line, out):
    hi, lo = split(reply)
    low = (reply - hi.astype(F32) - lo.astype(F32)).astype(BF16)
    first = ((0,), (0,))
    match = match[...]
    got = dot(hi, match, first) + (dot(lo, match, first) + dot(low, match, first))
    mine = got * mine[...]
    t = [jnp.sum(mine[c * 8 : c * 8 + 8, :], axis=0, keepdims=True) for c in range(6)]
    b = [burgers[i : i + 1, :] for i in range(3)]
    v = [line[i : i + 1, :] for i in range(3)]
    push_x = t[0] * b[0] + t[5] * b[1] + t[4] * b[2]
    push_y = t[5] * b[0] + t[1] * b[1] + t[3] * b[2]
    push_z = t[4] * b[0] + t[3] * b[1] + t[2] * b[2]
    out[0:1, :] = push_y * v[2] - push_z * v[1]
    out[1:2, :] = push_z * v[0] - push_x * v[2]
    out[2:3, :] = push_x * v[1] - push_y * v[0]


def scratch_plan():
    half = pltpu.VMEM((2, 2, 256, 256), BF16)
    sem = pltpu.SemaphoreType.DMA
    plan = {
        "inside": pltpu.SemaphoreType.REGULAR,
        "dist": pltpu.VMEM((9, NX, NY, GRID), F32),
        "ids": pltpu.VMEM((NX, NY, GRID), jnp.int32),
        "load_sem": sem((2, 4)),
        "polar": pltpu.VMEM((6, NX, NY, GRID), F32),
        "moduli": pltpu.VMEM((2, NX, NY, GRID), F32),
        "tz": half,
        "ty": half,
        "tx": half,
        "txi": half,
        "tyi": half,
        "tzi": pltpu.VMEM((2, 256, 512), BF16),
        "table_sem": sem((6,)),
        "ox": pltpu.VMEM((2, 3, NY, GRID), F32),
        "oy": pltpu.VMEM((2, 3, NX, GRID), F32),
        "fx": pltpu.VMEM((2, 3, NY, GRID), F32),
        "fy": pltpu.VMEM((2, 3, NX, GRID), F32),
        "face_sem": sem((3, 2, 4)),
        "hx": pltpu.VMEM((2, 3, NY, GRID), F32),
        "hy": pltpu.VMEM((2, 3, NX, GRID), F32),
        "yface": pltpu.VMEM((2, 3, NX, GRID), F32),
        "back_sem": sem((3, 2, 4)),
        "base": pltpu.VMEM((3, 256, 512), F32),
        "force": pltpu.VMEM((2, 512, 256), BF16),
        "yrows": pltpu.VMEM((2, 512, 128), F32),
        "xrows": half,
        "waves": pltpu.VMEM((2, 3, 256, 256), F32),
        "solved": pltpu.VMEM((2, 2, 3, 256, 256), BF16),
        "lines": pltpu.VMEM((2, 512, 256), BF16),
        "disp": pltpu.VMEM((3, NX, NY, GRID), F32),
        "grad": pltpu.VMEM((3, NX, NY, GRID), F32),
        "stress": pltpu.VMEM((6, NX, NY, GRID), F32),
        "store_sem": sem((1,)),
        "rows": pltpu.VMEM((2, 512, 1536), BF16),
        "asked": pltpu.VMEM((128, 128), jnp.int32),
        "pick": pltpu.VMEM((1024, 512), BF16),
        "gain": pltpu.VMEM((1024, 256), F32),
        "slot": pltpu.VMEM((1, 512), F32),
        "reply": pltpu.VMEM((128, 128), F32),
        "match": pltpu.VMEM((128, 512), BF16),
        "mine": pltpu.VMEM((128, 512), F32),
    }
    exchanges = {
        "exa": ("py", 1, (NPX, 128), jnp.int32),
        "exb": ("px", 1, (NPY, 128), jnp.int32),
        "exc": ("px", 1, (NPY, 128), F32),
        "exd": ("py", 1, (NPX, 128), F32),
    }
    return plan, exchanges


class Names:
    pass


def whole_body(*refs):
    plan, exchanges = scratch_plan()
    n_in, n_out = 18, 2
    (
        moduli_in, source, tile, centre, burgers, line, sx, sy, sz, weights,
        dist_h, ids_h, tz_h, ty_h, tx_h, txi_h, tyi_h, tzi_h,
    ) = refs[:n_in]
    stress_h, seg_force = refs[n_in : n_in + n_out]
    rest = list(refs[n_in + n_out :])
    r = Names()
    for name in plan:
        setattr(r, name, rest.pop(0))
    for name, (axis, _, _, _) in exchanges.items():
        setattr(r, name, Exchange(axis, rest.pop(0), rest.pop(0), rest.pop(0), rest.pop(0)))

    r.there = Turn(rest.pop(0), rest.pop(0), rest.pop(0), rest.pop(0))
    r.back = Turn(rest.pop(0), rest.pop(0), rest.pop(0), rest.pop(0))

    px, py = lax.axis_index("px"), lax.axis_index("py")
    loads = []
    for g in range(4):
        here = pl.ds(g * 4, 4)
        loads.append(
            (
                pltpu.make_async_copy(dist_h.at[:, here], r.dist.at[:, here], r.load_sem.at[0, g]),
                pltpu.make_async_copy(ids_h.at[here], r.ids.at[here], r.load_sem.at[1, g]),
            )
        )
        for load in loads[-1]:
            load.start()
    pairs = ((tz_h, r.tz), (ty_h, r.ty), (tx_h, r.tx), (txi_h, r.txi), (tyi_h, r.tyi), (tzi_h, r.tzi))
    tables = [pltpu.make_async_copy(a, b, r.table_sem.at[i]) for i, (a, b) in enumerate(pairs)]
    for table in tables:
        table.start()
    greet(px, py)

    slot = request_part(source, tile, centre, r.asked)
    r.slot[...] = slot
    for p in range(NPY):
        r.exa.wire[0, p] = r.asked[p * NPX : p * NPX + NPX, :]
    lookup = table_of(moduli_in)
    for g in range(4):
        for load in loads[g]:
            load.wait()
        polar_part(g * 4, 4, r.dist, r.ids, lookup, r.polar, r.moduli)
    for side in range(2):
        for k, comp in enumerate((0, 5, 4)):
            r.ox[side, k] = r.polar[comp, side * (NX - 1)]
        for k, comp in enumerate((5, 1, 3)):
            r.oy[side, k] = r.polar[comp, :, side * (NY - 1), :]

    left, right = lax.rem(px + NPX - 1, NPX), lax.rem(px + 1, NPX)
    down, up = lax.rem(py + NPY - 1, NPY), lax.rem(py + 1, NPY)
    sides = [(left, py), (right, py), (px, down), (px, up)]

    def face(src, dst, sems, to, k):
        return send(src, dst, (sems.at[0, k], sems.at[1, k]), sides[to])

    halo = []
    for c in range(3):
        sems = r.face_sem.at[c]
        halo += [
            face(r.ox.at[0, c], r.fx.at[1, c], sems, 0, 1),
            face(r.ox.at[1, c], r.fx.at[0, c], sems, 1, 0),
            face(r.oy.at[0, c], r.fy.at[1, c], sems, 2, 3),
            face(r.oy.at[1, c], r.fy.at[0, c], sems, 3, 2),
        ]
    pl.semaphore_wait(pltpu.get_barrier_semaphore(), NPX + NPY - 2)
    for copy in halo:
        copy.start()
    greet_on(r.inside, px, py)
    r.exa.start(0)
    tables[0].wait()

    def local(c, carry):
        forward_z_local(c, r.polar, r.tz, r.base, r.force)
        return carry

    lax.fori_loop(0, 3, local, 0)
    for c in range(3):
        for copy in halo[4 * c : 4 * c + 4]:
            copy.wait_recv()
        forward_z(c, r.polar, (r.fx, r.fy), r.tz, r.base, r.there.wire, r.force)
        if c == 0:
            pl.semaphore_wait(r.inside, NPX - 1)
        r.there.start(c)
    r.exa.arrive(0)
    r.asked[...] = r.exa.got[0].reshape(128, 128)
    for p in range(NPX):
        r.exb.wire[0, p] = r.asked[pl.ds(p, NPY, stride=NPX), :]
    r.exb.start(0)
    owners = lax.broadcasted_iota(jnp.int32, (128, 512), 0)
    r.match[...] = (owners == row_of(source[...])).astype(F32).astype(BF16)
    r.mine[...] = jnp.where((owners % 8).astype(F32) == r.slot[...], 1.0, 0.0)
    tables[1].wait()
    tables[2].wait()

    def step_plane(c, carry):
        r.there.arrive(c)
        forward_plane(c, r.there.got, r.ty, r.tx, r.waves, r.yrows, r.xrows)
        return carry

    lax.fori_loop(0, 3, step_plane, 0)
    solve(r.waves, r.solved, sx, sy, sz, px * NPY + py)
    tables[3].wait()
    tables[4].wait()

    def step_back(c, carry):
        inverse_plane(c, r.solved, r.txi, r.tyi, r.back.wire, r.yrows)
        r.back.start(c)
        return carry

    lax.fori_loop(0, 3, step_back, 0)
    tables[5].wait()
    r.exb.arrive(0)
    for p in range(NPX):
        r.asked[p * NPY : p * NPY + NPY, :] = r.exb.got[0, p]
    pick_part(r.asked, weights, r.pick, r.gain)

    def faces_back(c):
        sems = r.back_sem.at[c]
        return [
            face(r.disp.at[c, 0], r.hx.at[1, c], sems, 0, 1),
            face(r.disp.at[c, NX - 1], r.hx.at[0, c], sems, 1, 0),
            face(r.yface.at[0, c], r.hy.at[1, c], sems, 2, 3),
            face(r.yface.at[1, c], r.hy.at[0, c], sems, 3, 2),
        ]

    backs = []
    for c in range(3):
        r.back.arrive(c)
        inverse_z(c, r.back.got, r.tzi, r.disp, r.yface, r.lines)
        backs += faces_back(c)
        for copy in backs[4 * c :]:
            copy.start()
        inverse_z_grad(c, r.tzi, r.grad, r.lines)

    def stress(late):
        for first, count in ((0, 1), (1, NX - 2), (NX - 1, 1)):
            stress_part(
                first, count, late, r.disp, r.grad, r.hx, r.hy, r.polar, r.moduli, r.stress, r.rows
            )

    for copy in backs[:8]:
        copy.wait_recv()
    stress(False)
    reply = reply_part((0, 1, 2, 5), r.pick, r.gain, r.rows, jnp.zeros((128, 128), F32))
    for copy in backs[8:]:
        copy.wait_recv()
    stress(True)
    store = pltpu.make_async_copy(r.stress, stress_h, r.store_sem.at[0])
    store.start()
    r.reply[...] = reply_part((3, 4), r.pick, r.gain, r.rows, reply)
    for p in range(NPX):
        r.exc.wire[0, p] = r.reply[p * NPY : p * NPY + NPY, :]
    r.exc.start(0)
    for copy in halo + backs:
        copy.wait_send()
    for c in range(3):
        r.there.finish(c)
        r.back.finish(c)
    r.exa.finish(0)
    r.exb.finish(0)
    r.exc.arrive(0)
    r.reply[...] = r.exc.got[0].reshape(128, 128)
    for p in range(NPY):
        r.exd.wire[0, p] = r.reply[pl.ds(p, NPX, stride=NPY), :]
    r.exd.start(0)
    store.wait()
    r.exd.arrive(0)
    force_part(r.exd.got[0].reshape(128, 128), r.match, r.mine, burgers, line, seg_force)
    r.exc.finish(0)
    r.exd.finish(0)


def finish_body(stress_in, force_in, stress_out, force_out, buffer, sems):
    count = 8
    width = NX // count
    spans = [pl.ds(i * width, width) for i in range(count)]
    loads = [
        pltpu.make_async_copy(stress_in.at[:, s], buffer.at[:, s], sems.at[0, i]) for i, s in enumerate(spans)
    ]
    stores = [
        pltpu.make_async_copy(buffer.at[:, s], stress_out.at[:, s], sems.at[1, i]) for i, s in enumerate(spans)
    ]
    for load in loads:
        load.start()
    force_out[...] = force_in[...]
    for load, store in zip(loads, stores):
        load.wait()
        store.start()
    for store in stores:
        store.wait()


def shards(dist, ids, moduli, seg_source, seg_tile, seg_center, burgers, line_vector):
    fwd_z, inv_z = z_tables()
    fwd_h, inv_h = half_tables()
    order = x_order()
    tz, tzi = two_parts(fwd_z), two_parts(inv_z)
    tx, txi = two_parts(fwd_h[:, :, order]), two_parts(inv_h[:, order, :])
    ty = two_parts(fwd_h.transpose(0, 2, 1))
    tyi = two_parts(inv_h.transpose(0, 2, 1))
    sx, sy, sz = wave_lines()
    weights = two_parts(tile_weights())
    plan, exchanges = scratch_plan()
    scratch = list(plan.values())
    for axis, parts, block, dtype in exchanges.values():
        scratch += exchange_scratch(axis, parts, block, dtype)
    scratch += turn_scratch() + turn_scratch()
    hbm = pl.BlockSpec(memory_space=pl.ANY)
    stress, seg_force = (
        pl.pallas_call(
            whole_body,
            out_shape=(sds((6, NX, NY, GRID)), sds((3, 512))),
            in_specs=[VM] * 10 + [hbm] * 8,
            out_specs=(hbm, VM),
            scratch_shapes=scratch,
            compiler_params=pltpu.CompilerParams(
                vmem_limit_bytes=VMEM_LIMIT, collective_id=0, has_side_effects=True
            ),
        )(
            moduli,
            seg_source.reshape(1, 512),
            seg_tile.reshape(1, 512),
            seg_center.reshape(1, 512),
            burgers,
            line_vector,
            sx,
            sy,
            sz,
            weights,
            dist,
            ids,
            tz,
            ty,
            tx,
            txi,
            tyi,
            tzi,
        )
    )
    return tuple(
        pl.pallas_call(
            finish_body,
            out_shape=(sds((6, NX, NY, GRID)), sds((3, 512))),
            in_specs=[hbm, VM],
            out_specs=(hbm, VM),
            scratch_shapes=[
                pltpu.VMEM((6, NX, NY, GRID), F32),
                pltpu.SemaphoreType.DMA((2, 8)),
            ],
            compiler_params=pltpu.CompilerParams(vmem_limit_bytes=VMEM_LIMIT),
        )(stress, seg_force)
    )


def solution(mesh):
    return jax.shard_map(
        shards,
        mesh=mesh,
        in_specs=(
            P(None, "px", "py", None),
            P("px", "py", None),
            P(),
            P(("px", "py"), None),
            P(("px", "py")),
            P(("px", "py")),
            P(None, ("px", "py")),
            P(None, ("px", "py")),
        ),
        out_specs=(P(None, "px", "py", None), P(None, ("px", "py"))),
        check_vma=False,
    )
```

```python
import functools

import jax
import jax.numpy as jnp
import ml_dtypes
import numpy as np
from jax import lax
from jax.experimental import pallas as pl
from jax.experimental.pallas import tpu as pltpu
from jax.sharding import PartitionSpec as P

F32 = jnp.float32
BF16 = jnp.bfloat16
REF_LAMBDA = 1.25
REF_SHEAR = 1.25
GRID = 256
HALF = 128
NPX = 16
NPY = 8
DEVICES = NPX * NPY
NX = 16
NY = 32
VMEM_LIMIT = 60 * 1024 * 1024
VM = pl.BlockSpec(memory_space=pltpu.VMEM)


def two_parts(table):
    table = np.asarray(table, np.float32)
    high = table.astype(ml_dtypes.bfloat16)
    low = (table - high.astype(np.float32)).astype(ml_dtypes.bfloat16)
    return np.stack([high, low])


def z_tables():
    z = np.arange(GRID)
    fwd = np.zeros((GRID, GRID))
    inv = np.zeros((GRID, GRID))
    for row in range(GRID):
        wave, ri = row // 2, row % 2
        angle = 2 * np.pi * ((wave * z) % GRID) / GRID
        if wave == 0:
            line = np.ones(GRID) if ri == 0 else 1.0 - 2.0 * (z % 2)
            fwd[row], inv[row] = line, line / GRID
        else:
            line = np.cos(angle) if ri == 0 else -np.sin(angle)
            fwd[row], inv[row] = line, 2 * line / GRID
    step = np.roll(np.eye(GRID), 1, 1) - np.roll(np.eye(GRID), -1, 1)
    fwd = 0.5 * np.stack([fwd, fwd @ step])
    inv = np.concatenate([inv, inv @ step.T], axis=1)
    return fwd, inv


def half_tables():
    k = np.arange(HALF)
    fwd, inv = [], []
    for e in range(2):
        angle = 2 * np.pi * (((2 * k[:, None] + e) * k[None, :]) % GRID) / GRID
        cos, sin = np.cos(angle), np.sin(angle)
        fwd.append(np.block([[cos, sin], [-sin, cos]]))
        inv.append(np.block([[cos.T, -sin.T], [sin.T, cos.T]]) / GRID)
    return np.stack(fwd), np.stack(inv)


def x_order():
    index = np.arange(HALF).reshape(8, 4, 4)
    order = index.transpose(1, 0, 2).reshape(-1)
    return np.concatenate([order, order + HALF])


def sines():
    wave = np.arange(GRID)
    line = np.sin(2 * np.pi * wave / GRID)
    line[wave % HALF == 0] = 0.0
    return line


def wave_lines():
    line = sines()
    sx = np.stack([line[0::2], line[1::2]])[:, :, None] * np.ones((1, 1, 128))
    sy = np.concatenate([line[0::2], line[1::2]])[None, :]
    sz = line[:128, None] * np.ones((1, 128))
    return sx.astype(np.float32), sy.astype(np.float32), sz.astype(np.float32)


def tile_weights():
    v = np.arange(128, dtype=np.float64)
    weights = np.exp(-((v[None, :] - v[:, None]) ** 2) / (2.0 * 16.0**2))
    return weights / weights.sum(axis=1, keepdims=True)


def split(values):
    high = values.astype(BF16)
    low = (values - high.astype(F32)).astype(BF16)
    return high, low


def dot(a, b, dims=((1,), (0,))):
    return lax.dot_general(a, b, (dims, ((), ())), preferred_element_type=F32)


def dot3(a, b, dims=((1,), (0,))):
    (ah, al), (bh, bl) = a, b
    return dot(ah, bh, dims) + (dot(ah, bl, dims) + dot(al, bh, dims))


def swap_groups(values):
    count = len(values)
    width = 128 // count
    lane = lax.broadcasted_iota(jnp.int32, values[0].shape, values[0].ndim - 1)
    axis = values[0].ndim - 1
    values = list(values)
    step = 1
    while step < count:
        first = ((lane // (width * step)) % 2) == 0
        out = list(values)
        for i in range(count):
            if i & step == 0:
                low, high = values[i], values[i + step]
                out[i] = jnp.where(first, low, pltpu.roll(high, width * step, axis))
                out[i + step] = jnp.where(first, pltpu.roll(low, 128 - width * step, axis), high)
        values = out
        step *= 2
    return values


def send(src, dst, sems, where):
    return pltpu.make_async_remote_copy(
        src_ref=src,
        dst_ref=dst,
        send_sem=sems[0],
        recv_sem=sems[1],
        device_id=where,
        device_id_type=pl.DeviceIdType.MESH,
    )


def hops(mask):
    return sum((0, 1, 2, 1)[(mask >> shift) % 4] for shift in (1, 3, 5))


def peers(px, py):
    me = px * NPY + py
    masks = sorted([(53 * k) % DEVICES for k in range(1, DEVICES)], key=lambda mask: -hops(mask))
    return [jnp.bitwise_xor(me, mask) for mask in masks]


def place(device):
    return (device // NPY, lax.rem(device, NPY))


def greet(px, py):
    barrier = pltpu.get_barrier_semaphore()
    for d in range(1, NPY):
        where = (px, lax.rem(py + d, NPY))
        pl.semaphore_signal(barrier, inc=1, device_id=where, device_id_type=pl.DeviceIdType.MESH)
    for d in range(1, NPX):
        where = (lax.rem(px + d, NPX), py)
        pl.semaphore_signal(barrier, inc=1, device_id=where, device_id_type=pl.DeviceIdType.MESH)


def greet_on(inside, px, py):
    for d in range(1, NPX):
        where = (lax.rem(px + d, NPX), py)
        pl.semaphore_signal(inside, inc=1, device_id=where, device_id_type=pl.DeviceIdType.MESH)


class Turn:
    def __init__(self, wire, got, sems, own_sem):
        self.wire, self.got, self.sems, self.own_sem = wire, got, sems, own_sem
        self.px, self.py = lax.axis_index("px"), lax.axis_index("py")
        self.me = self.px * NPY + self.py

    def rows(self, ref, part, device):
        return ref.at[part, pl.ds(pl.multiple_of(device * 8, 8), 8)]

    def own(self, part):
        return pltpu.make_async_copy(
            self.rows(self.wire, part, self.me), self.rows(self.got, part, self.me), self.own_sem.at[part]
        )

    def start(self, part):
        sems = (self.sems.at[0, part], self.sems.at[1, part])
        for peer in peers(self.px, self.py):
            send(
                self.rows(self.wire, part, peer), self.rows(self.got, part, self.me), sems, place(peer)
            ).start()
        self.own(part).start()

    def all(self, side, part):
        block = self.got.at[part, pl.ds(0, 8 * DEVICES - 8)]
        return pltpu.make_async_copy(block, block, self.sems.at[side, part])

    def arrive(self, part):
        self.own(part).wait()
        self.all(1, part).wait()

    def finish(self, part):
        self.all(0, part).wait()


def turn_scratch():
    return [
        pltpu.VMEM((3, 8 * DEVICES, 128), F32),
        pltpu.VMEM((3, 8 * DEVICES, 128), F32),
        pltpu.SemaphoreType.DMA((2, 3)),
        pltpu.SemaphoreType.DMA((3,)),
    ]


class Exchange:
    def __init__(self, axis, wire, got, sems, own_sem):
        self.count = NPX if axis == "px" else NPY
        self.axis, self.wire, self.got, self.sems, self.own_sem = axis, wire, got, sems, own_sem
        self.px, self.py = lax.axis_index("px"), lax.axis_index("py")
        self.me = self.px if axis == "px" else self.py

    def own(self, part):
        return pltpu.make_async_copy(
            self.wire.at[part, self.me], self.got.at[part, self.me], self.own_sem.at[part]
        )

    def start(self, part):
        for d in range(1, self.count):
            peer = lax.rem(self.me + d, self.count)
            where = (peer, self.py) if self.axis == "px" else (self.px, peer)
            sems = (self.sems.at[0, part], self.sems.at[1, part])
            send(self.wire.at[part, peer], self.got.at[part, self.me], sems, where).start()
        self.own(part).start()

    def all(self, side, part):
        block = self.got.at[part, pl.ds(0, self.count - 1)]
        return pltpu.make_async_copy(block, block, self.sems.at[side, part])

    def arrive(self, part):
        self.own(part).wait()
        self.all(1, part).wait()

    def finish(self, part):
        self.all(0, part).wait()


def exchange_scratch(axis, parts, block, dtype=F32):
    count = NPX if axis == "px" else NPY
    return [
        pltpu.VMEM((parts, count) + block, dtype),
        pltpu.VMEM((parts, count) + block, dtype),
        pltpu.SemaphoreType.DMA((2, parts)),
        pltpu.SemaphoreType.DMA((parts,)),
    ]


def sds(shape, dtype=F32):
    return jax.ShapeDtypeStruct(shape, dtype)


def moduli_of(table, ids):
    lame, shear = [], []
    for half in range(2):
        index = ids[:, half * 128 : (half + 1) * 128]
        lame.append(jnp.take_along_axis(table, index, axis=1))
        shear.append(jnp.take_along_axis(table, index + 64, axis=1))
    return jnp.concatenate(lame, axis=1), jnp.concatenate(shear, axis=1)


def table_of(moduli_ref):
    row = jnp.concatenate([moduli_ref[0:1, :], moduli_ref[1:2, :]], axis=1)
    return jnp.broadcast_to(row, (NY, 128))


def polar_part(first, count, dist, ids, table, polar, moduli):
    def at_x(x, carry):
        lame, shear = moduli_of(table, ids[x])
        moduli[0, x] = lame
        moduli[1, x] = shear
        exx, eyy, ezz = dist[0, x], dist[4, x], dist[8, x]
        trace = lame * (exx + eyy + ezz)
        twice = shear + shear
        polar[0, x] = -(twice * exx + trace)
        polar[1, x] = -(twice * eyy + trace)
        polar[2, x] = -(twice * ezz + trace)
        polar[3, x] = -(shear * (dist[5, x] + dist[7, x]))
        polar[4, x] = -(shear * (dist[2, x] + dist[6, x]))
        polar[5, x] = -(shear * (dist[1, x] + dist[3, x]))
        return carry

    lax.fori_loop(first, first + count, at_x, 0)


def row_of(device):
    return (device % NPY) * NPX + device // NPY


def request_part(source, tile, centre, asked):
    src_lane = row_of(source[...]).astype(F32)
    src = jnp.transpose(jnp.broadcast_to(src_lane, (128, 512)))
    same = src[:, 0:1] == src_lane
    first = lax.broadcasted_iota(jnp.int32, (512, 512), 0)
    second = lax.broadcasted_iota(jnp.int32, (512, 512), 1)
    slot_lane = jnp.sum(jnp.where(same & (first < second), 1.0, 0.0), axis=0, keepdims=True)
    match = (src == lax.broadcasted_iota(jnp.int32, (512, 128), 1).astype(F32)).astype(F32).astype(BF16)
    row = lax.broadcasted_iota(jnp.int32, (8, 512), 0).astype(F32)
    here = row == slot_lane
    tile_v = tile[...]
    values = [tile_v // 8, tile_v % 8, centre[...]]
    rows = [jnp.where(here, v.astype(F32), 0.0) for v in values]
    stacked = jnp.concatenate(rows + [jnp.zeros((8, 512), F32)], axis=0).astype(BF16)
    got = dot(stacked, match)
    both = jnp.concatenate([got[0:8] * 8.0 + got[8:16], got[16:24], jnp.zeros((112, 128), F32)], axis=0)
    asked[...] = jnp.transpose(both).astype(jnp.int32)
    return slot_lane


def shift_y(values, before, after):
    row = lax.broadcasted_iota(jnp.int32, values.shape, 0)
    up = jnp.where(row == NY - 1, after, pltpu.roll(values, NY - 1, 0))
    down = jnp.where(row == 0, before, pltpu.roll(values, 1, 0))
    return up - down


LAST = ((1,), (1,))


def forward_z_local(c, polar, tz, waves, force):
    for x in range(NX):
        hi, lo = split(polar[4 - c, x])
        force[0, x * NY : (x + 1) * NY, :] = hi
        force[1, x * NY : (x + 1) * NY, :] = lo
    waves[c] = dot3((tz[0, 1], tz[1, 1]), (force[0], force[1]), LAST)


def forward_z(c, polar, faces, tz, base, wire, force):
    cx = (6 - c) * ((c + 1) // 2)
    cy = 5 - c - 3 * lax.rem(c, 2)
    fx, fy = faces
    for x in range(NX):
        after = fx[1, c] if x == NX - 1 else polar[cx, x + 1]
        before = fx[0, c] if x == 0 else polar[cx, x - 1]
        grad_y = shift_y(polar[cy, x], fy[0, c, x : x + 1, :], fy[1, c, x : x + 1, :])
        hi, lo = split((after - before) + grad_y)
        force[0, x * NY : (x + 1) * NY, :] = hi
        force[1, x * NY : (x + 1) * NY, :] = lo
    waves = base[c] + dot3((tz[0, 0], tz[1, 0]), (force[0], force[1]), LAST)
    for t in range(32):
        for xg in range(4):
            wire[c, pl.ds(32 * t + xg, 8, stride=4), :] = waves[
                8 * t : 8 * t + 8, xg * 128 : xg * 128 + 128
            ]


def forward_plane(c, got, ty, tx, waves, yrows, xrows):
    for q in range(NPX):
        row = q * 64
        low = swap_groups([got[c, row + p * 8 : row + p * 8 + 8, :] for p in range(4)])
        high = swap_groups([got[c, row + p * 8 : row + p * 8 + 8, :] for p in range(4, 8)])
        for x4 in range(4):
            to = pl.ds(q * 4 + x4, 8, stride=64)
            yrows[0, to, :] = low[x4] + high[x4]
            yrows[1, to, :] = low[x4] - high[x4]
    for e in range(2):
        rows = jnp.concatenate([yrows[e, :256, :], yrows[e, 256:, :]], axis=1)
        out = dot3(split(rows), (ty[0, e], ty[1, e]))
        for xg in range(4):
            a, b = out[xg * 64 : xg * 64 + 32, :], out[xg * 64 + 32 : xg * 64 + 64, :]
            for ex in range(2):
                hi, lo = split(a + b if ex == 0 else a - b)
                for ri in range(2):
                    to = slice(ri * 128 + xg * 32, ri * 128 + xg * 32 + 32)
                    xrows[0, ex, to, e * 128 : e * 128 + 128] = hi[:, ri * 128 : ri * 128 + 128]
                    xrows[1, ex, to, e * 128 : e * 128 + 128] = lo[:, ri * 128 : ri * 128 + 128]
    for ex in range(2):
        waves[ex, c] = dot3((tx[0, ex], tx[1, ex]), (xrows[0, ex], xrows[1, ex]))


def solve(waves, solved, sx, sy, sz, kz):
    sy = sy[...]
    sz = sz[pl.ds(kz, 1), :]
    sz = jnp.concatenate([sz, sz], axis=1)
    coupling = (REF_LAMBDA + REF_SHEAR) / (REF_LAMBDA + 2.0 * REF_SHEAR)
    rest = sy * sy + sz * sz
    for ex in range(2):
        wx = jnp.concatenate([sx[ex], sx[ex]], axis=1)
        squared = wx * wx + rest
        null = squared == 0.0
        inverse = jnp.where(null, 0.0, 1.0 / jnp.where(null, 1.0, squared))
        scale = inverse * (1.0 / REF_SHEAR)
        for ri in range(2):
            parts = [waves[ex, c, ri * 128 : ri * 128 + 128, :] for c in range(3)]
            common = coupling * inverse * (wx * parts[0] + sy * parts[1] + sz * parts[2])
            for c, line in enumerate((wx, sy, sz)):
                hi, lo = split(scale * (parts[c] - common * line))
                solved[0, ex, c, ri * 128 : ri * 128 + 128, :] = hi
                solved[1, ex, c, ri * 128 : ri * 128 + 128, :] = lo


def inverse_plane(c, solved, txi, tyi, wire, yrows):
    backs = [dot3((txi[0, ex], txi[1, ex]), (solved[0, ex, c], solved[1, ex, c])) for ex in range(2)]
    halves = (backs[0] + backs[1], backs[0] - backs[1])
    outs = []
    for e in range(2):
        lane = slice(e * 128, e * 128 + 128)
        sides = []
        for ri in range(2):
            blocks = []
            for xg in range(4):
                row = ri * 128 + xg * 32
                blocks += [halves[0][row : row + 32, lane], halves[1][row : row + 32, lane]]
            sides.append(jnp.concatenate(blocks, axis=0))
        outs.append(dot3(split(jnp.concatenate(sides, axis=1)), (tyi[0, e], tyi[1, e])))
    for half, out in enumerate((outs[0] + outs[1], outs[0] - outs[1])):
        yrows[half, :256, :] = out[:, :128]
        yrows[half, 256:, :] = out[:, 128:]
    for q in range(NPX):
        for half in range(2):
            tiles = [yrows[half, pl.ds(q * 4 + x4, 8, stride=64), :] for x4 in range(4)]
            for p, tile in enumerate(swap_groups(tiles)):
                row = q * 64 + half * 32 + p * 8
                wire[c, row : row + 8, :] = tile


def inverse_z(c, got, tzi, disp, yface, lines):
    for xg in range(4):
        turned = jnp.transpose(got[c, pl.ds(xg, 256, stride=4), :])
        hi, lo = split(turned)
        lines[0, xg * 128 : xg * 128 + 128, :] = hi
        lines[1, xg * 128 : xg * 128 + 128, :] = lo
    out = dot3((lines[0], lines[1]), (tzi[0, :, :256], tzi[1, :, :256]))
    for x in range(NX):
        disp[c, x] = out[x * NY : (x + 1) * NY, :]
        yface[0, c, x : x + 1] = out[x * NY : x * NY + 1, :]
        yface[1, c, x : x + 1] = out[x * NY + NY - 1 : x * NY + NY, :]


def inverse_z_grad(c, tzi, grad, lines):
    out = dot3((lines[0], lines[1]), (tzi[0, :, 256:], tzi[1, :, 256:]))
    for x in range(NX):
        grad[c, x] = out[x * NY : (x + 1) * NY, :]


def stress_part(first, count, late, disp, grad, hx, hy, polar, moduli, stress, rows):
    def at_x(x, carry):
        shear = moduli[1, x]
        row = pl.ds(pl.multiple_of(x * NY, NY), NY)

        def grad_x(c):
            after = hx[1, c] if first == NX - 1 else disp[c, x + 1]
            before = hx[0, c] if first == 0 else disp[c, x - 1]
            return after - before

        def grad_y(c):
            return shift_y(disp[c, x], hy[0, c, pl.ds(x, 1), :], hy[1, c, pl.ds(x, 1), :])

        half = 0.5 * shear
        if late:
            parts = {3: half * (grad[1, x] + grad_y(2)), 4: half * (grad[0, x] + grad_x(2))}
        else:
            exx, eyy, ezz = grad_x(0), grad_y(1), grad[2, x]
            trace = (0.5 * moduli[0, x]) * (exx + eyy + ezz)
            parts = {
                0: shear * exx + trace,
                1: shear * eyy + trace,
                2: shear * ezz + trace,
                5: half * (grad_y(0) + grad_x(1)),
            }
        for c, part in parts.items():
            total = part + polar[c, x]
            stress[c, x] = total
            hi, lo = split(total)
            rows[0, row, c * 256 : c * 256 + 256] = hi
            rows[1, row, c * 256 : c * 256 + 256] = lo
        return carry

    lax.fori_loop(first, first + count, at_x, 0)


def pick_part(asked, weights, pick, gain):
    column = lax.broadcasted_iota(jnp.int32, (128, 512), 1)
    lane = lax.broadcasted_iota(jnp.int32, (128, 128), 1)
    lane256 = lax.broadcasted_iota(jnp.int32, (128, 256), 1)
    for k in range(8):
        here = slice(k * 128, k * 128 + 128)
        tile = asked[:, k : k + 1]
        centre = asked[:, 8 + k : 9 + k]
        pick[here, :] = (column == tile // 2).astype(F32).astype(BF16)
        at = (lane == centre).astype(F32).astype(BF16)
        row = dot(at, weights[0]) + dot(at, weights[1])
        row = jnp.concatenate([row, row], axis=1)
        gain[here, :] = jnp.where(lane256 // 128 == tile % 2, row, 0.0)


def reply_part(comps, pick, gain, rows, out):
    lane = lax.broadcasted_iota(jnp.int32, (128, 128), 1)
    for c in comps:
        here = slice(c * 256, c * 256 + 256)
        picked = dot(pick[...], rows[0, :, here]) + dot(pick[...], rows[1, :, here])
        picked = picked * gain[...]
        total = jnp.sum(picked[:, :128] + picked[:, 128:], axis=1, keepdims=True)
        for k in range(8):
            out = jnp.where(lane == c * 8 + k, total[k * 128 : k * 128 + 128], out)
    return out


def force_part(reply, match, mine, burgers, line, out):
    hi, lo = split(reply)
    low = (reply - hi.astype(F32) - lo.astype(F32)).astype(BF16)
    first = ((0,), (0,))
    match = match[...]
    got = dot(hi, match, first) + (dot(lo, match, first) + dot(low, match, first))
    mine = got * mine[...]
    t = [jnp.sum(mine[c * 8 : c * 8 + 8, :], axis=0, keepdims=True) for c in range(6)]
    b = [burgers[i : i + 1, :] for i in range(3)]
    v = [line[i : i + 1, :] for i in range(3)]
    push_x = t[0] * b[0] + t[5] * b[1] + t[4] * b[2]
    push_y = t[5] * b[0] + t[1] * b[1] + t[3] * b[2]
    push_z = t[4] * b[0] + t[3] * b[1] + t[2] * b[2]
    out[0:1, :] = push_y * v[2] - push_z * v[1]
    out[1:2, :] = push_z * v[0] - push_x * v[2]
    out[2:3, :] = push_x * v[1] - push_y * v[0]


def scratch_plan():
    half = pltpu.VMEM((2, 2, 256, 256), BF16)
    sem = pltpu.SemaphoreType.DMA
    plan = {
        "inside": pltpu.SemaphoreType.REGULAR,
        "dist": pltpu.VMEM((9, NX, NY, GRID), F32),
        "ids": pltpu.VMEM((NX, NY, GRID), jnp.int32),
        "load_sem": sem((2, 4)),
        "polar": pltpu.VMEM((6, NX, NY, GRID), F32),
        "moduli": pltpu.VMEM((2, NX, NY, GRID), F32),
        "tz": half,
        "ty": half,
        "tx": half,
        "txi": half,
        "tyi": half,
        "tzi": pltpu.VMEM((2, 256, 512), BF16),
        "table_sem": sem((9,)),
        "sx": pltpu.VMEM((2, 128, 128), F32),
        "sz": pltpu.VMEM((128, 128), F32),
        "weights": pltpu.VMEM((2, 128, 128), BF16),
        "ox": pltpu.VMEM((2, 3, NY, GRID), F32),
        "oy": pltpu.VMEM((2, 3, NX, GRID), F32),
        "fx": pltpu.VMEM((2, 3, NY, GRID), F32),
        "fy": pltpu.VMEM((2, 3, NX, GRID), F32),
        "face_sem": sem((3, 2, 4)),
        "hx": pltpu.VMEM((2, 3, NY, GRID), F32),
        "hy": pltpu.VMEM((2, 3, NX, GRID), F32),
        "yface": pltpu.VMEM((2, 3, NX, GRID), F32),
        "back_sem": sem((3, 2, 4)),
        "base": pltpu.VMEM((3, 256, 512), F32),
        "force": pltpu.VMEM((2, 512, 256), BF16),
        "yrows": pltpu.VMEM((2, 512, 128), F32),
        "xrows": half,
        "waves": pltpu.VMEM((2, 3, 256, 256), F32),
        "solved": pltpu.VMEM((2, 2, 3, 256, 256), BF16),
        "lines": pltpu.VMEM((2, 512, 256), BF16),
        "disp": pltpu.VMEM((3, NX, NY, GRID), F32),
        "grad": pltpu.VMEM((3, NX, NY, GRID), F32),
        "stress": pltpu.VMEM((6, NX, NY, GRID), F32),
        "store_sem": sem((1,)),
        "rows": pltpu.VMEM((2, 512, 1536), BF16),
        "asked": pltpu.VMEM((128, 128), jnp.int32),
        "pick": pltpu.VMEM((1024, 512), BF16),
        "gain": pltpu.VMEM((1024, 256), F32),
        "slot": pltpu.VMEM((1, 512), F32),
        "reply": pltpu.VMEM((128, 128), F32),
        "match": pltpu.VMEM((128, 512), BF16),
        "mine": pltpu.VMEM((128, 512), F32),
    }
    exchanges = {
        "exa": ("py", 1, (NPX, 128), jnp.int32),
        "exb": ("px", 1, (NPY, 128), jnp.int32),
        "exc": ("px", 1, (NPY, 128), F32),
        "exd": ("py", 1, (NPX, 128), F32),
    }
    return plan, exchanges


class Names:
    pass


def whole_body(*refs):
    plan, exchanges = scratch_plan()
    n_in, n_out = 18, 2
    (
        moduli_in, source, tile, centre, burgers, line, sy,
        sx_h, sz_h, weights_h, dist_h, ids_h, tz_h, ty_h, tx_h, txi_h, tyi_h, tzi_h,
    ) = refs[:n_in]
    stress_h, seg_force = refs[n_in : n_in + n_out]
    rest = list(refs[n_in + n_out :])
    r = Names()
    for name in plan:
        setattr(r, name, rest.pop(0))
    for name, (axis, _, _, _) in exchanges.items():
        setattr(r, name, Exchange(axis, rest.pop(0), rest.pop(0), rest.pop(0), rest.pop(0)))

    r.there = Turn(rest.pop(0), rest.pop(0), rest.pop(0), rest.pop(0))
    r.back = Turn(rest.pop(0), rest.pop(0), rest.pop(0), rest.pop(0))

    px, py = lax.axis_index("px"), lax.axis_index("py")
    loads = []
    for g in range(4):
        here = pl.ds(g * 4, 4)
        loads.append(
            (
                pltpu.make_async_copy(dist_h.at[:, here], r.dist.at[:, here], r.load_sem.at[0, g]),
                pltpu.make_async_copy(ids_h.at[here], r.ids.at[here], r.load_sem.at[1, g]),
            )
        )
        for load in loads[-1]:
            load.start()
    pairs = (
        (tz_h, r.tz), (ty_h, r.ty), (tx_h, r.tx), (txi_h, r.txi), (tyi_h, r.tyi), (tzi_h, r.tzi),
        (sx_h, r.sx), (sz_h, r.sz), (weights_h, r.weights),
    )
    tables = [pltpu.make_async_copy(a, b, r.table_sem.at[i]) for i, (a, b) in enumerate(pairs)]
    tables[0].start()
    greet(px, py)

    slot = request_part(source, tile, centre, r.asked)
    r.slot[...] = slot
    for p in range(NPY):
        r.exa.wire[0, p] = r.asked[p * NPX : p * NPX + NPX, :]
    lookup = table_of(moduli_in)
    for g in range(4):
        for load in loads[g]:
            load.wait()
        polar_part(g * 4, 4, r.dist, r.ids, lookup, r.polar, r.moduli)
    for side in range(2):
        for k, comp in enumerate((0, 5, 4)):
            r.ox[side, k] = r.polar[comp, side * (NX - 1)]
        for k, comp in enumerate((5, 1, 3)):
            r.oy[side, k] = r.polar[comp, :, side * (NY - 1), :]

    left, right = lax.rem(px + NPX - 1, NPX), lax.rem(px + 1, NPX)
    down, up = lax.rem(py + NPY - 1, NPY), lax.rem(py + 1, NPY)
    sides = [(left, py), (right, py), (px, down), (px, up)]

    def face(src, dst, sems, to, k):
        return send(src, dst, (sems.at[0, k], sems.at[1, k]), sides[to])

    halo = []
    for c in range(3):
        sems = r.face_sem.at[c]
        halo += [
            face(r.ox.at[0, c], r.fx.at[1, c], sems, 0, 1),
            face(r.ox.at[1, c], r.fx.at[0, c], sems, 1, 0),
            face(r.oy.at[0, c], r.fy.at[1, c], sems, 2, 3),
            face(r.oy.at[1, c], r.fy.at[0, c], sems, 3, 2),
        ]
    pl.semaphore_wait(pltpu.get_barrier_semaphore(), NPX + NPY - 2)
    for copy in halo:
        copy.start()
    greet_on(r.inside, px, py)
    for table in tables[1:]:
        table.start()
    r.exa.start(0)
    tables[0].wait()

    def local(c, carry):
        forward_z_local(c, r.polar, r.tz, r.base, r.force)
        return carry

    lax.fori_loop(0, 3, local, 0)
    for c in range(3):
        for copy in halo[4 * c : 4 * c + 4]:
            copy.wait_recv()
        forward_z(c, r.polar, (r.fx, r.fy), r.tz, r.base, r.there.wire, r.force)
        if c == 0:
            pl.semaphore_wait(r.inside, NPX - 1)
        r.there.start(c)
    r.exa.arrive(0)
    r.asked[...] = r.exa.got[0].reshape(128, 128)
    for p in range(NPX):
        r.exb.wire[0, p] = r.asked[pl.ds(p, NPY, stride=NPX), :]
    r.exb.start(0)
    owners = lax.broadcasted_iota(jnp.int32, (128, 512), 0)
    r.match[...] = (owners == row_of(source[...])).astype(F32).astype(BF16)
    r.mine[...] = jnp.where((owners % 8).astype(F32) == r.slot[...], 1.0, 0.0)
    tables[1].wait()
    tables[2].wait()

    def step_plane(c, carry):
        r.there.arrive(c)
        forward_plane(c, r.there.got, r.ty, r.tx, r.waves, r.yrows, r.xrows)
        return carry

    lax.fori_loop(0, 3, step_plane, 0)
    for table in tables[6:]:
        table.wait()
    solve(r.waves, r.solved, r.sx, sy, r.sz, px * NPY + py)
    tables[3].wait()
    tables[4].wait()

    def step_back(c, carry):
        inverse_plane(c, r.solved, r.txi, r.tyi, r.back.wire, r.yrows)
        r.back.start(c)
        return carry

    lax.fori_loop(0, 3, step_back, 0)
    tables[5].wait()
    r.exb.arrive(0)
    for p in range(NPX):
        r.asked[p * NPY : p * NPY + NPY, :] = r.exb.got[0, p]
    pick_part(r.asked, r.weights, r.pick, r.gain)

    def faces_back(c):
        sems = r.back_sem.at[c]
        return [
            face(r.disp.at[c, 0], r.hx.at[1, c], sems, 0, 1),
            face(r.disp.at[c, NX - 1], r.hx.at[0, c], sems, 1, 0),
            face(r.yface.at[0, c], r.hy.at[1, c], sems, 2, 3),
            face(r.yface.at[1, c], r.hy.at[0, c], sems, 3, 2),
        ]

    backs = []
    for c in range(3):
        r.back.arrive(c)
        inverse_z(c, r.back.got, r.tzi, r.disp, r.yface, r.lines)
        backs += faces_back(c)
        for copy in backs[4 * c :]:
            copy.start()
        inverse_z_grad(c, r.tzi, r.grad, r.lines)

    def stress(late):
        for first, count in ((0, 1), (1, NX - 2), (NX - 1, 1)):
            stress_part(
                first, count, late, r.disp, r.grad, r.hx, r.hy, r.polar, r.moduli, r.stress, r.rows
            )

    for copy in backs[:8]:
        copy.wait_recv()
    stress(False)
    reply = reply_part((0, 1, 2, 5), r.pick, r.gain, r.rows, jnp.zeros((128, 128), F32))
    for copy in backs[8:]:
        copy.wait_recv()
    stress(True)
    store = pltpu.make_async_copy(r.stress, stress_h, r.store_sem.at[0])
    store.start()
    r.reply[...] = reply_part((3, 4), r.pick, r.gain, r.rows, reply)
    for p in range(NPX):
        r.exc.wire[0, p] = r.reply[p * NPY : p * NPY + NPY, :]
    r.exc.start(0)
    for copy in halo + backs:
        copy.wait_send()
    for c in range(3):
        r.there.finish(c)
        r.back.finish(c)
    r.exa.finish(0)
    r.exb.finish(0)
    r.exc.arrive(0)
    r.reply[...] = r.exc.got[0].reshape(128, 128)
    for p in range(NPY):
        r.exd.wire[0, p] = r.reply[pl.ds(p, NPX, stride=NPY), :]
    r.exd.start(0)
    store.wait()
    r.exd.arrive(0)
    force_part(r.exd.got[0].reshape(128, 128), r.match, r.mine, burgers, line, seg_force)
    r.exc.finish(0)
    r.exd.finish(0)


def finish_body(stress_in, force_in, stress_out, force_out, buffer, sems):
    count = 8
    width = NX // count
    spans = [pl.ds(i * width, width) for i in range(count)]
    loads = [
        pltpu.make_async_copy(stress_in.at[:, s], buffer.at[:, s], sems.at[0, i]) for i, s in enumerate(spans)
    ]
    stores = [
        pltpu.make_async_copy(buffer.at[:, s], stress_out.at[:, s], sems.at[1, i]) for i, s in enumerate(spans)
    ]
    for load in loads:
        load.start()
    force_out[...] = force_in[...]
    for load, store in zip(loads, stores):
        load.wait()
        store.start()
    for store in stores:
        store.wait()


def shards(dist, ids, moduli, seg_source, seg_tile, seg_center, burgers, line_vector):
    fwd_z, inv_z = z_tables()
    fwd_h, inv_h = half_tables()
    order = x_order()
    tz, tzi = two_parts(fwd_z), two_parts(inv_z)
    tx, txi = two_parts(fwd_h[:, :, order]), two_parts(inv_h[:, order, :])
    ty = two_parts(fwd_h.transpose(0, 2, 1))
    tyi = two_parts(inv_h.transpose(0, 2, 1))
    sx, sy, sz = wave_lines()
    weights = two_parts(tile_weights())
    plan, exchanges = scratch_plan()
    scratch = list(plan.values())
    for axis, parts, block, dtype in exchanges.values():
        scratch += exchange_scratch(axis, parts, block, dtype)
    scratch += turn_scratch() + turn_scratch()
    hbm = pl.BlockSpec(memory_space=pl.ANY)
    stress, seg_force = (
        pl.pallas_call(
            whole_body,
            out_shape=(sds((6, NX, NY, GRID)), sds((3, 512))),
            in_specs=[VM] * 7 + [hbm] * 11,
            out_specs=(hbm, VM),
            scratch_shapes=scratch,
            compiler_params=pltpu.CompilerParams(
                vmem_limit_bytes=VMEM_LIMIT, collective_id=0, has_side_effects=True
            ),
        )(
            moduli,
            seg_source.reshape(1, 512),
            seg_tile.reshape(1, 512),
            seg_center.reshape(1, 512),
            burgers,
            line_vector,
            sy,
            sx,
            sz,
            weights,
            dist,
            ids,
            tz,
            ty,
            tx,
            txi,
            tyi,
            tzi,
        )
    )
    return tuple(
        pl.pallas_call(
            finish_body,
            out_shape=(sds((6, NX, NY, GRID)), sds((3, 512))),
            in_specs=[hbm, VM],
            out_specs=(hbm, VM),
            scratch_shapes=[
                pltpu.VMEM((6, NX, NY, GRID), F32),
                pltpu.SemaphoreType.DMA((2, 8)),
            ],
            compiler_params=pltpu.CompilerParams(vmem_limit_bytes=VMEM_LIMIT),
        )(stress, seg_force)
    )


def solution(mesh):
    return jax.shard_map(
        shards,
        mesh=mesh,
        in_specs=(
            P(None, "px", "py", None),
            P("px", "py", None),
            P(),
            P(("px", "py"), None),
            P(("px", "py")),
            P(("px", "py")),
            P(None, ("px", "py")),
            P(None, ("px", "py")),
        ),
        out_specs=(P(None, "px", "py", None), P(None, ("px", "py"))),
        check_vma=False,
    )
```

```python
import functools

import jax
import jax.numpy as jnp
import ml_dtypes
import numpy as np
from jax import lax
from jax.experimental import pallas as pl
from jax.experimental.pallas import tpu as pltpu
from jax.sharding import PartitionSpec as P

F32 = jnp.float32
BF16 = jnp.bfloat16
REF_LAMBDA = 1.25
REF_SHEAR = 1.25
GRID = 256
HALF = 128
NPX = 16
NPY = 8
DEVICES = NPX * NPY
NX = 16
NY = 32
VMEM_LIMIT = 60 * 1024 * 1024
VM = pl.BlockSpec(memory_space=pltpu.VMEM)


def two_parts(table):
    table = np.asarray(table, np.float32)
    high = table.astype(ml_dtypes.bfloat16)
    low = (table - high.astype(np.float32)).astype(ml_dtypes.bfloat16)
    return np.stack([high, low])


def z_tables():
    z = np.arange(GRID)
    fwd = np.zeros((GRID, GRID))
    inv = np.zeros((GRID, GRID))
    for row in range(GRID):
        wave, ri = row // 2, row % 2
        angle = 2 * np.pi * ((wave * z) % GRID) / GRID
        if wave == 0:
            line = np.ones(GRID) if ri == 0 else 1.0 - 2.0 * (z % 2)
            fwd[row], inv[row] = line, line / GRID
        else:
            line = np.cos(angle) if ri == 0 else -np.sin(angle)
            fwd[row], inv[row] = line, 2 * line / GRID
    step = np.roll(np.eye(GRID), 1, 1) - np.roll(np.eye(GRID), -1, 1)
    fwd = 0.5 * np.stack([fwd, fwd @ step])
    inv = np.concatenate([inv, inv @ step.T], axis=1)
    return fwd, inv


def half_tables():
    k = np.arange(HALF)
    fwd, inv = [], []
    for e in range(2):
        angle = 2 * np.pi * (((2 * k[:, None] + e) * k[None, :]) % GRID) / GRID
        cos, sin = np.cos(angle), np.sin(angle)
        fwd.append(np.block([[cos, sin], [-sin, cos]]))
        inv.append(np.block([[cos.T, -sin.T], [sin.T, cos.T]]) / GRID)
    return np.stack(fwd), np.stack(inv)


def x_order():
    index = np.arange(HALF).reshape(8, 4, 4)
    order = index.transpose(1, 0, 2).reshape(-1)
    return np.concatenate([order, order + HALF])


def sines():
    wave = np.arange(GRID)
    line = np.sin(2 * np.pi * wave / GRID)
    line[wave % HALF == 0] = 0.0
    return line


def wave_lines():
    line = sines()
    sx = np.stack([line[0::2], line[1::2]])[:, :, None] * np.ones((1, 1, 128))
    sy = np.concatenate([line[0::2], line[1::2]])[None, :]
    sz = line[:128, None] * np.ones((1, 128))
    return sx.astype(np.float32), sy.astype(np.float32), sz.astype(np.float32)


def tile_weights():
    v = np.arange(128, dtype=np.float64)
    weights = np.exp(-((v[None, :] - v[:, None]) ** 2) / (2.0 * 16.0**2))
    return weights / weights.sum(axis=1, keepdims=True)


def split(values):
    high = values.astype(BF16)
    low = (values - high.astype(F32)).astype(BF16)
    return high, low


def dot(a, b, dims=((1,), (0,))):
    return lax.dot_general(a, b, (dims, ((), ())), preferred_element_type=F32)


def dot3(a, b, dims=((1,), (0,))):
    (ah, al), (bh, bl) = a, b
    return dot(ah, bh, dims) + (dot(ah, bl, dims) + dot(al, bh, dims))


def swap_groups(values):
    count = len(values)
    width = 128 // count
    lane = lax.broadcasted_iota(jnp.int32, values[0].shape, values[0].ndim - 1)
    axis = values[0].ndim - 1
    values = list(values)
    step = 1
    while step < count:
        first = ((lane // (width * step)) % 2) == 0
        out = list(values)
        for i in range(count):
            if i & step == 0:
                low, high = values[i], values[i + step]
                out[i] = jnp.where(first, low, pltpu.roll(high, width * step, axis))
                out[i + step] = jnp.where(first, pltpu.roll(low, 128 - width * step, axis), high)
        values = out
        step *= 2
    return values


def send(src, dst, sems, where):
    return pltpu.make_async_remote_copy(
        src_ref=src,
        dst_ref=dst,
        send_sem=sems[0],
        recv_sem=sems[1],
        device_id=where,
        device_id_type=pl.DeviceIdType.MESH,
    )


def hops(mask):
    return sum((0, 1, 2, 1)[(mask >> shift) % 4] for shift in (1, 3, 5))


def peers(px, py):
    me = px * NPY + py
    masks = sorted([(53 * k) % DEVICES for k in range(1, DEVICES)], key=lambda mask: -hops(mask))
    return [jnp.bitwise_xor(me, mask) for mask in masks]


def place(device):
    return (device // NPY, lax.rem(device, NPY))


def greet(px, py):
    barrier = pltpu.get_barrier_semaphore()
    for d in range(1, NPY):
        where = (px, lax.rem(py + d, NPY))
        pl.semaphore_signal(barrier, inc=1, device_id=where, device_id_type=pl.DeviceIdType.MESH)
    for d in range(1, NPX):
        where = (lax.rem(px + d, NPX), py)
        pl.semaphore_signal(barrier, inc=1, device_id=where, device_id_type=pl.DeviceIdType.MESH)


def greet_on(inside, px, py):
    for d in range(1, NPX):
        where = (lax.rem(px + d, NPX), py)
        pl.semaphore_signal(inside, inc=1, device_id=where, device_id_type=pl.DeviceIdType.MESH)


class Turn:
    def __init__(self, wire, got, sems, own_sem):
        self.wire, self.got, self.sems, self.own_sem = wire, got, sems, own_sem
        self.px, self.py = lax.axis_index("px"), lax.axis_index("py")
        self.me = self.px * NPY + self.py

    def rows(self, ref, part, device):
        return ref.at[part, pl.ds(pl.multiple_of(device * 8, 8), 8)]

    def own(self, part):
        return pltpu.make_async_copy(
            self.rows(self.wire, part, self.me), self.rows(self.got, part, self.me), self.own_sem.at[part]
        )

    def start(self, part):
        sems = (self.sems.at[0, part], self.sems.at[1, part])
        for peer in peers(self.px, self.py):
            send(
                self.rows(self.wire, part, peer), self.rows(self.got, part, self.me), sems, place(peer)
            ).start()
        self.own(part).start()

    def all(self, side, part):
        block = self.got.at[part, pl.ds(0, 8 * DEVICES - 8)]
        return pltpu.make_async_copy(block, block, self.sems.at[side, part])

    def arrive(self, part):
        self.own(part).wait()
        self.all(1, part).wait()

    def finish(self, part):
        self.all(0, part).wait()


def turn_scratch():
    return [
        pltpu.VMEM((3, 8 * DEVICES, 128), F32),
        pltpu.VMEM((3, 8 * DEVICES, 128), F32),
        pltpu.SemaphoreType.DMA((2, 3)),
        pltpu.SemaphoreType.DMA((3,)),
    ]


class Exchange:
    def __init__(self, axis, wire, got, sems, own_sem):
        self.count = NPX if axis == "px" else NPY
        self.axis, self.wire, self.got, self.sems, self.own_sem = axis, wire, got, sems, own_sem
        self.px, self.py = lax.axis_index("px"), lax.axis_index("py")
        self.me = self.px if axis == "px" else self.py

    def own(self, part):
        return pltpu.make_async_copy(
            self.wire.at[part, self.me], self.got.at[part, self.me], self.own_sem.at[part]
        )

    def start(self, part):
        shift = NPY if self.axis == "px" else 1
        for mask in sorted(range(1, self.count), key=lambda mask: -hops(mask * shift)):
            peer = jnp.bitwise_xor(self.me, mask)
            where = (peer, self.py) if self.axis == "px" else (self.px, peer)
            sems = (self.sems.at[0, part], self.sems.at[1, part])
            send(self.wire.at[part, peer], self.got.at[part, self.me], sems, where).start()
        self.own(part).start()

    def all(self, side, part):
        block = self.got.at[part, pl.ds(0, self.count - 1)]
        return pltpu.make_async_copy(block, block, self.sems.at[side, part])

    def arrive(self, part):
        self.own(part).wait()
        self.all(1, part).wait()

    def finish(self, part):
        self.all(0, part).wait()


def exchange_scratch(axis, parts, block, dtype=F32):
    count = NPX if axis == "px" else NPY
    return [
        pltpu.VMEM((parts, count) + block, dtype),
        pltpu.VMEM((parts, count) + block, dtype),
        pltpu.SemaphoreType.DMA((2, parts)),
        pltpu.SemaphoreType.DMA((parts,)),
    ]


def sds(shape, dtype=F32):
    return jax.ShapeDtypeStruct(shape, dtype)


def moduli_of(table, ids):
    lame, shear = [], []
    for half in range(2):
        index = ids[:, half * 128 : (half + 1) * 128]
        lame.append(jnp.take_along_axis(table, index, axis=1))
        shear.append(jnp.take_along_axis(table, index + 64, axis=1))
    return jnp.concatenate(lame, axis=1), jnp.concatenate(shear, axis=1)


def table_of(moduli_ref):
    row = jnp.concatenate([moduli_ref[0:1, :], moduli_ref[1:2, :]], axis=1)
    return jnp.broadcast_to(row, (NY, 128))


def polar_part(first, count, dist, ids, table, polar, moduli):
    def at_x(x, carry):
        lame, shear = moduli_of(table, ids[x])
        moduli[0, x] = lame
        moduli[1, x] = shear
        exx, eyy, ezz = dist[0, x], dist[4, x], dist[8, x]
        trace = lame * (exx + eyy + ezz)
        twice = shear + shear
        polar[0, x] = -(twice * exx + trace)
        polar[1, x] = -(twice * eyy + trace)
        polar[2, x] = -(twice * ezz + trace)
        polar[3, x] = -(shear * (dist[5, x] + dist[7, x]))
        polar[4, x] = -(shear * (dist[2, x] + dist[6, x]))
        polar[5, x] = -(shear * (dist[1, x] + dist[3, x]))
        return carry

    lax.fori_loop(first, first + count, at_x, 0)


def row_of(device):
    return (device % NPY) * NPX + device // NPY


def request_part(source, tile, centre, asked):
    src_lane = row_of(source[...]).astype(F32)
    src = jnp.transpose(jnp.broadcast_to(src_lane, (128, 512)))
    same = src[:, 0:1] == src_lane
    first = lax.broadcasted_iota(jnp.int32, (512, 512), 0)
    second = lax.broadcasted_iota(jnp.int32, (512, 512), 1)
    slot_lane = jnp.sum(jnp.where(same & (first < second), 1.0, 0.0), axis=0, keepdims=True)
    match = (src == lax.broadcasted_iota(jnp.int32, (512, 128), 1).astype(F32)).astype(F32).astype(BF16)
    row = lax.broadcasted_iota(jnp.int32, (8, 512), 0).astype(F32)
    here = row == slot_lane
    tile_v = tile[...]
    values = [tile_v // 8, tile_v % 8, centre[...]]
    rows = [jnp.where(here, v.astype(F32), 0.0) for v in values]
    stacked = jnp.concatenate(rows + [jnp.zeros((8, 512), F32)], axis=0).astype(BF16)
    got = dot(stacked, match)
    both = jnp.concatenate([got[0:8] * 8.0 + got[8:16], got[16:24], jnp.zeros((112, 128), F32)], axis=0)
    asked[...] = jnp.transpose(both).astype(jnp.int32)
    return slot_lane


def shift_y(values, before, after):
    row = lax.broadcasted_iota(jnp.int32, values.shape, 0)
    up = jnp.where(row == NY - 1, after, pltpu.roll(values, NY - 1, 0))
    down = jnp.where(row == 0, before, pltpu.roll(values, 1, 0))
    return up - down


LAST = ((1,), (1,))


def forward_z_local(c, polar, tz, waves, force):
    for x in range(NX):
        hi, lo = split(polar[4 - c, x])
        force[0, x * NY : (x + 1) * NY, :] = hi
        force[1, x * NY : (x + 1) * NY, :] = lo
    waves[c] = dot3((tz[0, 1], tz[1, 1]), (force[0], force[1]), LAST)


def forward_z(c, polar, faces, tz, base, wire, force):
    cx = (6 - c) * ((c + 1) // 2)
    cy = 5 - c - 3 * lax.rem(c, 2)
    fx, fy = faces
    for x in range(NX):
        after = fx[1, c] if x == NX - 1 else polar[cx, x + 1]
        before = fx[0, c] if x == 0 else polar[cx, x - 1]
        grad_y = shift_y(polar[cy, x], fy[0, c, x : x + 1, :], fy[1, c, x : x + 1, :])
        hi, lo = split((after - before) + grad_y)
        force[0, x * NY : (x + 1) * NY, :] = hi
        force[1, x * NY : (x + 1) * NY, :] = lo
    waves = base[c] + dot3((tz[0, 0], tz[1, 0]), (force[0], force[1]), LAST)
    for t in range(32):
        for xg in range(4):
            wire[c, pl.ds(32 * t + xg, 8, stride=4), :] = waves[
                8 * t : 8 * t + 8, xg * 128 : xg * 128 + 128
            ]


def forward_plane(c, got, ty, tx, waves, yrows, xrows):
    for q in range(NPX):
        row = q * 64
        low = swap_groups([got[c, row + p * 8 : row + p * 8 + 8, :] for p in range(4)])
        high = swap_groups([got[c, row + p * 8 : row + p * 8 + 8, :] for p in range(4, 8)])
        for x4 in range(4):
            to = pl.ds(q * 4 + x4, 8, stride=64)
            yrows[0, to, :] = low[x4] + high[x4]
            yrows[1, to, :] = low[x4] - high[x4]
    for e in range(2):
        rows = jnp.concatenate([yrows[e, :256, :], yrows[e, 256:, :]], axis=1)
        out = dot3(split(rows), (ty[0, e], ty[1, e]))
        for xg in range(4):
            a, b = out[xg * 64 : xg * 64 + 32, :], out[xg * 64 + 32 : xg * 64 + 64, :]
            for ex in range(2):
                hi, lo = split(a + b if ex == 0 else a - b)
                for ri in range(2):
                    to = slice(ri * 128 + xg * 32, ri * 128 + xg * 32 + 32)
                    xrows[0, ex, to, e * 128 : e * 128 + 128] = hi[:, ri * 128 : ri * 128 + 128]
                    xrows[1, ex, to, e * 128 : e * 128 + 128] = lo[:, ri * 128 : ri * 128 + 128]
    for ex in range(2):
        waves[ex, c] = dot3((tx[0, ex], tx[1, ex]), (xrows[0, ex], xrows[1, ex]))


def solve(waves, solved, sx, sy, sz, kz):
    sy = sy[...]
    sz = sz[pl.ds(kz, 1), :]
    sz = jnp.concatenate([sz, sz], axis=1)
    coupling = (REF_LAMBDA + REF_SHEAR) / (REF_LAMBDA + 2.0 * REF_SHEAR)
    rest = sy * sy + sz * sz
    for ex in range(2):
        wx = jnp.concatenate([sx[ex], sx[ex]], axis=1)
        squared = wx * wx + rest
        null = squared == 0.0
        inverse = jnp.where(null, 0.0, 1.0 / jnp.where(null, 1.0, squared))
        scale = inverse * (1.0 / REF_SHEAR)
        for ri in range(2):
            parts = [waves[ex, c, ri * 128 : ri * 128 + 128, :] for c in range(3)]
            common = coupling * inverse * (wx * parts[0] + sy * parts[1] + sz * parts[2])
            for c, line in enumerate((wx, sy, sz)):
                hi, lo = split(scale * (parts[c] - common * line))
                solved[0, ex, c, ri * 128 : ri * 128 + 128, :] = hi
                solved[1, ex, c, ri * 128 : ri * 128 + 128, :] = lo


def inverse_plane(c, solved, txi, tyi, wire, yrows):
    backs = [dot3((txi[0, ex], txi[1, ex]), (solved[0, ex, c], solved[1, ex, c])) for ex in range(2)]
    halves = (backs[0] + backs[1], backs[0] - backs[1])
    outs = []
    for e in range(2):
        lane = slice(e * 128, e * 128 + 128)
        sides = []
        for ri in range(2):
            blocks = []
            for xg in range(4):
                row = ri * 128 + xg * 32
                blocks += [halves[0][row : row + 32, lane], halves[1][row : row + 32, lane]]
            sides.append(jnp.concatenate(blocks, axis=0))
        outs.append(dot3(split(jnp.concatenate(sides, axis=1)), (tyi[0, e], tyi[1, e])))
    for half, out in enumerate((outs[0] + outs[1], outs[0] - outs[1])):
        yrows[half, :256, :] = out[:, :128]
        yrows[half, 256:, :] = out[:, 128:]
    for q in range(NPX):
        for half in range(2):
            tiles = [yrows[half, pl.ds(q * 4 + x4, 8, stride=64), :] for x4 in range(4)]
            for p, tile in enumerate(swap_groups(tiles)):
                row = q * 64 + half * 32 + p * 8
                wire[c, row : row + 8, :] = tile


def inverse_z(c, got, tzi, disp, yface, lines):
    for xg in range(4):
        turned = jnp.transpose(got[c, pl.ds(xg, 256, stride=4), :])
        hi, lo = split(turned)
        lines[0, xg * 128 : xg * 128 + 128, :] = hi
        lines[1, xg * 128 : xg * 128 + 128, :] = lo
    out = dot3((lines[0], lines[1]), (tzi[0, :, :256], tzi[1, :, :256]))
    for x in range(NX):
        disp[c, x] = out[x * NY : (x + 1) * NY, :]
        yface[0, c, x : x + 1] = out[x * NY : x * NY + 1, :]
        yface[1, c, x : x + 1] = out[x * NY + NY - 1 : x * NY + NY, :]


def inverse_z_grad(c, tzi, grad, lines):
    out = dot3((lines[0], lines[1]), (tzi[0, :, 256:], tzi[1, :, 256:]))
    for x in range(NX):
        grad[c, x] = out[x * NY : (x + 1) * NY, :]


def stress_part(first, count, late, disp, grad, hx, hy, polar, moduli, stress, rows):
    def at_x(x, carry):
        shear = moduli[1, x]
        row = pl.ds(pl.multiple_of(x * NY, NY), NY)

        def grad_x(c):
            after = hx[1, c] if first == NX - 1 else disp[c, x + 1]
            before = hx[0, c] if first == 0 else disp[c, x - 1]
            return after - before

        def grad_y(c):
            return shift_y(disp[c, x], hy[0, c, pl.ds(x, 1), :], hy[1, c, pl.ds(x, 1), :])

        half = 0.5 * shear
        if late:
            parts = {3: half * (grad[1, x] + grad_y(2)), 4: half * (grad[0, x] + grad_x(2))}
        else:
            exx, eyy, ezz = grad_x(0), grad_y(1), grad[2, x]
            trace = (0.5 * moduli[0, x]) * (exx + eyy + ezz)
            parts = {
                0: shear * exx + trace,
                1: shear * eyy + trace,
                2: shear * ezz + trace,
                5: half * (grad_y(0) + grad_x(1)),
            }
        for c, part in parts.items():
            total = part + polar[c, x]
            stress[c, x] = total
            hi, lo = split(total)
            rows[0, row, c * 256 : c * 256 + 256] = hi
            rows[1, row, c * 256 : c * 256 + 256] = lo
        return carry

    lax.fori_loop(first, first + count, at_x, 0)


def pick_part(asked, weights, pick, gain):
    column = lax.broadcasted_iota(jnp.int32, (128, 512), 1)
    lane = lax.broadcasted_iota(jnp.int32, (128, 128), 1)
    lane256 = lax.broadcasted_iota(jnp.int32, (128, 256), 1)
    for k in range(8):
        here = slice(k * 128, k * 128 + 128)
        tile = asked[:, k : k + 1]
        centre = asked[:, 8 + k : 9 + k]
        pick[here, :] = (column == tile // 2).astype(F32).astype(BF16)
        at = (lane == centre).astype(F32).astype(BF16)
        row = dot(at, weights[0]) + dot(at, weights[1])
        row = jnp.concatenate([row, row], axis=1)
        gain[here, :] = jnp.where(lane256 // 128 == tile % 2, row, 0.0)


def reply_part(comps, pick, gain, rows, out):
    lane = lax.broadcasted_iota(jnp.int32, (128, 128), 1)
    for c in comps:
        here = slice(c * 256, c * 256 + 256)
        picked = dot(pick[...], rows[0, :, here]) + dot(pick[...], rows[1, :, here])
        picked = picked * gain[...]
        total = jnp.sum(picked[:, :128] + picked[:, 128:], axis=1, keepdims=True)
        for k in range(8):
            out = jnp.where(lane == c * 8 + k, total[k * 128 : k * 128 + 128], out)
    return out


def force_part(reply, match, mine, burgers, line, out):
    hi, lo = split(reply)
    low = (reply - hi.astype(F32) - lo.astype(F32)).astype(BF16)
    first = ((0,), (0,))
    match = match[...]
    got = dot(hi, match, first) + (dot(lo, match, first) + dot(low, match, first))
    mine = got * mine[...]
    t = [jnp.sum(mine[c * 8 : c * 8 + 8, :], axis=0, keepdims=True) for c in range(6)]
    b = [burgers[i : i + 1, :] for i in range(3)]
    v = [line[i : i + 1, :] for i in range(3)]
    push_x = t[0] * b[0] + t[5] * b[1] + t[4] * b[2]
    push_y = t[5] * b[0] + t[1] * b[1] + t[3] * b[2]
    push_z = t[4] * b[0] + t[3] * b[1] + t[2] * b[2]
    out[0:1, :] = push_y * v[2] - push_z * v[1]
    out[1:2, :] = push_z * v[0] - push_x * v[2]
    out[2:3, :] = push_x * v[1] - push_y * v[0]


def scratch_plan():
    half = pltpu.VMEM((2, 2, 256, 256), BF16)
    sem = pltpu.SemaphoreType.DMA
    plan = {
        "inside": pltpu.SemaphoreType.REGULAR,
        "dist": pltpu.VMEM((9, NX, NY, GRID), F32),
        "ids": pltpu.VMEM((NX, NY, GRID), jnp.int32),
        "load_sem": sem((2, 4)),
        "polar": pltpu.VMEM((6, NX, NY, GRID), F32),
        "moduli": pltpu.VMEM((2, NX, NY, GRID), F32),
        "tz": half,
        "ty": half,
        "tx": half,
        "txi": half,
        "tyi": half,
        "tzi": pltpu.VMEM((2, 256, 512), BF16),
        "table_sem": sem((9,)),
        "sx": pltpu.VMEM((2, 128, 128), F32),
        "sz": pltpu.VMEM((128, 128), F32),
        "weights": pltpu.VMEM((2, 128, 128), BF16),
        "ox": pltpu.VMEM((2, 3, NY, GRID), F32),
        "oy": pltpu.VMEM((2, 3, NX, GRID), F32),
        "fx": pltpu.VMEM((2, 3, NY, GRID), F32),
        "fy": pltpu.VMEM((2, 3, NX, GRID), F32),
        "face_sem": sem((3, 2, 4)),
        "hx": pltpu.VMEM((2, 3, NY, GRID), F32),
        "hy": pltpu.VMEM((2, 3, NX, GRID), F32),
        "yface": pltpu.VMEM((2, 3, NX, GRID), F32),
        "back_sem": sem((3, 2, 4)),
        "base": pltpu.VMEM((3, 256, 512), F32),
        "force": pltpu.VMEM((2, 512, 256), BF16),
        "yrows": pltpu.VMEM((2, 512, 128), F32),
        "xrows": half,
        "waves": pltpu.VMEM((2, 3, 256, 256), F32),
        "solved": pltpu.VMEM((2, 2, 3, 256, 256), BF16),
        "lines": pltpu.VMEM((2, 512, 256), BF16),
        "disp": pltpu.VMEM((3, NX, NY, GRID), F32),
        "grad": pltpu.VMEM((3, NX, NY, GRID), F32),
        "stress": pltpu.VMEM((6, NX, NY, GRID), F32),
        "store_sem": sem((1,)),
        "rows": pltpu.VMEM((2, 512, 1536), BF16),
        "asked": pltpu.VMEM((128, 128), jnp.int32),
        "pick": pltpu.VMEM((1024, 512), BF16),
        "gain": pltpu.VMEM((1024, 256), F32),
        "slot": pltpu.VMEM((1, 512), F32),
        "reply": pltpu.VMEM((128, 128), F32),
        "match": pltpu.VMEM((128, 512), BF16),
        "mine": pltpu.VMEM((128, 512), F32),
    }
    exchanges = {
        "exa": ("py", 1, (NPX, 128), jnp.int32),
        "exb": ("px", 1, (NPY, 128), jnp.int32),
        "exc": ("px", 1, (NPY, 128), F32),
        "exd": ("py", 1, (NPX, 128), F32),
    }
    return plan, exchanges


class Names:
    pass


def whole_body(*refs):
    plan, exchanges = scratch_plan()
    n_in, n_out = 18, 2
    (
        moduli_in, source, tile, centre, burgers, line, sy,
        sx_h, sz_h, weights_h, dist_h, ids_h, tz_h, ty_h, tx_h, txi_h, tyi_h, tzi_h,
    ) = refs[:n_in]
    stress_h, seg_force = refs[n_in : n_in + n_out]
    rest = list(refs[n_in + n_out :])
    r = Names()
    for name in plan:
        setattr(r, name, rest.pop(0))
    for name, (axis, _, _, _) in exchanges.items():
        setattr(r, name, Exchange(axis, rest.pop(0), rest.pop(0), rest.pop(0), rest.pop(0)))

    r.there = Turn(rest.pop(0), rest.pop(0), rest.pop(0), rest.pop(0))
    r.back = Turn(rest.pop(0), rest.pop(0), rest.pop(0), rest.pop(0))

    px, py = lax.axis_index("px"), lax.axis_index("py")
    loads = []
    for g in range(4):
        here = pl.ds(g * 4, 4)
        loads.append(
            (
                pltpu.make_async_copy(dist_h.at[:, here], r.dist.at[:, here], r.load_sem.at[0, g]),
                pltpu.make_async_copy(ids_h.at[here], r.ids.at[here], r.load_sem.at[1, g]),
            )
        )
        for load in loads[-1]:
            load.start()
    pairs = (
        (tz_h, r.tz), (ty_h, r.ty), (tx_h, r.tx), (txi_h, r.txi), (tyi_h, r.tyi), (tzi_h, r.tzi),
        (sx_h, r.sx), (sz_h, r.sz), (weights_h, r.weights),
    )
    tables = [pltpu.make_async_copy(a, b, r.table_sem.at[i]) for i, (a, b) in enumerate(pairs)]
    tables[0].start()
    greet(px, py)

    slot = request_part(source, tile, centre, r.asked)
    r.slot[...] = slot
    for p in range(NPY):
        r.exa.wire[0, p] = r.asked[p * NPX : p * NPX + NPX, :]
    lookup = table_of(moduli_in)
    for g in range(4):
        for load in loads[g]:
            load.wait()
        polar_part(g * 4, 4, r.dist, r.ids, lookup, r.polar, r.moduli)
    for side in range(2):
        for k, comp in enumerate((0, 5, 4)):
            r.ox[side, k] = r.polar[comp, side * (NX - 1)]
        for k, comp in enumerate((5, 1, 3)):
            r.oy[side, k] = r.polar[comp, :, side * (NY - 1), :]

    left, right = lax.rem(px + NPX - 1, NPX), lax.rem(px + 1, NPX)
    down, up = lax.rem(py + NPY - 1, NPY), lax.rem(py + 1, NPY)
    sides = [(left, py), (right, py), (px, down), (px, up)]

    def face(src, dst, sems, to, k):
        return send(src, dst, (sems.at[0, k], sems.at[1, k]), sides[to])

    halo = []
    for c in range(3):
        sems = r.face_sem.at[c]
        halo += [
            face(r.ox.at[0, c], r.fx.at[1, c], sems, 0, 1),
            face(r.ox.at[1, c], r.fx.at[0, c], sems, 1, 0),
            face(r.oy.at[0, c], r.fy.at[1, c], sems, 2, 3),
            face(r.oy.at[1, c], r.fy.at[0, c], sems, 3, 2),
        ]
    pl.semaphore_wait(pltpu.get_barrier_semaphore(), NPX + NPY - 2)
    for copy in halo:
        copy.start()
    greet_on(r.inside, px, py)
    for table in tables[1:]:
        table.start()
    r.exa.start(0)
    tables[0].wait()

    def local(c, carry):
        forward_z_local(c, r.polar, r.tz, r.base, r.force)
        return carry

    lax.fori_loop(0, 3, local, 0)
    for c in range(3):
        for copy in halo[4 * c : 4 * c + 4]:
            copy.wait_recv()
        forward_z(c, r.polar, (r.fx, r.fy), r.tz, r.base, r.there.wire, r.force)
        if c == 0:
            pl.semaphore_wait(r.inside, NPX - 1)
        r.there.start(c)
    r.exa.arrive(0)
    r.asked[...] = r.exa.got[0].reshape(128, 128)
    for p in range(NPX):
        r.exb.wire[0, p] = r.asked[pl.ds(p, NPY, stride=NPX), :]
    r.exb.start(0)
    owners = lax.broadcasted_iota(jnp.int32, (128, 512), 0)
    r.match[...] = (owners == row_of(source[...])).astype(F32).astype(BF16)
    r.mine[...] = jnp.where((owners % 8).astype(F32) == r.slot[...], 1.0, 0.0)
    tables[1].wait()
    tables[2].wait()

    def step_plane(c, carry):
        r.there.arrive(c)
        forward_plane(c, r.there.got, r.ty, r.tx, r.waves, r.yrows, r.xrows)
        return carry

    lax.fori_loop(0, 3, step_plane, 0)
    for table in tables[6:]:
        table.wait()
    solve(r.waves, r.solved, r.sx, sy, r.sz, px * NPY + py)
    tables[3].wait()
    tables[4].wait()

    def step_back(c, carry):
        inverse_plane(c, r.solved, r.txi, r.tyi, r.back.wire, r.yrows)
        r.back.start(c)
        return carry

    lax.fori_loop(0, 3, step_back, 0)
    tables[5].wait()
    r.exb.arrive(0)
    for p in range(NPX):
        r.asked[p * NPY : p * NPY + NPY, :] = r.exb.got[0, p]
    pick_part(r.asked, r.weights, r.pick, r.gain)

    def faces_back(c):
        sems = r.back_sem.at[c]
        return [
            face(r.disp.at[c, 0], r.hx.at[1, c], sems, 0, 1),
            face(r.disp.at[c, NX - 1], r.hx.at[0, c], sems, 1, 0),
            face(r.yface.at[0, c], r.hy.at[1, c], sems, 2, 3),
            face(r.yface.at[1, c], r.hy.at[0, c], sems, 3, 2),
        ]

    backs = []
    for c in range(3):
        r.back.arrive(c)
        inverse_z(c, r.back.got, r.tzi, r.disp, r.yface, r.lines)
        backs += faces_back(c)
        for copy in backs[4 * c :]:
            copy.start()
        inverse_z_grad(c, r.tzi, r.grad, r.lines)

    def stress(late):
        for first, count in ((0, 1), (1, NX - 2), (NX - 1, 1)):
            stress_part(
                first, count, late, r.disp, r.grad, r.hx, r.hy, r.polar, r.moduli, r.stress, r.rows
            )

    for copy in backs[:8]:
        copy.wait_recv()
    stress(False)
    reply = reply_part((0, 1, 2, 5), r.pick, r.gain, r.rows, jnp.zeros((128, 128), F32))
    for copy in backs[8:]:
        copy.wait_recv()
    stress(True)
    store = pltpu.make_async_copy(r.stress, stress_h, r.store_sem.at[0])
    store.start()
    r.reply[...] = reply_part((3, 4), r.pick, r.gain, r.rows, reply)
    for p in range(NPX):
        r.exc.wire[0, p] = r.reply[p * NPY : p * NPY + NPY, :]
    r.exc.start(0)
    for copy in halo + backs:
        copy.wait_send()
    for c in range(3):
        r.there.finish(c)
        r.back.finish(c)
    r.exa.finish(0)
    r.exb.finish(0)
    r.exc.arrive(0)
    r.reply[...] = r.exc.got[0].reshape(128, 128)
    for p in range(NPY):
        r.exd.wire[0, p] = r.reply[pl.ds(p, NPX, stride=NPY), :]
    r.exd.start(0)
    store.wait()
    r.exd.arrive(0)
    force_part(r.exd.got[0].reshape(128, 128), r.match, r.mine, burgers, line, seg_force)
    r.exc.finish(0)
    r.exd.finish(0)


def finish_body(stress_in, force_in, stress_out, force_out, buffer, sems):
    count = 8
    width = NX // count
    spans = [pl.ds(i * width, width) for i in range(count)]
    loads = [
        pltpu.make_async_copy(stress_in.at[:, s], buffer.at[:, s], sems.at[0, i]) for i, s in enumerate(spans)
    ]
    stores = [
        pltpu.make_async_copy(buffer.at[:, s], stress_out.at[:, s], sems.at[1, i]) for i, s in enumerate(spans)
    ]
    for load in loads:
        load.start()
    force_out[...] = force_in[...]
    for load, store in zip(loads, stores):
        load.wait()
        store.start()
    for store in stores:
        store.wait()


def shards(dist, ids, moduli, seg_source, seg_tile, seg_center, burgers, line_vector):
    fwd_z, inv_z = z_tables()
    fwd_h, inv_h = half_tables()
    order = x_order()
    tz, tzi = two_parts(fwd_z), two_parts(inv_z)
    tx, txi = two_parts(fwd_h[:, :, order]), two_parts(inv_h[:, order, :])
    ty = two_parts(fwd_h.transpose(0, 2, 1))
    tyi = two_parts(inv_h.transpose(0, 2, 1))
    sx, sy, sz = wave_lines()
    weights = two_parts(tile_weights())
    plan, exchanges = scratch_plan()
    scratch = list(plan.values())
    for axis, parts, block, dtype in exchanges.values():
        scratch += exchange_scratch(axis, parts, block, dtype)
    scratch += turn_scratch() + turn_scratch()
    hbm = pl.BlockSpec(memory_space=pl.ANY)
    stress, seg_force = (
        pl.pallas_call(
            whole_body,
            out_shape=(sds((6, NX, NY, GRID)), sds((3, 512))),
            in_specs=[VM] * 7 + [hbm] * 11,
            out_specs=(hbm, VM),
            scratch_shapes=scratch,
            compiler_params=pltpu.CompilerParams(
                vmem_limit_bytes=VMEM_LIMIT, collective_id=0, has_side_effects=True
            ),
        )(
            moduli,
            seg_source.reshape(1, 512),
            seg_tile.reshape(1, 512),
            seg_center.reshape(1, 512),
            burgers,
            line_vector,
            sy,
            sx,
            sz,
            weights,
            dist,
            ids,
            tz,
            ty,
            tx,
            txi,
            tyi,
            tzi,
        )
    )
    return tuple(
        pl.pallas_call(
            finish_body,
            out_shape=(sds((6, NX, NY, GRID)), sds((3, 512))),
            in_specs=[hbm, VM],
            out_specs=(hbm, VM),
            scratch_shapes=[
                pltpu.VMEM((6, NX, NY, GRID), F32),
                pltpu.SemaphoreType.DMA((2, 8)),
            ],
            compiler_params=pltpu.CompilerParams(vmem_limit_bytes=VMEM_LIMIT),
        )(stress, seg_force)
    )


def solution(mesh):
    return jax.shard_map(
        shards,
        mesh=mesh,
        in_specs=(
            P(None, "px", "py", None),
            P("px", "py", None),
            P(),
            P(("px", "py"), None),
            P(("px", "py")),
            P(("px", "py")),
            P(None, ("px", "py")),
            P(None, ("px", "py")),
        ),
        out_specs=(P(None, "px", "py", None), P(None, ("px", "py"))),
        check_vma=False,
    )
```
